256 devices in a mesh: gz: 8 (over y, core), xy: 32 (over x, z).
Axes of the slice: x: 4, y: 4, z: 8, core: 2. Of those that a mesh axis runs over, the one named last changes fastest.
Arguments:
- populations: float32 [19, 256, 32, 1024], P(None, 'xy', None, 'gz'), may hold values from 0.6 to 1.4
- solid: int32 [256, 32, 1024], P('xy', None, 'gz'), may hold values 0 or 1
- knudsen: float32 [256, 32, 1024], P('xy', None, 'gz'), may hold values from 0.05 to 5
- wall_cells: int32 [8, 131072], P('gz', 'xy'), may hold values from 0 to 32767, as said below
- wall_target: int32 [8, 131072], P('gz', 'xy'), may hold values from 0 to 131071, as said below
- coverage: float32 [4096, 256], P(('gz', 'xy')), may hold values from 0.05 to 0.95
- tile_links: int32 [4096, 4], P(('gz', 'xy')), may hold values from 0 to 511, as said below
Outputs:
- updated: float32 [19, 256, 32, 1024], P(None, 'xy', None, 'gz')
- new_coverage: float32 [4096, 256], P(('gz', 'xy'))
The draws below stay inside these ranges and needn't reach their ends.
Inputs may be any that keep to these rules, and one draw needn't show every extreme that they name: `wall_cells`: the 4096 entries of one brick are distinct cell numbers of that brick. `wall_target`: an entry is an owner index along xy times 4096 plus a cell place within that owner's 16 tiles; at most 256 wall cells of one brick feed one owner. A patch cell may be fed by several wall cells or by none. `tile_links`: tile numbers count within the gz row of the tile.
All inputs are finite; a program needn't handle non-finite values. No bound on the sum of `solid` on one device may be relied on, other than what follows from the above.
Results may differ from the reference program's by a relative error of at most 0.0003.
Values sent between devices are 32-bit elements; how exact they have to be, the bound alone decides.
A program may use at most 64 MiB of HBM per device.

```python
import math
import jax
import jax.numpy as jnp
from jax import lax

CX = 8
NY = 32
CZ = 128
PATCH = 256
TILE_SIDE = 16
SWEEPS = 2
NX = 256
NZ = 1024
WALLS = 4096
BUCKET = 256
ROW_TILES = 512
TILES = 4096
N_GZ = 8
N_XY = 32


def draw_wall_cells(key, part):
    key = jax.random.fold_in(key, 11)
    cell_count = CX * NY * CZ
    subkeys = jax.random.split(key, 2 * N_GZ * N_XY)

    def choose_cells(first_key, second_key):
        inner = jax.random.permutation(first_key, cell_count - 2)[:WALLS - 2].astype(jnp.int32) + 1
        listed = jnp.concatenate([jnp.array([0, cell_count - 1], jnp.int32), inner])
        return jax.random.permutation(second_key, listed)
    picked = jax.vmap(choose_cells)(subkeys[0::2], subkeys[1::2])
    return picked.reshape(N_GZ, N_XY * WALLS).astype(jnp.int32)


def draw_wall_target(key, part):
    key = jax.random.fold_in(key, 12)
    heat_key, noise_key, lane_key, order_key = jax.random.split(key, 4)
    owners = N_XY
    candidate_count = owners * BUCKET
    candidates = jnp.arange(candidate_count, dtype=jnp.int32)
    candidate_owner = candidates // BUCKET
    heat = jax.random.randint(heat_key, (N_GZ, owners), 0, 3)
    heat = heat.at[:, 0].set(3).at[:, owners - 1].set(3)
    noise = jax.random.randint(noise_key, (N_GZ, owners, candidate_count), 0, 256)
    score = ((heat[:, candidate_owner] * 256)[:, None, :] + noise) * candidate_count + candidates[None, None, :]
    chosen = lax.top_k(score, WALLS)[1].astype(jnp.int32)
    owner_index = chosen // BUCKET
    copy_index = chosen % BUCKET
    brick_index = jnp.arange(owners, dtype=jnp.int32)[None, :, None]
    lane_index = jax.random.randint(lane_key, chosen.shape, 0, WALLS)
    lane_index = jnp.where((brick_index == 0) & (owner_index == 0) & (copy_index == 0), 0, lane_index)
    lane_index = jnp.where((brick_index == 0) & (owner_index == owners - 1) & (copy_index == 0), WALLS - 1, lane_index)
    target = owner_index * WALLS + lane_index
    order_keys = jax.random.split(order_key, N_GZ * owners)
    orders = jax.vmap(lambda subkey: jax.random.permutation(subkey, WALLS))(order_keys).reshape(N_GZ, owners, WALLS)
    target = jnp.take_along_axis(target, orders, axis=2)
    return target.reshape(N_GZ, owners * WALLS).astype(jnp.int32)


def draw_tile_links(key, part):
    key = jax.random.fold_in(key, 13)
    south_key, north_key = jax.random.split(key, 2)
    tile_number = jnp.tile(jnp.arange(ROW_TILES, dtype=jnp.int32), N_GZ)
    south = (tile_number + jax.random.randint(south_key, tile_number.shape, 1, ROW_TILES)) % ROW_TILES
    north = (tile_number + jax.random.randint(north_key, tile_number.shape, 1, ROW_TILES)) % ROW_TILES
    north = jnp.where(tile_number == 0, ROW_TILES // 2, north)
    west = (tile_number - 1) % ROW_TILES
    east = (tile_number + 1) % ROW_TILES
    return jnp.stack([west, east, south, north], axis=1).astype(jnp.int32)


def touch_ends(values, rng, least, largest):
    shape = values.shape
    index_at = [jax.random.randint(jax.random.fold_in(rng, axis), (), 0, shape[axis]) for axis in range(len(shape))]
    values = values.at[tuple(index_at)].set(least)
    longest = shape.index(max(shape))
    index_at[longest] = (index_at[longest] + 1) % shape[longest]
    return values.at[tuple(index_at)].set(largest)


def shard_levels(key, dims, cuts, smallest, largest):
    factor_of = 1.0
    for dim, blocks in cuts:
        heights = jax.random.uniform(jax.random.fold_in(jax.random.fold_in(key, 6), dim), (blocks,), jnp.float32, smallest / len(cuts), largest / len(cuts))
        factor_of = factor_of * jnp.repeat(jnp.exp(heights), dims[dim] // blocks).reshape((-1,) + (1,) * (len(dims) - 1 - dim))
    return factor_of


def setup_inputs(seed: int = 0) -> dict:
    key_of = jax.random.split(jax.random.key(seed), 8)
    return {
        "populations": jnp.clip(0.6 + 0.79999995 * jax.random.uniform(key_of[0], (19, NX, NY, NZ), jnp.float32) ** shard_levels(key_of[0], (19, NX, NY, NZ), ((1, 32), (3, 8)), -0.2, 0.2), 0.6, 1.4),
        "solid": touch_ends((jax.random.randint(key_of[1], (NX, NY, NZ), 0, 5) < 1).astype(jnp.int32), jax.random.fold_in(key_of[1], 1), 0, 1),
        "knudsen": jnp.clip(jnp.exp(math.log(5.0) - 4.6051702 * jax.random.uniform(key_of[2], (NX, NY, NZ), jnp.float32) ** shard_levels(key_of[2], (NX, NY, NZ), ((0, 32), (2, 8)), -0.2, 0.2)), 0.05, 5.0),
        "wall_cells": draw_wall_cells(jax.random.fold_in(key_of[7], 71), 0),
        "wall_target": draw_wall_target(jax.random.fold_in(key_of[7], 71), 0),
        "coverage": jnp.clip(0.05 + 0.9 * jax.random.uniform(key_of[5], (TILES, PATCH), jnp.float32) ** shard_levels(key_of[5], (TILES, PATCH), ((0, 256),), -0.2, 0.2), 0.05, 0.95),
        "tile_links": draw_tile_links(jax.random.fold_in(key_of[7], 71), 0),
    }


VELOCITIES = [(0, 0, 0), (0, 1, 0), (0, -1, 0), (1, 0, 0), (-1, 0, 0), (0, 0, 1), (0, 0, -1),
              (1, 1, 0), (-1, -1, 0), (1, -1, 0), (-1, 1, 0),
              (1, 0, 1), (-1, 0, -1), (1, 0, -1), (-1, 0, 1),
              (0, 1, 1), (0, -1, -1), (0, 1, -1), (0, -1, 1)]
WEIGHT_TABLE = [1.0 / 3.0] + [1.0 / 18.0] * 6 + [1.0 / 36.0] * 12
OPPOSITE = [VELOCITIES.index(tuple(-component for component in velocity)) for velocity in VELOCITIES]
ADSORB_RATE = 0.3
DESORB_RATE = 0.2
SURFACE_DIFFUSION = 2.0
REMOVAL = 0.5


def collide(populations, solid, knudsen):
    shape_tail = (19,) + (1,) * (populations.ndim - 1)
    weights = jnp.asarray(WEIGHT_TABLE, jnp.float32).reshape(shape_tail)
    along_x = jnp.asarray([velocity[0] for velocity in VELOCITIES], jnp.float32).reshape(shape_tail)
    along_y = jnp.asarray([velocity[1] for velocity in VELOCITIES], jnp.float32).reshape(shape_tail)
    along_z = jnp.asarray([velocity[2] for velocity in VELOCITIES], jnp.float32).reshape(shape_tail)
    weighted = weights * populations
    density = jnp.sum(weighted, axis=0)
    speed_x = jnp.sum(along_x * weighted, axis=0) / density
    speed_y = jnp.sum(along_y * weighted, axis=0) / density
    speed_z = jnp.sum(along_z * weighted, axis=0) / density
    projection = along_x * speed_x + along_y * speed_y + along_z * speed_z
    square = speed_x * speed_x + speed_y * speed_y + speed_z * speed_z
    balance = density * (1.0 + 3.0 * projection + 4.5 * projection * projection - 1.5 * square)
    relax_rate = 1.0 / (0.5 + 0.5 / (1.0 + 2.0 * knudsen))
    relaxed = populations - relax_rate * (populations - balance)
    bounced = populations[jnp.asarray(OPPOSITE, jnp.int32)]
    return jnp.where(solid == 1, bounced, relaxed)


def stencil(tile_grid, west_side, east_side, south_side, north_side, source):
    leftward = jnp.concatenate([west_side[:, :, None], tile_grid[:, :, :-1]], axis=2)
    rightward = jnp.concatenate([tile_grid[:, :, 1:], east_side[:, :, None]], axis=2)
    beneath = jnp.concatenate([south_side[:, None, :], tile_grid[:, :-1, :]], axis=1)
    overhead = jnp.concatenate([tile_grid[:, 1:, :], north_side[:, None, :]], axis=1)
    total = leftward + rightward + beneath + overhead
    return (source + SURFACE_DIFFUSION * total) / (1.0 + 4.0 * SURFACE_DIFFUSION)


def sweep_row(coverage_now, source, links):
    tile_grid = coverage_now.reshape(-1, TILE_SIDE, TILE_SIDE)
    far_index = TILE_SIDE - 1
    west_side = tile_grid[links[:, 0], :, far_index]
    east_side = tile_grid[links[:, 1], :, 0]
    south_side = tile_grid[links[:, 2], far_index, :]
    north_side = tile_grid[links[:, 3], 0, :]
    result = stencil(tile_grid, west_side, east_side, south_side, north_side, source.reshape(tile_grid.shape))
    return result.reshape(coverage_now.shape)


def collide_block(bundle):
    return collide(bundle[0], bundle[1], bundle[2])


def roll_member(bundle):
    return jnp.roll(bundle[0], (bundle[1], bundle[2], bundle[3]), axis=(0, 1, 2))


def supply_row(targets, values):
    return jnp.zeros((N_XY * WALLS,), jnp.float32).at[targets].add(values)


def reference(populations, solid, knudsen, wall_cells, wall_target, coverage, tile_links):
    blocks = populations.reshape(19, N_XY, CX, NY, NZ).transpose(1, 0, 2, 3, 4)
    collided = lax.map(collide_block, (blocks, solid.reshape(N_XY, CX, NY, NZ), knudsen.reshape(N_XY, CX, NY, NZ)))
    collided = collided.transpose(1, 0, 2, 3, 4).reshape(19, NX, NY, NZ)
    shift_x = jnp.asarray([velocity[0] for velocity in VELOCITIES], jnp.int32)
    shift_y = jnp.asarray([velocity[1] for velocity in VELOCITIES], jnp.int32)
    shift_z = jnp.asarray([velocity[2] for velocity in VELOCITIES], jnp.int32)
    read = lax.map(roll_member, (collided, shift_x, shift_y, shift_z))
    density = jnp.zeros((NX, NY, NZ), jnp.float32)
    for member in range(19):
        density = density + WEIGHT_TABLE[member] * read[member]
    cell_number = wall_cells.reshape(N_GZ, N_XY, WALLS)
    local_x = cell_number // (NY * CZ)
    grid_y = (cell_number // CZ) % NY
    local_z = cell_number % CZ
    grid_x = jnp.arange(N_XY, dtype=jnp.int32)[None, :, None] * CX + local_x
    grid_z = jnp.arange(N_GZ, dtype=jnp.int32)[:, None, None] * CZ + local_z
    wall_density = density[grid_x, grid_y, grid_z].reshape(N_GZ, N_XY * WALLS)
    supply = jax.vmap(supply_row)(wall_target, wall_density)
    initial = coverage.reshape(N_GZ, ROW_TILES, PATCH)
    supply = supply.reshape(initial.shape)
    source = initial + ADSORB_RATE * supply * (1.0 - initial) - DESORB_RATE * initial
    links = tile_links.reshape(N_GZ, ROW_TILES, 4)
    coverage_now = initial
    for sweep_index in range(SWEEPS):
        coverage_now = jax.vmap(sweep_row)(coverage_now, source, links)
    change = (coverage_now - initial).reshape(N_GZ, N_XY * WALLS)
    wall_change = jnp.take_along_axis(change, wall_target, axis=1).reshape(N_GZ, N_XY, WALLS)
    updated = read.at[:, grid_x, grid_y, grid_z].add(-REMOVAL * wall_change[None])
    return updated, coverage_now.reshape(TILES, PATCH)
```

```python
import jax
import jax.numpy as jnp
from jax import lax
from jax.experimental import pallas as pl
from jax.experimental.pallas import tpu as pltpu
from jax.sharding import PartitionSpec as P

MESH = pl.DeviceIdType.MESH
F32 = jnp.float32
BF16 = jnp.bfloat16

VELOCITIES = [
    (0, 0, 0),
    (0, 1, 0),
    (0, -1, 0),
    (1, 0, 0),
    (-1, 0, 0),
    (0, 0, 1),
    (0, 0, -1),
    (1, 1, 0),
    (-1, -1, 0),
    (1, -1, 0),
    (-1, 1, 0),
    (1, 0, 1),
    (-1, 0, -1),
    (1, 0, -1),
    (-1, 0, 1),
    (0, 1, 1),
    (0, -1, -1),
    (0, 1, -1),
    (0, -1, 1),
]
WEIGHTS = [1.0 / 3.0] + [1.0 / 18.0] * 6 + [1.0 / 36.0] * 12
X_PLUS = [q for q in range(19) if VELOCITIES[q][0] == 1]
X_MINUS = [q for q in range(19) if VELOCITIES[q][0] == -1]
Z_PLUS = [q for q in range(19) if VELOCITIES[q][2] == 1]
Z_MINUS = [q for q in range(19) if VELOCITIES[q][2] == -1]

N_GZ = 8
N_XY = 32
CX = 8
NY = 32
CZ = 128
SLOTS = 256
CHUNKS = 16
OTHERS = N_XY - 1
GREETED = OTHERS + 6


def iota(shape, dim):
    return lax.broadcasted_iota(jnp.int32, shape, dim)


def split(values):
    high = values.astype(BF16)
    low = (values - high.astype(F32)).astype(BF16)
    return high, low


def hits(mask):
    return jnp.where(mask, 1.0, 0.0).astype(BF16)


def dot(left, right):
    return lax.dot_general(left, right, (((1,), (0,)), ((), ())), preferred_element_type=F32)


def dot_nt(left, right):
    return lax.dot_general(left, right, (((1,), (1,)), ((), ())), preferred_element_type=F32)


def roll(values, shift, axis):
    shift = shift % values.shape[axis]
    return values if shift == 0 else pltpu.roll(values, shift, axis)


def edge_picker():
    cell, lane = iota((512, 128), 0), iota((512, 128), 1)
    side, place = (lane >> 4) & 3, lane & 15
    wanted = jnp.where(
        side == 0,
        place * 16 + 15,
        jnp.where(side == 1, place * 16, jnp.where(side == 2, 240 + place, place)),
    )
    return hits(cell == (lane >> 6) * 256 + wanted)


def tile_edges(cover, picker):
    both = jnp.concatenate([cover[0:8], cover[8:16]], axis=1)
    high, low = split(both)
    return dot(high, picker) + dot(low, picker)


def neighbour_matrix():
    a, b = iota((256, 256), 0), iota((256, 256), 1)
    same_row = (a >> 4) == (b >> 4)
    near = (same_row & (jnp.abs(a - b) == 1)) | (jnp.abs(a - b) == 16)
    inner = hits(near)
    s, k = iota((128, 256), 0), iota((128, 256), 1)
    side, place = (s >> 4) & 3, s & 15
    cell = jnp.where(
        side == 0,
        place * 16,
        jnp.where(side == 1, place * 16 + 15, jnp.where(side == 2, place, 240 + place)),
    )
    return jnp.concatenate([inner, inner, hits(k == cell)], axis=0)


def gather_edges(edges, link_hits, link_half):
    high, low = split(edges)
    found = dot(link_hits, jnp.concatenate([high, low], axis=1))
    lane = iota((16, 64), 1)
    out_high = jnp.zeros((16, 64), F32)
    out_low = jnp.zeros((16, 64), F32)
    for side in range(4):
        part = found[side * 16 : (side + 1) * 16]
        second = link_half[side] == 1
        h = jnp.where(second, part[:, 64:128], part[:, 0:64])
        l = jnp.where(second, part[:, 192:256], part[:, 128:192])
        here = (lane >> 4) == side
        out_high = jnp.where(here, h, out_high)
        out_low = jnp.where(here, l, out_low)
    return jnp.concatenate([out_high, out_low], axis=1)


def sweep(cover, source, borders, matrix):
    high, low = split(cover)
    row = jnp.concatenate([high, low, borders.astype(BF16)], axis=1)
    return (source + 2.0 * dot(row, matrix)) * (1.0 / 9.0)


def kernel(
    pop_hbm,
    solid_hbm,
    knudsen_hbm,
    cells_ref,
    targets_ref,
    cover_ref,
    links_ref,
    read_hbm,
    cover_out,
    correction_out,
    pop,
    solid,
    knudsen,
    rd,
    zs_p,
    zs_m,
    zr_p,
    zr_m,
    dens,
    owner_hits,
    slot_xy,
    slot_z,
    place_send,
    place_recv,
    value_send,
    value_recv,
    change_send,
    change_recv,
    edge_send0,
    edge_recv0,
    edge_send1,
    edge_recv1,
    corr_acc,
    load_sem,
    store_sem,
    halo_send,
    halo_recv,
    all_send,
    all_recv,
):
    gz = lax.axis_index("gz")
    me = lax.axis_index("xy")
    gz_up, gz_down = lax.rem(gz + 1, N_GZ), lax.rem(gz + N_GZ - 1, N_GZ)
    up, down = lax.rem(me + 1, N_XY), lax.rem(me + N_XY - 1, N_XY)

    loads = [
        pltpu.make_async_copy(solid_hbm, solid, load_sem.at[8]),
        pltpu.make_async_copy(knudsen_hbm, knudsen, load_sem.at[9]),
    ]
    for copy in loads:
        copy.start()
    for x in (0, 7, 1, 2, 3, 4, 5, 6):
        pltpu.make_async_copy(pop_hbm.at[:, x], pop.at[:, x], load_sem.at[x]).start()

    barrier = pltpu.get_barrier_semaphore()

    def greet(i, unused):
        other = lax.rem(me + i, N_XY)
        pl.semaphore_signal(barrier, inc=1, device_id=(gz, other), device_id_type=MESH)
        return unused

    for device in (
        (gz_up, me),
        (gz_down, me),
        (gz_up, up),
        (gz_up, down),
        (gz_down, up),
        (gz_down, down),
    ):
        pl.semaphore_signal(barrier, inc=1, device_id=device, device_id_type=MESH)
    lax.fori_loop(1, N_XY, greet, 0)

    picker = edge_picker()
    cover = cover_ref[...]
    edges = tile_edges(cover, picker)
    edge_send0[...] = edges
    edge_recv0[me] = edges
    pl.semaphore_wait(barrier, GREETED)

    def to_all(source_of, target_ref, index):
        def send(i, unused):
            other = lax.rem(me + i, N_XY)
            pltpu.make_async_remote_copy(
                src_ref=source_of(other),
                dst_ref=target_ref.at[me],
                send_sem=all_send.at[index],
                recv_sem=all_recv.at[index],
                device_id=(gz, other),
                device_id_type=MESH,
            ).start()
            return unused

        lax.fori_loop(1, N_XY, send, 0)

    def all_copy(ref, index):
        part = ref.at[pl.ds(0, OTHERS)]
        return pltpu.make_async_remote_copy(
            src_ref=part,
            dst_ref=part,
            send_sem=all_send.at[index],
            recv_sem=all_recv.at[index],
            device_id=(gz, up),
            device_id_type=MESH,
        )

    to_all(lambda other: edge_send0, edge_recv0, 0)

    for copy in loads:
        copy.wait()
    lane8 = iota((8, 128), 1)

    def collide_plane(x):
        pltpu.make_async_copy(pop_hbm.at[:, x], pop.at[:, x], load_sem.at[x]).wait()
        kn = knudsen[x]
        sol = solid[x] == 1
        axis_sum = jnp.zeros((NY, CZ), F32)
        diag_sum = jnp.zeros((NY, CZ), F32)
        axis_m = [None] * 3
        diag_m = [None] * 3
        for q in range(1, 19, 2):
            p, m = pop[q, x], pop[q + 1, x]
            if q < 7:
                axis_sum = axis_sum + (p + m)
            else:
                diag_sum = diag_sum + (p + m)
            diff = p - m
            for axis in range(3):
                c = VELOCITIES[q][axis]
                sums = axis_m if q < 7 else diag_m
                if c == 0:
                    continue
                if sums[axis] is None:
                    sums[axis] = diff if c == 1 else -diff
                else:
                    sums[axis] = sums[axis] + diff if c == 1 else sums[axis] - diff
        rest = pop[0, x]
        density = (1.0 / 3.0) * rest + (1.0 / 18.0) * axis_sum + (1.0 / 36.0) * diag_sum
        inverse = 1.0 / density
        speed = [
            ((1.0 / 18.0) * axis_m[axis] + (1.0 / 36.0) * diag_m[axis]) * inverse
            for axis in range(3)
        ]
        square = speed[0] * speed[0] + speed[1] * speed[1] + speed[2] * speed[2]
        relax = (1.0 + 2.0 * kn) / (1.0 + kn)
        keep = 1.0 - relax
        gain = relax * density
        base = gain - 1.5 * gain * square
        gain3 = 3.0 * gain
        rd[0, x + 1] = jnp.where(sol, rest, keep * rest + base)
        tile_p = jnp.zeros((8, 128), F32)
        tile_m = jnp.zeros((8, 128), F32)
        for q in range(1, 19, 2):
            p, m = pop[q, x], pop[q + 1, x]
            along = None
            for axis in range(3):
                c = VELOCITIES[q][axis]
                if c == 0:
                    continue
                if along is None:
                    along = speed[axis] if c == 1 else -speed[axis]
                else:
                    along = along + speed[axis] if c == 1 else along - speed[axis]
            odd = gain3 * along
            even = base + 1.5 * odd * along
            new_p = jnp.where(sol, m, keep * p + (even + odd))
            new_m = jnp.where(sol, p, keep * m + (even - odd))
            for member, value in ((q, new_p), (q + 1, new_m)):
                cx, cy, cz = VELOCITIES[member]
                value = roll(value, cy, 0)
                value = roll(value, cz, 1)
                rd[member, x + 1 + cx] = value
                if cz == 1:
                    k = Z_PLUS.index(member)
                    for block in range(4):
                        at = k * 4 + block
                        moved = roll(value[block * 8 : block * 8 + 8], at, 1)
                        tile_p = jnp.where(lane8 == at, moved, tile_p)
                if cz == -1:
                    k = Z_MINUS.index(member)
                    for block in range(4):
                        at = k * 4 + block
                        moved = roll(value[block * 8 : block * 8 + 8], at + 1, 1)
                        tile_m = jnp.where(lane8 == at, moved, tile_m)
        zs_p[x] = tile_p
        zs_m[x] = tile_m

    def edge_step(i, unused):
        collide_plane(i * 7)
        return unused

    def inner_step(i, unused):
        collide_plane(i)
        return unused

    def halo(source, target, index, device):
        return pltpu.make_async_remote_copy(
            src_ref=source,
            dst_ref=target,
            send_sem=halo_send.at[index],
            recv_sem=halo_recv.at[index],
            device_id=device,
            device_id_type=MESH,
        )

    lax.fori_loop(0, 2, edge_step, 0)
    halos = []
    for k in range(5):
        halos.append(halo(rd.at[X_PLUS[k], 9], rd.at[X_PLUS[k], 1], k, (gz, up)))
        halos.append(halo(rd.at[X_MINUS[k], 0], rd.at[X_MINUS[k], 8], 5 + k, (gz, down)))
    halos.append(halo(zs_p.at[7], zr_p.at[0], 12, (gz_up, up)))
    halos.append(halo(zs_p.at[0], zr_p.at[9], 13, (gz_up, down)))
    halos.append(halo(zs_m.at[7], zr_m.at[0], 14, (gz_down, up)))
    halos.append(halo(zs_m.at[0], zr_m.at[9], 15, (gz_down, down)))
    for copy in halos:
        copy.start()
    lax.fori_loop(1, 7, inner_step, 0)
    faces = [
        halo(zs_p, zr_p.at[pl.ds(1, CX)], 10, (gz_up, me)),
        halo(zs_m, zr_m.at[pl.ds(1, CX)], 11, (gz_down, me)),
    ]
    for copy in faces:
        copy.start()
    halos = halos + faces

    owner_row = iota((N_XY, SLOTS), 0)

    def mark_owner(c, unused):
        owner = targets_ref[c] >> 12
        start = pl.multiple_of(c * N_XY, N_XY)
        owner_hits[pl.ds(start, N_XY), :] = hits(owner_row == owner)
        return unused

    lax.fori_loop(0, CHUNKS, mark_owner, 0)
    before = hits(iota((SLOTS, SLOTS), 0) < iota((SLOTS, SLOTS), 1))
    ones = jnp.ones((SLOTS, SLOTS), BF16)
    rank_row = iota((SLOTS, SLOTS), 0)

    def fill_slots(c, carry):
        base, table = carry
        start = pl.multiple_of(c * N_XY, N_XY)
        marks = owner_hits[pl.ds(start, N_XY), :]
        ranks = dot(marks, before) + base
        base = base + dot(marks, ones)
        target = targets_ref[c]
        cell = cells_ref[c]
        mine = owner_row == (target >> 12)
        rank = jnp.sum(jnp.where(mine, ranks, 0.0), axis=0, keepdims=True).astype(jnp.int32)
        place = target & 4095
        fields = [
            cell >> 7,
            (cell & 127) + 1,
            ((place >> 7) & 1) * 16 + (place >> 8),
            place & 127,
        ]
        left = jnp.concatenate(
            [jnp.where(mine, field.astype(F32), 0.0) for field in fields], axis=0
        ).astype(BF16)
        return base, table + dot_nt(left, hits(rank_row == rank))

    unused, table = lax.fori_loop(
        0,
        CHUNKS,
        fill_slots,
        (jnp.zeros((N_XY, SLOTS), F32), jnp.zeros((4 * N_XY, SLOTS), F32)),
    )
    places = table[64:96] * 128.0 + table[96:128]
    for owner in range(N_XY):
        slot_xy[owner] = table[owner : owner + 1]
        slot_z[owner] = table[32 + owner : 33 + owner] - 1.0
        place_send[owner] = places[owner : owner + 1]
    place_recv[me] = place_send[me]
    to_all(lambda other: place_send.at[other], place_recv, 1)

    for copy in halos:
        copy.wait_recv()

    def finish_plane(x, unused):
        lane = iota((NY, CZ), 1)
        total = None
        for q in range(19):
            cx, cy, cz = VELOCITIES[q]
            value = rd[q, x + 1]
            if cz != 0:
                k = (Z_PLUS if cz == 1 else Z_MINUS).index(q)
                got = (zr_p if cz == 1 else zr_m)[x - cx + 1]
                edge = 0 if cz == 1 else 127
                border = jnp.concatenate(
                    [roll(got, edge - (k * 4 + block), 1) for block in range(4)], axis=0
                )
                value = jnp.where(lane == edge, border, value)
                rd[q, x + 1] = value
            term = WEIGHTS[q] * value
            total = term if total is None else total + term
        dens[pl.ds(pl.multiple_of(x * NY, NY), NY), :] = total
        return unused

    lax.fori_loop(0, CX, finish_plane, 0)
    store = pltpu.make_async_copy(rd.at[:, pl.ds(1, CX)], read_hbm, store_sem)
    store.start()

    high, low = split(jnp.transpose(dens[...]))
    dens_t = jnp.concatenate([high, low], axis=0)
    row256 = iota((SLOTS, SLOTS), 0).astype(F32)
    row128 = iota((CZ, SLOTS), 0).astype(F32)
    row32 = iota((N_XY, SLOTS), 0).astype(F32)

    def slot_density(owner):
        found = dot(dens_t, hits(row256 == slot_xy[owner]))
        both = found[0:128] + found[128:256]
        return jnp.sum(jnp.where(row128 == slot_z[owner], both, 0.0), axis=0, keepdims=True)

    def send_value(i, unused):
        other = lax.rem(me + i, N_XY)
        value_send[other] = slot_density(other)
        pltpu.make_async_remote_copy(
            src_ref=value_send.at[other],
            dst_ref=value_recv.at[me],
            send_sem=all_send.at[2],
            recv_sem=all_recv.at[2],
            device_id=(gz, other),
            device_id_type=MESH,
        ).start()
        return unused

    lax.fori_loop(1, N_XY, send_value, 0)
    value_recv[me] = slot_density(me)
    links = links_ref[...]
    link_hits = []
    link_half = []
    lane256 = iota((16, 256), 1)
    for side in range(4):
        tile = links[:, side : side + 1]
        link_hits.append(hits(lane256 == (tile >> 4) * 8 + (tile & 7)))
        link_half.append((tile >> 3) & 1)
    link_hits = jnp.concatenate(link_hits, axis=0)
    matrix = neighbour_matrix()
    all_copy(edge_recv0, 0).wait_recv()
    borders = gather_edges(edge_recv0[...].reshape(256, 128), link_hits, link_half)
    all_copy(place_recv, 1).wait_recv()
    all_copy(value_recv, 2).wait_recv()

    def add_supply(i, total):
        value = value_recv[i]
        place = place_recv[i]
        row = jnp.floor(place * (1.0 / 128.0))
        here = row32 == row
        high = value.astype(BF16).astype(F32)
        left = jnp.concatenate(
            [jnp.where(here, high, 0.0), jnp.where(here, value - high, 0.0)], axis=0
        ).astype(BF16)
        return total + dot_nt(left, hits(row128 == place - 128.0 * row))

    supply = lax.fori_loop(0, N_XY, add_supply, jnp.zeros((64, 128), F32))
    supply = supply[0:32] + supply[32:64]
    supply = jnp.concatenate([supply[0:16], supply[16:32]], axis=1)
    source = cover + 0.3 * supply * (1.0 - cover) - 0.2 * cover
    first = sweep(cover, source, borders, matrix)
    edges = tile_edges(first, picker)
    edge_send1[...] = edges
    edge_recv1[me] = edges
    to_all(lambda other: edge_send1, edge_recv1, 3)
    all_copy(edge_recv1, 3).wait_recv()
    borders = gather_edges(edge_recv1[...].reshape(256, 128), link_hits, link_half)
    second = sweep(first, source, borders, matrix)
    cover_out[...] = second
    change = -0.5 * (second - cover)
    change = jnp.concatenate([change[:, 0:128], change[:, 128:256]], axis=0)
    high, low = split(change)
    change = jnp.concatenate([high, low], axis=0)

    def slot_change(brick):
        place = place_recv[brick]
        row = jnp.floor(place * (1.0 / 128.0))
        found = dot(change, hits(row128 == place - 128.0 * row))
        both = found[0:32] + found[32:64]
        return jnp.sum(jnp.where(row32 == row, both, 0.0), axis=0, keepdims=True)

    def send_change(i, unused):
        other = lax.rem(me + i, N_XY)
        change_send[other] = slot_change(other)
        pltpu.make_async_remote_copy(
            src_ref=change_send.at[other],
            dst_ref=change_recv.at[me],
            send_sem=all_send.at[4],
            recv_sem=all_recv.at[4],
            device_id=(gz, other),
            device_id_type=MESH,
        ).start()
        return unused

    lax.fori_loop(1, N_XY, send_change, 0)
    change_recv[me] = slot_change(me)
    corr_acc[...] = jnp.zeros_like(corr_acc)
    all_copy(change_recv, 4).wait_recv()

    def add_change(owner, unused):
        value = change_recv[owner]
        here = row128 == slot_z[owner]
        high = value.astype(BF16).astype(F32)
        right = jnp.concatenate(
            [jnp.where(here, high, 0.0), jnp.where(here, value - high, 0.0)], axis=0
        ).astype(BF16)
        corr_acc[...] += dot_nt(hits(row256 == slot_xy[owner]), right)
        return unused

    lax.fori_loop(0, N_XY, add_change, 0)
    correction_out[...] = corr_acc[:, 0:128] + corr_acc[:, 128:256]

    for copy in halos:
        copy.wait_send()
    for ref, index in (
        (edge_recv0, 0),
        (place_recv, 1),
        (value_recv, 2),
        (edge_recv1, 3),
        (change_recv, 4),
    ):
        all_copy(ref, index).wait_send()
    store.wait()


def shards(populations, solid, knudsen, wall_cells, wall_target, coverage, tile_links):
    anywhere = pl.BlockSpec(memory_space=pl.ANY)
    vmem = pl.BlockSpec(memory_space=pltpu.VMEM)
    slots = pltpu.VMEM((N_XY, 1, SLOTS), F32)
    edge_table = pltpu.VMEM((N_XY, 8, 128), F32)
    read, new_coverage, correction = pl.pallas_call(
        kernel,
        out_shape=(
            jax.ShapeDtypeStruct((19, CX, NY, CZ), F32),
            jax.ShapeDtypeStruct((16, 256), F32),
            jax.ShapeDtypeStruct((256, 128), F32),
        ),
        in_specs=[anywhere] * 3 + [vmem] * 4,
        out_specs=(anywhere, vmem, vmem),
        scratch_shapes=[
            pltpu.VMEM((19, CX, NY, CZ), F32),
            pltpu.VMEM((CX, NY, CZ), jnp.int32),
            pltpu.VMEM((CX, NY, CZ), F32),
            pltpu.VMEM((19, CX + 2, NY, CZ), F32),
            pltpu.VMEM((CX, 8, 128), F32),
            pltpu.VMEM((CX, 8, 128), F32),
            pltpu.VMEM((CX + 2, 8, 128), F32),
            pltpu.VMEM((CX + 2, 8, 128), F32),
            pltpu.VMEM((CX * NY, CZ), F32),
            pltpu.VMEM((CHUNKS * N_XY, SLOTS), BF16),
            slots,
            slots,
            slots,
            slots,
            slots,
            slots,
            slots,
            slots,
            pltpu.VMEM((8, 128), F32),
            edge_table,
            pltpu.VMEM((8, 128), F32),
            edge_table,
            pltpu.VMEM((256, 256), F32),
            pltpu.SemaphoreType.DMA((10,)),
            pltpu.SemaphoreType.DMA,
            pltpu.SemaphoreType.DMA((16,)),
            pltpu.SemaphoreType.DMA((16,)),
            pltpu.SemaphoreType.DMA((5,)),
            pltpu.SemaphoreType.DMA((5,)),
        ],
        compiler_params=pltpu.CompilerParams(
            collective_id=0, has_side_effects=True, vmem_limit_bytes=32 * 1024 * 1024
        ),
    )(
        populations,
        solid,
        knudsen,
        wall_cells.reshape(CHUNKS, 1, SLOTS),
        wall_target.reshape(CHUNKS, 1, SLOTS),
        coverage,
        tile_links,
    )
    updated = read + correction.reshape(1, CX, NY, CZ)
    return updated, new_coverage


def solution(mesh):
    in_specs = (
        P(None, "xy", None, "gz"),
        P("xy", None, "gz"),
        P("xy", None, "gz"),
        P("gz", "xy"),
        P("gz", "xy"),
        P(("gz", "xy"), None),
        P(("gz", "xy"), None),
    )
    out_specs = (P(None, "xy", None, "gz"), P(("gz", "xy"), None))
    return jax.shard_map(shards, mesh=mesh, in_specs=in_specs, out_specs=out_specs, check_vma=False)
```

```python
import jax
import jax.numpy as jnp
from jax import lax
from jax.experimental import pallas as pl
from jax.experimental.pallas import tpu as pltpu
from jax.sharding import PartitionSpec as P

MESH = pl.DeviceIdType.MESH
F32 = jnp.float32
BF16 = jnp.bfloat16

VELOCITIES = [
    (0, 0, 0),
    (0, 1, 0),
    (0, -1, 0),
    (1, 0, 0),
    (-1, 0, 0),
    (0, 0, 1),
    (0, 0, -1),
    (1, 1, 0),
    (-1, -1, 0),
    (1, -1, 0),
    (-1, 1, 0),
    (1, 0, 1),
    (-1, 0, -1),
    (1, 0, -1),
    (-1, 0, 1),
    (0, 1, 1),
    (0, -1, -1),
    (0, 1, -1),
    (0, -1, 1),
]
WEIGHTS = [1.0 / 3.0] + [1.0 / 18.0] * 6 + [1.0 / 36.0] * 12
X_PLUS = [q for q in range(19) if VELOCITIES[q][0] == 1]
X_MINUS = [q for q in range(19) if VELOCITIES[q][0] == -1]
Z_PLUS = [q for q in range(19) if VELOCITIES[q][2] == 1]
Z_MINUS = [q for q in range(19) if VELOCITIES[q][2] == -1]

N_GZ = 8
N_XY = 32
CX = 8
NY = 32
CZ = 128
SLOTS = 256
CHUNKS = 16
OTHERS = N_XY - 1
GREETED = OTHERS + 6
GROUP = 4
GROUPS = N_XY // GROUP


def iota(shape, dim):
    return lax.broadcasted_iota(jnp.int32, shape, dim)


def split(values):
    high = values.astype(BF16)
    low = (values - high.astype(F32)).astype(BF16)
    return high, low


def hits(mask):
    return jnp.where(mask, 1.0, 0.0).astype(BF16)


def hits16(rows, row):
    return jnp.where(rows == row.astype(BF16), BF16(1.0), BF16(0.0))


def dot(left, right):
    return lax.dot_general(left, right, (((1,), (0,)), ((), ())), preferred_element_type=F32)


def dot_nt(left, right):
    return lax.dot_general(left, right, (((1,), (1,)), ((), ())), preferred_element_type=F32)


def centred(step, size):
    return size // 2 + ((step + 1) // 2) * (1 - 2 * (step % 2))


def partner(me, step):
    z = (me % 8 + centred(step // 4, 8)) % 8
    x = (me // 8 + centred(step % 4, 4)) % 4
    return x * 8 + z


def roll(values, shift, axis):
    shift = shift % values.shape[axis]
    return values if shift == 0 else pltpu.roll(values, shift, axis)


def edge_picker():
    cell, lane = iota((512, 128), 0), iota((512, 128), 1)
    side, place = (lane >> 4) & 3, lane & 15
    wanted = jnp.where(
        side == 0,
        place * 16 + 15,
        jnp.where(side == 1, place * 16, jnp.where(side == 2, 240 + place, place)),
    )
    return hits(cell == (lane >> 6) * 256 + wanted)


def tile_edges(cover, picker):
    both = jnp.concatenate([cover[0:8], cover[8:16]], axis=1)
    high, low = split(both)
    return dot(high, picker) + dot(low, picker)


def neighbour_matrix():
    a, b = iota((256, 256), 0), iota((256, 256), 1)
    same_row = (a >> 4) == (b >> 4)
    near = (same_row & (jnp.abs(a - b) == 1)) | (jnp.abs(a - b) == 16)
    inner = hits(near)
    s, k = iota((128, 256), 0), iota((128, 256), 1)
    side, place = (s >> 4) & 3, s & 15
    cell = jnp.where(
        side == 0,
        place * 16,
        jnp.where(side == 1, place * 16 + 15, jnp.where(side == 2, place, 240 + place)),
    )
    return jnp.concatenate([inner, inner, hits(k == cell)], axis=0)


def gather_edges(edges, link_hits, link_half):
    high, low = split(edges)
    found = dot(link_hits, jnp.concatenate([high, low], axis=1))
    lane = iota((16, 64), 1)
    out_high = jnp.zeros((16, 64), F32)
    out_low = jnp.zeros((16, 64), F32)
    for side in range(4):
        part = found[side * 16 : (side + 1) * 16]
        second = link_half[side] == 1
        h = jnp.where(second, part[:, 64:128], part[:, 0:64])
        l = jnp.where(second, part[:, 192:256], part[:, 128:192])
        here = (lane >> 4) == side
        out_high = jnp.where(here, h, out_high)
        out_low = jnp.where(here, l, out_low)
    return jnp.concatenate([out_high, out_low], axis=1)


def sweep(cover, source, borders, matrix):
    high, low = split(cover)
    row = jnp.concatenate([high, low, borders.astype(BF16)], axis=1)
    return (source + 2.0 * dot(row, matrix)) * (1.0 / 9.0)


def kernel(
    pop_hbm,
    solid_hbm,
    knudsen_hbm,
    cells_hbm,
    targets_hbm,
    cover_hbm,
    links_hbm,
    read_ref,
    cover_out,
    correction_out,
    pop,
    solid,
    knudsen,
    cells_ref,
    targets_ref,
    cover_ref,
    links_ref,
    rd,
    zs_p,
    zs_m,
    zr_p,
    zr_m,
    dens,
    owner_hits,
    ranks_ref,
    totals_ref,
    xy_hits,
    lane_hits,
    slot_xy,
    slot_z,
    place_row,
    place_send,
    place_recv,
    value_send,
    value_recv,
    change_send,
    change_recv,
    edge_send0,
    edge_recv0,
    edge_send1,
    edge_recv1,
    corr_acc,
    load_sem,
    halo_send,
    halo_recv,
    all_send,
    all_recv,
):
    gz = lax.axis_index("gz")
    me = lax.axis_index("xy")
    gz_up, gz_down = lax.rem(gz + 1, N_GZ), lax.rem(gz + N_GZ - 1, N_GZ)
    up, down = lax.rem(me + 1, N_XY), lax.rem(me + N_XY - 1, N_XY)

    def load(source, target, index):
        copy = pltpu.make_async_copy(source, target, load_sem.at[index])
        copy.start()
        return copy

    plane_loads = {}
    plane_loads[0] = load(pop_hbm.at[:, 0], pop.at[:, 0], 0)
    cell_loads = [load(solid_hbm, solid, 8), load(knudsen_hbm, knudsen, 9)]
    plane_loads[7] = load(pop_hbm.at[:, 7], pop.at[:, 7], 7)
    for x in range(1, 7):
        plane_loads[x] = load(pop_hbm.at[:, x], pop.at[:, x], x)
    wall_loads = [
        load(cells_hbm, cells_ref, 10),
        load(targets_hbm, targets_ref, 11),
        load(cover_hbm, cover_ref, 12),
        load(links_hbm, links_ref, 13),
    ]

    barrier = pltpu.get_barrier_semaphore()

    def greet(i, unused):
        pl.semaphore_signal(
            barrier, inc=1, device_id=(gz, partner(me, i)), device_id_type=MESH
        )
        return unused

    lax.fori_loop(0, OTHERS, greet, 0)
    for device in (
        (gz_up, up),
        (gz_up, down),
        (gz_down, up),
        (gz_down, down),
        (gz_up, me),
        (gz_down, me),
    ):
        pl.semaphore_signal(barrier, inc=1, device_id=device, device_id_type=MESH)

    def send_one(source, target, index, other):
        pltpu.make_async_remote_copy(
            src_ref=source,
            dst_ref=target,
            send_sem=all_send.at[index],
            recv_sem=all_recv.at[index],
            device_id=(gz, other),
            device_id_type=MESH,
        ).start()

    def send_steps(source_of, target_ref, index, first, last):
        def send(i, unused):
            other = partner(me, i)
            send_one(source_of(other), target_ref.at[me], index, other)
            return unused

        lax.fori_loop(first, last, send, 0)

    def all_copy(ref, index):
        part = ref.at[pl.ds(0, OTHERS)]
        return pltpu.make_async_remote_copy(
            src_ref=part,
            dst_ref=part,
            send_sem=all_send.at[index],
            recv_sem=all_recv.at[index],
            device_id=(gz, up),
            device_id_type=MESH,
        )

    lane8 = iota((8, 128), 1)

    def collide_plane(x):
        kn = knudsen[x]
        sol = solid[x] == 1
        axis_sum = jnp.zeros((NY, CZ), F32)
        diag_sum = jnp.zeros((NY, CZ), F32)
        axis_m = [None] * 3
        diag_m = [None] * 3
        for q in range(1, 19, 2):
            p, m = pop[q, x], pop[q + 1, x]
            if q < 7:
                axis_sum = axis_sum + (p + m)
            else:
                diag_sum = diag_sum + (p + m)
            diff = p - m
            for axis in range(3):
                c = VELOCITIES[q][axis]
                sums = axis_m if q < 7 else diag_m
                if c == 0:
                    continue
                if sums[axis] is None:
                    sums[axis] = diff if c == 1 else -diff
                else:
                    sums[axis] = sums[axis] + diff if c == 1 else sums[axis] - diff
        rest = pop[0, x]
        density = (1.0 / 3.0) * rest + (1.0 / 18.0) * axis_sum + (1.0 / 36.0) * diag_sum
        inverse = 1.0 / density
        speed = [
            ((1.0 / 18.0) * axis_m[axis] + (1.0 / 36.0) * diag_m[axis]) * inverse
            for axis in range(3)
        ]
        square = speed[0] * speed[0] + speed[1] * speed[1] + speed[2] * speed[2]
        relax = (1.0 + 2.0 * kn) / (1.0 + kn)
        keep = 1.0 - relax
        gain = relax * density
        base = gain - 1.5 * gain * square
        gain3 = 3.0 * gain
        rd[0, x + 1] = jnp.where(sol, rest, keep * rest + base)
        tile_p = jnp.zeros((8, 128), F32)
        tile_m = jnp.zeros((8, 128), F32)
        for q in range(1, 19, 2):
            p, m = pop[q, x], pop[q + 1, x]
            along = None
            for axis in range(3):
                c = VELOCITIES[q][axis]
                if c == 0:
                    continue
                if along is None:
                    along = speed[axis] if c == 1 else -speed[axis]
                else:
                    along = along + speed[axis] if c == 1 else along - speed[axis]
            odd = gain3 * along
            even = base + 1.5 * odd * along
            new_p = jnp.where(sol, m, keep * p + (even + odd))
            new_m = jnp.where(sol, p, keep * m + (even - odd))
            for member, value in ((q, new_p), (q + 1, new_m)):
                cx, cy, cz = VELOCITIES[member]
                value = roll(value, cy, 0)
                value = roll(value, cz, 1)
                rd[member, x + 1 + cx] = value
                if cz == 1:
                    k = Z_PLUS.index(member)
                    for block in range(4):
                        at = k * 4 + block
                        moved = roll(value[block * 8 : block * 8 + 8], at, 1)
                        tile_p = jnp.where(lane8 == at, moved, tile_p)
                if cz == -1:
                    k = Z_MINUS.index(member)
                    for block in range(4):
                        at = k * 4 + block
                        moved = roll(value[block * 8 : block * 8 + 8], at + 1, 1)
                        tile_m = jnp.where(lane8 == at, moved, tile_m)
        zs_p[x] = tile_p
        zs_m[x] = tile_m

    def edge_step(i, unused):
        collide_plane(i * 7)
        return unused

    def inner_step(i, unused):
        collide_plane(i)
        return unused

    def halo(source, target, index, device):
        return pltpu.make_async_remote_copy(
            src_ref=source,
            dst_ref=target,
            send_sem=halo_send.at[index],
            recv_sem=halo_recv.at[index],
            device_id=device,
            device_id_type=MESH,
        )

    for copy in cell_loads + [plane_loads[0], plane_loads[7]]:
        copy.wait()
    lax.fori_loop(0, 2, edge_step, 0)
    pl.semaphore_wait(barrier, GREETED)
    halos = []
    halos.append(halo(zs_p.at[7], zr_p.at[0], 12, (gz_up, up)))
    halos.append(halo(zs_p.at[0], zr_p.at[9], 13, (gz_up, down)))
    halos.append(halo(zs_m.at[7], zr_m.at[0], 14, (gz_down, up)))
    halos.append(halo(zs_m.at[0], zr_m.at[9], 15, (gz_down, down)))
    for k in range(5):
        halos.append(halo(rd.at[X_PLUS[k], 9], rd.at[X_PLUS[k], 1], k, (gz, up)))
        halos.append(halo(rd.at[X_MINUS[k], 0], rd.at[X_MINUS[k], 8], 5 + k, (gz, down)))
    for copy in halos:
        copy.start()
    for x in range(1, 7):
        plane_loads[x].wait()
    lax.fori_loop(1, 7, inner_step, 0)
    faces = [
        halo(zs_p, zr_p.at[pl.ds(1, CX)], 10, (gz_up, me)),
        halo(zs_m, zr_m.at[pl.ds(1, CX)], 11, (gz_down, me)),
    ]
    for copy in faces:
        copy.start()
    halos = halos + faces
    for copy in wall_loads:
        copy.wait()

    picker = edge_picker()
    cover = cover_ref[...]
    edges = tile_edges(cover, picker)
    edge_send0[...] = edges
    edge_recv0[me] = edges
    send_steps(lambda other: edge_send0, edge_recv0, 0, 0, OTHERS)

    owner_row = iota((N_XY, SLOTS), 0)
    row256 = iota((SLOTS, SLOTS), 0).astype(F32).astype(BF16)
    row128 = iota((CZ, SLOTS), 0).astype(F32)
    row128_16 = row128.astype(BF16)
    row32 = iota((N_XY, SLOTS), 0).astype(F32)

    for c in range(CHUNKS):
        owner_hits[c * N_XY : (c + 1) * N_XY, :] = hits(owner_row == (targets_ref[c] >> 12))
    before = hits(iota((SLOTS, SLOTS), 0) < iota((SLOTS, SLOTS), 1))
    ranks_ref[...] = dot(owner_hits[...], before)
    totals_ref[...] = dot(owner_hits[...], jnp.ones((SLOTS, SLOTS), BF16))

    def fill_slots(g, carry):
        base, table = carry
        lefts, rights = [], []
        for k in range(GROUP):
            c = g * GROUP + k
            start = pl.multiple_of(c * N_XY, N_XY)
            ranks = ranks_ref[pl.ds(start, N_XY), :] + base
            base = base + totals_ref[pl.ds(start, N_XY), :]
            target = targets_ref[c]
            cell = cells_ref[c]
            mine = owner_row == (target >> 12)
            rank = jnp.sum(jnp.where(mine, ranks, 0.0), axis=0, keepdims=True)
            place = target & 4095
            fields = [
                cell >> 7,
                (cell & 127) + 1,
                ((place >> 7) & 1) * 16 + (place >> 8),
                place & 127,
            ]
            lefts.append(
                jnp.concatenate(
                    [jnp.where(mine, field.astype(F32), 0.0) for field in fields], axis=0
                ).astype(BF16)
            )
            rights.append(hits16(row256, rank))
        table = table + dot_nt(jnp.concatenate(lefts, axis=1), jnp.concatenate(rights, axis=1))
        return base, table

    unused, table = lax.fori_loop(
        0,
        CHUNKS // GROUP,
        fill_slots,
        (jnp.zeros((N_XY, SLOTS), F32), jnp.zeros((4 * N_XY, SLOTS), F32)),
    )
    places = table[64:96] * 128.0 + table[96:128]
    for owner in range(N_XY):
        slot_xy[owner] = table[owner : owner + 1]
        slot_z[owner] = table[32 + owner : 33 + owner] - 1.0
        place_send[owner] = places[owner : owner + 1]
    place_recv[me] = place_send[me]
    send_steps(lambda other: place_send.at[other], place_recv, 1, 0, OTHERS)

    def mark_cells(g, unused):
        for k in range(GROUP):
            owner = g * GROUP + k
            xy_hits[owner] = hits16(row256, slot_xy[owner])
        return unused

    lax.fori_loop(0, GROUPS, mark_cells, 0)

    for copy in halos:
        copy.wait_recv()

    def finish_plane(x, unused):
        lane = iota((NY, CZ), 1)
        total = None
        for q in range(19):
            cx, cy, cz = VELOCITIES[q]
            value = rd[q, x + 1]
            if cz != 0:
                k = (Z_PLUS if cz == 1 else Z_MINUS).index(q)
                got = (zr_p if cz == 1 else zr_m)[x - cx + 1]
                edge = 0 if cz == 1 else 127
                border = jnp.concatenate(
                    [roll(got, edge - (k * 4 + block), 1) for block in range(4)], axis=0
                )
                value = jnp.where(lane == edge, border, value)
            read_ref[q, x] = value
            term = WEIGHTS[q] * value
            total = term if total is None else total + term
        dens[pl.ds(pl.multiple_of(x * NY, NY), NY), :] = total
        return unused

    lax.fori_loop(0, CX, finish_plane, 0)

    high, low = split(jnp.transpose(dens[...]))
    dens_t = jnp.concatenate([high, low], axis=0)

    def send_values(g, unused):
        others = [partner(me, g * GROUP + k) for k in range(GROUP)]
        for other in others:
            found = dot(dens_t, xy_hits[other])
            both = found[0:128] + found[128:256]
            value_send[other] = jnp.sum(
                jnp.where(row128 == slot_z[other], both, 0.0), axis=0, keepdims=True
            )
        send_steps(
            lambda other: value_send.at[other],
            value_recv,
            2,
            g * GROUP,
            jnp.minimum(g * GROUP + GROUP, OTHERS),
        )
        return unused

    lax.fori_loop(0, GROUPS, send_values, 0)
    value_recv[me] = value_send[me]

    links = jnp.transpose(links_ref[...].astype(F32)).astype(jnp.int32)
    link_hits = []
    link_half = []
    lane256 = iota((16, 256), 1)
    for side in range(4):
        tile = links[:, side : side + 1]
        link_hits.append(hits(lane256 == (tile >> 4) * 8 + (tile & 7)))
        link_half.append((tile >> 3) & 1)
    link_hits = jnp.concatenate(link_hits, axis=0)
    matrix = neighbour_matrix()
    all_copy(edge_recv0, 0).wait_recv()
    borders = gather_edges(edge_recv0[...].reshape(256, 128), link_hits, link_half)
    all_copy(place_recv, 1).wait_recv()

    def mark_places(g, unused):
        for k in range(GROUP):
            brick = g * GROUP + k
            place = place_recv[brick]
            row = jnp.floor(place * (1.0 / 128.0))
            place_row[brick] = row
            lane_hits[brick] = hits16(row128_16, place - 128.0 * row)
        return unused

    lax.fori_loop(0, GROUPS, mark_places, 0)
    all_copy(value_recv, 2).wait_recv()

    def add_supply(g, total):
        lefts, rights = [], []
        for k in range(GROUP):
            brick = g * GROUP + k
            value = value_recv[brick]
            here = row32 == place_row[brick]
            high = value.astype(BF16).astype(F32)
            lefts.append(
                jnp.concatenate(
                    [jnp.where(here, high, 0.0), jnp.where(here, value - high, 0.0)], axis=0
                ).astype(BF16)
            )
            rights.append(lane_hits[brick])
        return total + dot_nt(jnp.concatenate(lefts, axis=1), jnp.concatenate(rights, axis=1))

    supply = lax.fori_loop(0, GROUPS, add_supply, jnp.zeros((64, 128), F32))
    supply = supply[0:32] + supply[32:64]
    supply = jnp.concatenate([supply[0:16], supply[16:32]], axis=1)
    source = cover + 0.3 * supply * (1.0 - cover) - 0.2 * cover
    first = sweep(cover, source, borders, matrix)
    edges = tile_edges(first, picker)
    edge_send1[...] = edges
    edge_recv1[me] = edges
    send_steps(lambda other: edge_send1, edge_recv1, 3, 0, OTHERS)
    all_copy(edge_recv1, 3).wait_recv()
    borders = gather_edges(edge_recv1[...].reshape(256, 128), link_hits, link_half)
    second = sweep(first, source, borders, matrix)
    cover_out[...] = second
    change = -0.5 * (second - cover)
    change = jnp.concatenate([change[:, 0:128], change[:, 128:256]], axis=0)
    high, low = split(change)
    change = jnp.concatenate([high, low], axis=0)

    def send_changes(g, unused):
        others = [partner(me, g * GROUP + k) for k in range(GROUP)]
        for other in others:
            found = dot(change, lane_hits[other])
            both = found[0:32] + found[32:64]
            change_send[other] = jnp.sum(
                jnp.where(row32 == place_row[other], both, 0.0), axis=0, keepdims=True
            )
        send_steps(
            lambda other: change_send.at[other],
            change_recv,
            4,
            g * GROUP,
            jnp.minimum(g * GROUP + GROUP, OTHERS),
        )
        return unused

    lax.fori_loop(0, GROUPS, send_changes, 0)
    change_recv[me] = change_send[me]
    corr_acc[...] = jnp.zeros_like(corr_acc)
    for copy in halos:
        copy.wait_send()
    all_copy(change_recv, 4).wait_recv()

    def add_change(g, unused):
        lefts, rights = [], []
        for k in range(GROUP):
            owner = g * GROUP + k
            value = change_recv[owner]
            here = row128 == slot_z[owner]
            high = value.astype(BF16).astype(F32)
            rights.append(
                jnp.concatenate(
                    [jnp.where(here, high, 0.0), jnp.where(here, value - high, 0.0)], axis=0
                ).astype(BF16)
            )
            lefts.append(xy_hits[owner])
        corr_acc[...] += dot_nt(jnp.concatenate(lefts, axis=1), jnp.concatenate(rights, axis=1))
        return unused

    lax.fori_loop(0, GROUPS, add_change, 0)
    correction_out[...] = corr_acc[:, 0:128] + corr_acc[:, 128:256]
    for ref, index in (
        (edge_recv0, 0),
        (place_recv, 1),
        (value_recv, 2),
        (edge_recv1, 3),
        (change_recv, 4),
    ):
        all_copy(ref, index).wait_send()


def add_kernel(read_ref, correction_ref, cover_ref, updated_hbm, cover_hbm, stage, sem):
    cover_copy = pltpu.make_async_copy(cover_ref, cover_hbm, sem.at[CX])
    cover_copy.start()
    copies = []
    for x in range(CX):
        stage[:, x] = read_ref[:, x] + correction_ref[x * NY : (x + 1) * NY, :][None]
        copies.append(pltpu.make_async_copy(stage.at[:, x], updated_hbm.at[:, x], sem.at[x]))
        copies[-1].start()
    for copy in copies:
        copy.wait()
    cover_copy.wait()


def shards(populations, solid, knudsen, wall_cells, wall_target, coverage, tile_links):
    hbm = pl.BlockSpec(memory_space=pltpu.HBM)
    vmem = pl.BlockSpec(memory_space=pltpu.VMEM)
    slots = pltpu.VMEM((N_XY, 1, SLOTS), F32)
    edge_table = pltpu.VMEM((N_XY, 8, 128), F32)
    walls = pltpu.VMEM((CHUNKS, 1, SLOTS), jnp.int32)
    whole = jax.ShapeDtypeStruct((19, CX, NY, CZ), F32)
    cover_shape = jax.ShapeDtypeStruct((16, 256), F32)
    read, new_coverage, correction = pl.pallas_call(
        kernel,
        out_shape=(whole, cover_shape, jax.ShapeDtypeStruct((256, 128), F32)),
        in_specs=[hbm] * 7,
        out_specs=(vmem, vmem, vmem),
        scratch_shapes=[
            pltpu.VMEM((19, CX, NY, CZ), F32),
            pltpu.VMEM((CX, NY, CZ), jnp.int32),
            pltpu.VMEM((CX, NY, CZ), F32),
            walls,
            walls,
            pltpu.VMEM((16, 256), F32),
            pltpu.VMEM((4, 16), jnp.int32),
            pltpu.VMEM((19, CX + 2, NY, CZ), F32),
            pltpu.VMEM((CX, 8, 128), F32),
            pltpu.VMEM((CX, 8, 128), F32),
            pltpu.VMEM((CX + 2, 8, 128), F32),
            pltpu.VMEM((CX + 2, 8, 128), F32),
            pltpu.VMEM((CX * NY, CZ), F32),
            pltpu.VMEM((CHUNKS * N_XY, SLOTS), BF16),
            pltpu.VMEM((CHUNKS * N_XY, SLOTS), F32),
            pltpu.VMEM((CHUNKS * N_XY, SLOTS), F32),
            pltpu.VMEM((N_XY, SLOTS, SLOTS), BF16),
            pltpu.VMEM((N_XY, CZ, SLOTS), BF16),
            slots,
            slots,
            slots,
            slots,
            slots,
            slots,
            slots,
            slots,
            slots,
            pltpu.VMEM((8, 128), F32),
            edge_table,
            pltpu.VMEM((8, 128), F32),
            edge_table,
            pltpu.VMEM((256, 256), F32),
            pltpu.SemaphoreType.DMA((14,)),
            pltpu.SemaphoreType.DMA((16,)),
            pltpu.SemaphoreType.DMA((16,)),
            pltpu.SemaphoreType.DMA((5,)),
            pltpu.SemaphoreType.DMA((5,)),
        ],
        compiler_params=pltpu.CompilerParams(
            collective_id=0, has_side_effects=True, vmem_limit_bytes=40 * 1024 * 1024
        ),
    )(
        *[
            pltpu.with_memory_space_constraint(array, pltpu.HBM)
            for array in (
                populations,
                solid,
                knudsen,
                wall_cells.reshape(CHUNKS, 1, SLOTS),
                wall_target.reshape(CHUNKS, 1, SLOTS),
                coverage,
                tile_links.T,
            )
        ]
    )
    updated, new_coverage = pl.pallas_call(
        add_kernel,
        out_shape=(whole, cover_shape),
        in_specs=[vmem, vmem, vmem],
        out_specs=(hbm, hbm),
        scratch_shapes=[
            pltpu.VMEM((19, CX, NY, CZ), F32),
            pltpu.SemaphoreType.DMA((CX + 1,)),
        ],
        compiler_params=pltpu.CompilerParams(vmem_limit_bytes=16 * 1024 * 1024),
    )(read, correction, new_coverage)
    return updated, new_coverage


def solution(mesh):
    in_specs = (
        P(None, "xy", None, "gz"),
        P("xy", None, "gz"),
        P("xy", None, "gz"),
        P("gz", "xy"),
        P("gz", "xy"),
        P(("gz", "xy"), None),
        P(("gz", "xy"), None),
    )
    out_specs = (P(None, "xy", None, "gz"), P(("gz", "xy"), None))
    return jax.shard_map(shards, mesh=mesh, in_specs=in_specs, out_specs=out_specs, check_vma=False)
```

```python
import jax
import jax.numpy as jnp
from jax import lax
from jax.experimental import pallas as pl
from jax.experimental.pallas import tpu as pltpu
from jax.sharding import PartitionSpec as P

MESH = pl.DeviceIdType.MESH
F32 = jnp.float32
BF16 = jnp.bfloat16

VELOCITIES = [
    (0, 0, 0),
    (0, 1, 0),
    (0, -1, 0),
    (1, 0, 0),
    (-1, 0, 0),
    (0, 0, 1),
    (0, 0, -1),
    (1, 1, 0),
    (-1, -1, 0),
    (1, -1, 0),
    (-1, 1, 0),
    (1, 0, 1),
    (-1, 0, -1),
    (1, 0, -1),
    (-1, 0, 1),
    (0, 1, 1),
    (0, -1, -1),
    (0, 1, -1),
    (0, -1, 1),
]
WEIGHTS = [1.0 / 3.0] + [1.0 / 18.0] * 6 + [1.0 / 36.0] * 12
X_PLUS = [q for q in range(19) if VELOCITIES[q][0] == 1]
X_MINUS = [q for q in range(19) if VELOCITIES[q][0] == -1]
Z_PLUS = [q for q in range(19) if VELOCITIES[q][2] == 1]
Z_MINUS = [q for q in range(19) if VELOCITIES[q][2] == -1]

N_GZ = 8
N_XY = 32
CX = 8
NY = 32
CZ = 128
SLOTS = 256
CHUNKS = 16
OTHERS = N_XY - 1
GREETED = OTHERS + 6
GROUP = 8
GROUPS = N_XY // GROUP


def iota(shape, dim):
    return lax.broadcasted_iota(jnp.int32, shape, dim)


def split(values):
    high = values.astype(BF16)
    low = (values - high.astype(F32)).astype(BF16)
    return high, low


def hits(mask):
    return jnp.where(mask, 1.0, 0.0).astype(BF16)


def hits16(rows, row):
    return jnp.where(rows == row.astype(BF16), BF16(1.0), BF16(0.0))


def dot(left, right):
    return lax.dot_general(left, right, (((1,), (0,)), ((), ())), preferred_element_type=F32)


def dot_nt(left, right):
    return lax.dot_general(left, right, (((1,), (1,)), ((), ())), preferred_element_type=F32)


def centred(step, size):
    return size // 2 + ((step + 1) // 2) * (1 - 2 * (step % 2))


def partner(me, step):
    z = (me % 8 + centred(step // 4, 8)) % 8
    x = (me // 8 + centred(step % 4, 4)) % 4
    return x * 8 + z


def roll(values, shift, axis):
    shift = shift % values.shape[axis]
    return values if shift == 0 else pltpu.roll(values, shift, axis)


def edge_picker():
    cell, lane = iota((512, 128), 0), iota((512, 128), 1)
    side, place = (lane >> 4) & 3, lane & 15
    wanted = jnp.where(
        side == 0,
        place * 16 + 15,
        jnp.where(side == 1, place * 16, jnp.where(side == 2, 240 + place, place)),
    )
    return hits(cell == (lane >> 6) * 256 + wanted)


def tile_edges(cover, picker):
    both = jnp.concatenate([cover[0:8], cover[8:16]], axis=1)
    high, low = split(both)
    return dot(high, picker) + dot(low, picker)


def neighbour_matrix():
    a, b = iota((256, 256), 0), iota((256, 256), 1)
    same_row = (a >> 4) == (b >> 4)
    near = (same_row & (jnp.abs(a - b) == 1)) | (jnp.abs(a - b) == 16)
    inner = hits(near)
    s, k = iota((128, 256), 0), iota((128, 256), 1)
    side, place = (s >> 4) & 3, s & 15
    cell = jnp.where(
        side == 0,
        place * 16,
        jnp.where(side == 1, place * 16 + 15, jnp.where(side == 2, place, 240 + place)),
    )
    return jnp.concatenate([inner, inner, hits(k == cell)], axis=0)


def gather_edges(edges, link_hits, link_half):
    high, low = split(edges)
    found = dot(link_hits, jnp.concatenate([high, low], axis=1))
    lane = iota((16, 64), 1)
    out_high = jnp.zeros((16, 64), F32)
    out_low = jnp.zeros((16, 64), F32)
    for side in range(4):
        part = found[side * 16 : (side + 1) * 16]
        second = link_half[side] == 1
        h = jnp.where(second, part[:, 64:128], part[:, 0:64])
        l = jnp.where(second, part[:, 192:256], part[:, 128:192])
        here = (lane >> 4) == side
        out_high = jnp.where(here, h, out_high)
        out_low = jnp.where(here, l, out_low)
    return jnp.concatenate([out_high, out_low], axis=1)


def sweep(cover, source, borders, matrix):
    high, low = split(cover)
    row = jnp.concatenate([high, low, borders.astype(BF16)], axis=1)
    return (source + 2.0 * dot(row, matrix)) * (1.0 / 9.0)


def kernel(
    pop_hbm,
    solid_hbm,
    knudsen_hbm,
    cells_hbm,
    targets_hbm,
    cover_hbm,
    links_hbm,
    read_ref,
    cover_out,
    correction_out,
    pop,
    solid,
    knudsen,
    cells_ref,
    targets_ref,
    cover_ref,
    links_ref,
    rd,
    zs_p,
    zs_m,
    zr_p,
    zr_m,
    dens,
    owner_hits,
    ranks_ref,
    totals_ref,
    xy_hits,
    lane_hits,
    slot_xy,
    slot_z,
    place_row,
    place_send,
    place_recv,
    value_send,
    value_recv,
    change_send,
    change_recv,
    edge_send0,
    edge_recv0,
    edge_send1,
    edge_recv1,
    link_send,
    link_recv,
    link_table,
    cell_hits,
    rank_hits,
    across_hits,
    along_hits,
    across_place,
    along_place,
    border_terms,
    load_sem,
    halo_send,
    halo_recv,
    all_send,
    all_recv,
):
    gz = lax.axis_index("gz")
    me = lax.axis_index("xy")
    gz_up, gz_down = lax.rem(gz + 1, N_GZ), lax.rem(gz + N_GZ - 1, N_GZ)
    up, down = lax.rem(me + 1, N_XY), lax.rem(me + N_XY - 1, N_XY)

    barrier = pltpu.get_barrier_semaphore()

    def greet(i, unused):
        pl.semaphore_signal(
            barrier, inc=1, device_id=(gz, partner(me, i)), device_id_type=MESH
        )
        return unused

    lax.fori_loop(0, OTHERS, greet, 0)
    for device in (
        (gz_up, up),
        (gz_up, down),
        (gz_down, up),
        (gz_down, down),
        (gz_up, me),
        (gz_down, me),
    ):
        pl.semaphore_signal(barrier, inc=1, device_id=device, device_id_type=MESH)

    def load(source, target, index):
        copy = pltpu.make_async_copy(source, target, load_sem.at[index])
        copy.start()
        return copy

    plane_loads = {}
    plane_loads[0] = load(pop_hbm.at[:, 0], pop.at[:, 0], 0)
    cell_loads = [load(solid_hbm, solid, 8), load(knudsen_hbm, knudsen, 9)]
    plane_loads[7] = load(pop_hbm.at[:, 7], pop.at[:, 7], 7)
    for x in range(1, 7):
        plane_loads[x] = load(pop_hbm.at[:, x], pop.at[:, x], x)
    wall_loads = [
        load(cells_hbm, cells_ref, 10),
        load(targets_hbm, targets_ref, 11),
        load(cover_hbm, cover_ref, 12),
        load(links_hbm, links_ref, 13),
    ]

    def send_one(source, target, index, other):
        pltpu.make_async_remote_copy(
            src_ref=source,
            dst_ref=target,
            send_sem=all_send.at[index],
            recv_sem=all_recv.at[index],
            device_id=(gz, other),
            device_id_type=MESH,
        ).start()

    def send_steps(source_of, target_ref, index, first, last):
        def send(i, unused):
            other = partner(me, i)
            send_one(source_of(other), target_ref.at[me], index, other)
            return unused

        lax.fori_loop(first, last, send, 0)

    def all_copy(ref, index):
        part = ref.at[pl.ds(0, OTHERS)]
        return pltpu.make_async_remote_copy(
            src_ref=part,
            dst_ref=part,
            send_sem=all_send.at[index],
            recv_sem=all_recv.at[index],
            device_id=(gz, up),
            device_id_type=MESH,
        )

    lane8 = iota((8, 128), 1)

    def collide_plane(x):
        kn = knudsen[x]
        sol = solid[x] == 1
        axis_sum = jnp.zeros((NY, CZ), F32)
        diag_sum = jnp.zeros((NY, CZ), F32)
        axis_m = [None] * 3
        diag_m = [None] * 3
        for q in range(1, 19, 2):
            p, m = pop[q, x], pop[q + 1, x]
            if q < 7:
                axis_sum = axis_sum + (p + m)
            else:
                diag_sum = diag_sum + (p + m)
            diff = p - m
            for axis in range(3):
                c = VELOCITIES[q][axis]
                sums = axis_m if q < 7 else diag_m
                if c == 0:
                    continue
                if sums[axis] is None:
                    sums[axis] = diff if c == 1 else -diff
                else:
                    sums[axis] = sums[axis] + diff if c == 1 else sums[axis] - diff
        rest = pop[0, x]
        density = (1.0 / 3.0) * rest + (1.0 / 18.0) * axis_sum + (1.0 / 36.0) * diag_sum
        inverse = 1.0 / density
        speed = [
            ((1.0 / 18.0) * axis_m[axis] + (1.0 / 36.0) * diag_m[axis]) * inverse
            for axis in range(3)
        ]
        square = speed[0] * speed[0] + speed[1] * speed[1] + speed[2] * speed[2]
        relax = (1.0 + 2.0 * kn) / (1.0 + kn)
        keep = 1.0 - relax
        gain = relax * density
        base = gain - 1.5 * gain * square
        gain3 = 3.0 * gain
        rd[0, x + 1] = jnp.where(sol, rest, keep * rest + base)
        tile_p = jnp.zeros((8, 128), F32)
        tile_m = jnp.zeros((8, 128), F32)
        for q in range(1, 19, 2):
            p, m = pop[q, x], pop[q + 1, x]
            along = None
            for axis in range(3):
                c = VELOCITIES[q][axis]
                if c == 0:
                    continue
                if along is None:
                    along = speed[axis] if c == 1 else -speed[axis]
                else:
                    along = along + speed[axis] if c == 1 else along - speed[axis]
            odd = gain3 * along
            even = base + 1.5 * odd * along
            new_p = jnp.where(sol, m, keep * p + (even + odd))
            new_m = jnp.where(sol, p, keep * m + (even - odd))
            for member, value in ((q, new_p), (q + 1, new_m)):
                cx, cy, cz = VELOCITIES[member]
                value = roll(value, cy, 0)
                value = roll(value, cz, 1)
                rd[member, x + 1 + cx] = value
                if cz == 1:
                    k = Z_PLUS.index(member)
                    for block in range(4):
                        at = k * 4 + block
                        moved = roll(value[block * 8 : block * 8 + 8], at, 1)
                        tile_p = jnp.where(lane8 == at, moved, tile_p)
                if cz == -1:
                    k = Z_MINUS.index(member)
                    for block in range(4):
                        at = k * 4 + block
                        moved = roll(value[block * 8 : block * 8 + 8], at + 1, 1)
                        tile_m = jnp.where(lane8 == at, moved, tile_m)
        zs_p[x] = tile_p
        zs_m[x] = tile_m

    def edge_step(i, unused):
        collide_plane(i * 7)
        return unused

    def inner_step(i, unused):
        collide_plane(i)
        return unused

    def halo(source, target, index, device):
        return pltpu.make_async_remote_copy(
            src_ref=source,
            dst_ref=target,
            send_sem=halo_send.at[index],
            recv_sem=halo_recv.at[index],
            device_id=device,
            device_id_type=MESH,
        )

    for copy in cell_loads + [plane_loads[0], plane_loads[7]]:
        copy.wait()
    lax.fori_loop(0, 2, edge_step, 0)
    for x in range(1, 7):
        plane_loads[x].wait()
    lax.fori_loop(1, 7, inner_step, 0)
    for copy in wall_loads:
        copy.wait()

    owner_row = iota((N_XY, SLOTS), 0)
    row256 = iota((SLOTS, SLOTS), 0).astype(F32).astype(BF16)
    row128 = iota((CZ, SLOTS), 0).astype(F32)
    row128_16 = row128.astype(BF16)
    row32 = iota((N_XY, SLOTS), 0).astype(F32)

    for c in range(CHUNKS):
        owner_hits[c * N_XY : (c + 1) * N_XY, :] = hits(owner_row == (targets_ref[c] >> 12))
    before = hits(iota((SLOTS, SLOTS), 0) < iota((SLOTS, SLOTS), 1))
    ranks_ref[...] = dot(owner_hits[...], before)
    totals_ref[...] = dot(owner_hits[...], jnp.ones((SLOTS, SLOTS), BF16))

    def fill_slots(g, carry):
        base, table = carry
        lefts, rights = [], []
        for k in range(GROUP):
            c = g * GROUP + k
            start = pl.multiple_of(c * N_XY, N_XY)
            ranks = ranks_ref[pl.ds(start, N_XY), :] + base
            base = base + totals_ref[pl.ds(start, N_XY), :]
            target = targets_ref[c]
            cell = cells_ref[c]
            mine = owner_row == (target >> 12)
            rank = jnp.sum(jnp.where(mine, ranks, 0.0), axis=0, keepdims=True)
            place = target & 4095
            fields = [
                cell >> 7,
                (cell & 127) + 1,
                ((place >> 7) & 1) * 16 + (place >> 8),
                place & 127,
            ]
            lefts.append(
                jnp.concatenate(
                    [jnp.where(mine, field.astype(F32), 0.0) for field in fields], axis=0
                ).astype(BF16)
            )
            rank_hits[c] = hits16(row256, rank)
            cell_hits[c] = hits16(row256, fields[0].astype(F32))
            rights.append(rank_hits[c])
        table = table + dot_nt(jnp.concatenate(lefts, axis=1), jnp.concatenate(rights, axis=1))
        return base, table

    unused, table = lax.fori_loop(
        0,
        CHUNKS // GROUP,
        fill_slots,
        (jnp.zeros((N_XY, SLOTS), F32), jnp.zeros((4 * N_XY, SLOTS), F32)),
    )
    places = table[64:96] * 128.0 + table[96:128]
    for owner in range(N_XY):
        slot_xy[owner] = table[owner : owner + 1]
        slot_z[owner] = table[32 + owner : 33 + owner] - 1.0
        place_send[owner] = places[owner : owner + 1]
    place_recv[me] = place_send[me]

    picker = edge_picker()
    cover = cover_ref[...]
    edges = tile_edges(cover, picker)
    edge_send0[...] = edges
    edge_recv0[me] = edges
    links = links_ref[...]
    codes = (links >> 4) * 8 + (links & 7) + ((links >> 3) & 1) * 256
    link_send[...] = jnp.zeros_like(link_send)
    link_send[:, 0:16] = codes.astype(F32)
    link_recv[me] = link_send[...]
    pl.semaphore_wait(barrier, GREETED)
    halos = []
    halos.append(halo(zs_p.at[7], zr_p.at[0], 12, (gz_up, up)))
    halos.append(halo(zs_p.at[0], zr_p.at[9], 13, (gz_up, down)))
    halos.append(halo(zs_m.at[7], zr_m.at[0], 14, (gz_down, up)))
    halos.append(halo(zs_m.at[0], zr_m.at[9], 15, (gz_down, down)))
    for k in range(5):
        halos.append(halo(rd.at[X_PLUS[k], 9], rd.at[X_PLUS[k], 1], k, (gz, up)))
        halos.append(halo(rd.at[X_MINUS[k], 0], rd.at[X_MINUS[k], 8], 5 + k, (gz, down)))
    halos.append(halo(zs_p, zr_p.at[pl.ds(1, CX)], 10, (gz_up, me)))
    halos.append(halo(zs_m, zr_m.at[pl.ds(1, CX)], 11, (gz_down, me)))
    for copy in halos:
        copy.start()
    send_steps(lambda other: place_send.at[other], place_recv, 1, 0, OTHERS)
    send_steps(lambda other: link_send, link_recv, 5, 0, OTHERS)
    send_steps(lambda other: edge_send0, edge_recv0, 0, 0, OTHERS)

    def mark_cells(g, unused):
        for k in range(GROUP):
            owner = g * GROUP + k
            xy_hits[owner] = hits16(row256, slot_xy[owner])
        return unused

    lax.fori_loop(0, GROUPS, mark_cells, 0)

    for copy in halos:
        copy.wait_recv()

    def finish_plane(x, unused):
        lane = iota((NY, CZ), 1)
        total = None
        for q in range(19):
            cx, cy, cz = VELOCITIES[q]
            value = rd[q, x + 1]
            if cz != 0:
                k = (Z_PLUS if cz == 1 else Z_MINUS).index(q)
                got = (zr_p if cz == 1 else zr_m)[x - cx + 1]
                edge = 0 if cz == 1 else 127
                border = jnp.concatenate(
                    [roll(got, edge - (k * 4 + block), 1) for block in range(4)], axis=0
                )
                value = jnp.where(lane == edge, border, value)
            read_ref[q, x] = value
            term = WEIGHTS[q] * value
            total = term if total is None else total + term
        dens[pl.ds(pl.multiple_of(x * NY, NY), NY), :] = total
        return unused

    lax.fori_loop(0, CX, finish_plane, 0)

    high, low = split(jnp.transpose(dens[...]))
    dens_t = jnp.concatenate([high, low], axis=0)

    def send_values(g, unused):
        others = [partner(me, g * GROUP + k) for k in range(GROUP)]
        for other in others:
            found = dot(dens_t, xy_hits[other])
            both = found[0:128] + found[128:256]
            value_send[other] = jnp.sum(
                jnp.where(row128 == slot_z[other], both, 0.0), axis=0, keepdims=True
            )
        send_steps(
            lambda other: value_send.at[other],
            value_recv,
            2,
            g * GROUP,
            jnp.minimum(g * GROUP + GROUP, OTHERS),
        )
        return unused

    lax.fori_loop(0, GROUPS, send_values, 0)
    value_recv[me] = value_send[me]

    links = jnp.transpose(links_ref[...].astype(F32)).astype(jnp.int32)
    link_hits = []
    link_half = []
    lane256 = iota((16, 256), 1)
    for side in range(4):
        tile = links[:, side : side + 1]
        link_hits.append(hits(lane256 == (tile >> 4) * 8 + (tile & 7)))
        link_half.append((tile >> 3) & 1)
    link_hits = jnp.concatenate(link_hits, axis=0)
    matrix = neighbour_matrix()
    all_copy(edge_recv0, 0).wait_recv()
    borders = gather_edges(edge_recv0[...].reshape(256, 128), link_hits, link_half)
    all_copy(place_recv, 1).wait_recv()

    def mark_places(g, unused):
        for k in range(GROUP):
            brick = g * GROUP + k
            place = place_recv[brick]
            row = jnp.floor(place * (1.0 / 128.0))
            place_row[brick] = row
            lane_hits[brick] = hits16(row128_16, place - 128.0 * row)
        return unused

    lax.fori_loop(0, GROUPS, mark_places, 0)
    all_copy(link_recv, 5).wait_recv()
    for owner in range(N_XY):
        link_table[owner * 4 : owner * 4 + 4, :] = link_recv[owner]
    codes = jnp.transpose(link_table[...])[0:16]
    second_half = jnp.where(codes >= 256.0, 1.0, 0.0)
    codes = jnp.concatenate([codes - 256.0 * second_half, second_half], axis=0).astype(BF16)
    row16 = iota((16, SLOTS), 0)

    def find_border(select, tile, valid, far, place):
        found = dot(codes, hits16(row128_16, select.astype(F32)))
        here = row16 == tile
        row = jnp.sum(jnp.where(here, found[0:16], 0.0), axis=0, keepdims=True)
        half = jnp.sum(jnp.where(here, found[16:32], 0.0), axis=0, keepdims=True)
        return jnp.where(valid, row, -1.0), half * 32.0 + (far * 16 + place).astype(F32)

    def mark_borders(g, unused):
        for k in range(GROUP):
            c = g * GROUP + k
            target = targets_ref[c]
            owner, tile = target >> 12, (target >> 8) & 15
            y, x = (target >> 4) & 15, target & 15
            far_x = jnp.where(x == 15, 1, 0)
            far_y = jnp.where(y == 15, 1, 0)
            row, place = find_border(owner * 4 + far_x, tile, (x == 0) | (x == 15), far_x, y)
            across_hits[c] = hits16(row256, row)
            across_place[c] = place
            row, place = find_border(owner * 4 + 2 + far_y, tile, (y == 0) | (y == 15), far_y, x)
            along_hits[c] = hits16(row256, row)
            along_place[c] = place
        return unused

    lax.fori_loop(0, CHUNKS // GROUP, mark_borders, 0)
    all_copy(value_recv, 2).wait_recv()

    def add_supply(g, total):
        lefts, rights = [], []
        for k in range(GROUP):
            brick = g * GROUP + k
            value = value_recv[brick]
            here = row32 == place_row[brick]
            high = value.astype(BF16).astype(F32)
            lefts.append(
                jnp.concatenate(
                    [jnp.where(here, high, 0.0), jnp.where(here, value - high, 0.0)], axis=0
                ).astype(BF16)
            )
            rights.append(lane_hits[brick])
        return total + dot_nt(jnp.concatenate(lefts, axis=1), jnp.concatenate(rights, axis=1))

    supply = lax.fori_loop(0, GROUPS, add_supply, jnp.zeros((64, 128), F32))
    supply = supply[0:32] + supply[32:64]
    supply = jnp.concatenate([supply[0:16], supply[16:32]], axis=1)
    source = cover + 0.3 * supply * (1.0 - cover) - 0.2 * cover
    first = sweep(cover, source, borders, matrix)
    edges = tile_edges(first, picker)
    edge_send1[...] = edges
    edge_recv1[me] = edges
    send_steps(lambda other: edge_send1, edge_recv1, 3, 0, OTHERS)
    high, low = split(first)
    second = dot(jnp.concatenate([high, low], axis=1), matrix[0:512])
    second = (source + 2.0 * second) * (1.0 / 9.0)
    change = -0.5 * (second - cover)
    change = jnp.concatenate([change[:, 0:128], change[:, 128:256]], axis=0)
    high, low = split(change)
    change = jnp.concatenate([high, low], axis=0)

    def send_changes(g, unused):
        others = [partner(me, g * GROUP + k) for k in range(GROUP)]
        for other in others:
            found = dot(change, lane_hits[other])
            both = found[0:32] + found[32:64]
            change_send[other] = jnp.sum(
                jnp.where(row32 == place_row[other], both, 0.0), axis=0, keepdims=True
            )
        send_steps(
            lambda other: change_send.at[other],
            change_recv,
            4,
            g * GROUP,
            jnp.minimum(g * GROUP + GROUP, OTHERS),
        )
        return unused

    lax.fori_loop(0, GROUPS, send_changes, 0)
    change_recv[me] = change_send[me]
    for copy in halos:
        copy.wait_send()
    all_copy(edge_recv1, 3).wait_recv()
    table = edge_recv1[...].reshape(256, 128)
    borders = gather_edges(table, link_hits, link_half)
    cover_out[...] = second + dot(borders.astype(BF16), matrix[512:640]) * (2.0 / 9.0)
    table = jnp.transpose(table)
    high, low = split(jnp.concatenate([table[0:32], table[64:96]], axis=0))
    across = jnp.concatenate([high, low], axis=0)
    high, low = split(jnp.concatenate([table[32:64], table[96:128]], axis=0))
    along = jnp.concatenate([high, low], axis=0)
    row64 = iota((64, SLOTS), 0).astype(F32)

    def add_borders(g, unused):
        for k in range(GROUP):
            c = g * GROUP + k
            found = dot(across, across_hits[c])
            total = jnp.where(row64 == across_place[c], found[0:64] + found[64:128], 0.0)
            found = dot(along, along_hits[c])
            total = total + jnp.where(
                row64 == along_place[c], found[0:64] + found[64:128], 0.0
            )
            border_terms[c] = jnp.sum(total, axis=0, keepdims=True) * (-1.0 / 9.0)
        return unused

    lax.fori_loop(0, CHUNKS // GROUP, add_borders, 0)
    all_copy(change_recv, 4).wait_recv()
    got = jnp.concatenate([change_recv[owner] for owner in range(N_XY)], axis=0)
    high, low = split(got)
    got = jnp.concatenate([high, low], axis=0)

    def add_change(g, total):
        lefts, rights = [], []
        for k in range(GROUP):
            c = g * GROUP + k
            found = dot(got, rank_hits[c])
            mine = owner_row == (targets_ref[c] >> 12)
            value = jnp.sum(
                jnp.where(mine, found[0:32] + found[32:64], 0.0), axis=0, keepdims=True
            )
            value = value + border_terms[c]
            here = row128 == (cells_ref[c] & 127).astype(F32)
            high = value.astype(BF16).astype(F32)
            rights.append(
                jnp.concatenate(
                    [jnp.where(here, high, 0.0), jnp.where(here, value - high, 0.0)], axis=0
                ).astype(BF16)
            )
            lefts.append(cell_hits[c])
        return total + dot_nt(jnp.concatenate(lefts, axis=1), jnp.concatenate(rights, axis=1))

    correction = lax.fori_loop(0, CHUNKS // GROUP, add_change, jnp.zeros((256, 256), F32))
    correction_out[...] = correction[:, 0:128] + correction[:, 128:256]
    for ref, index in (
        (edge_recv0, 0),
        (place_recv, 1),
        (value_recv, 2),
        (edge_recv1, 3),
        (change_recv, 4),
        (link_recv, 5),
    ):
        all_copy(ref, index).wait_send()


def add_kernel(read_ref, correction_ref, cover_ref, updated_hbm, cover_hbm, stage, sem):
    cover_copy = pltpu.make_async_copy(cover_ref, cover_hbm, sem.at[CX])
    cover_copy.start()
    copies = []
    for x in range(CX):
        stage[:, x] = read_ref[:, x] + correction_ref[x * NY : (x + 1) * NY, :][None]
        copies.append(pltpu.make_async_copy(stage.at[:, x], updated_hbm.at[:, x], sem.at[x]))
        copies[-1].start()
    for copy in copies:
        copy.wait()
    cover_copy.wait()


def shards(populations, solid, knudsen, wall_cells, wall_target, coverage, tile_links):
    hbm = pl.BlockSpec(memory_space=pltpu.HBM)
    vmem = pl.BlockSpec(memory_space=pltpu.VMEM)
    slots = pltpu.VMEM((N_XY, 1, SLOTS), F32)
    edge_table = pltpu.VMEM((N_XY, 8, 128), F32)
    by_chunk = pltpu.VMEM((CHUNKS, SLOTS, SLOTS), BF16)
    chunk_rows = pltpu.VMEM((CHUNKS, 1, SLOTS), F32)
    walls = pltpu.VMEM((CHUNKS, 1, SLOTS), jnp.int32)
    whole = jax.ShapeDtypeStruct((19, CX, NY, CZ), F32)
    cover_shape = jax.ShapeDtypeStruct((16, 256), F32)
    read, new_coverage, correction = pl.pallas_call(
        kernel,
        out_shape=(whole, cover_shape, jax.ShapeDtypeStruct((256, 128), F32)),
        in_specs=[hbm] * 7,
        out_specs=(vmem, vmem, vmem),
        scratch_shapes=[
            pltpu.VMEM((19, CX, NY, CZ), F32),
            pltpu.VMEM((CX, NY, CZ), jnp.int32),
            pltpu.VMEM((CX, NY, CZ), F32),
            walls,
            walls,
            pltpu.VMEM((16, 256), F32),
            pltpu.VMEM((4, 16), jnp.int32),
            pltpu.VMEM((19, CX + 2, NY, CZ), F32),
            pltpu.VMEM((CX, 8, 128), F32),
            pltpu.VMEM((CX, 8, 128), F32),
            pltpu.VMEM((CX + 2, 8, 128), F32),
            pltpu.VMEM((CX + 2, 8, 128), F32),
            pltpu.VMEM((CX * NY, CZ), F32),
            pltpu.VMEM((CHUNKS * N_XY, SLOTS), BF16),
            pltpu.VMEM((CHUNKS * N_XY, SLOTS), F32),
            pltpu.VMEM((CHUNKS * N_XY, SLOTS), F32),
            pltpu.VMEM((N_XY, SLOTS, SLOTS), BF16),
            pltpu.VMEM((N_XY, CZ, SLOTS), BF16),
            slots,
            slots,
            slots,
            slots,
            slots,
            slots,
            slots,
            slots,
            slots,
            pltpu.VMEM((8, 128), F32),
            edge_table,
            pltpu.VMEM((8, 128), F32),
            edge_table,
            pltpu.VMEM((4, 128), F32),
            pltpu.VMEM((N_XY, 4, 128), F32),
            pltpu.VMEM((4 * N_XY, 128), F32),
            by_chunk,
            by_chunk,
            by_chunk,
            by_chunk,
            chunk_rows,
            chunk_rows,
            chunk_rows,
            pltpu.SemaphoreType.DMA((14,)),
            pltpu.SemaphoreType.DMA((16,)),
            pltpu.SemaphoreType.DMA((16,)),
            pltpu.SemaphoreType.DMA((6,)),
            pltpu.SemaphoreType.DMA((6,)),
        ],
        compiler_params=pltpu.CompilerParams(
            collective_id=0, has_side_effects=True, vmem_limit_bytes=40 * 1024 * 1024
        ),
    )(
        *[
            pltpu.with_memory_space_constraint(array, pltpu.HBM)
            for array in (
                populations,
                solid,
                knudsen,
                wall_cells.reshape(CHUNKS, 1, SLOTS),
                wall_target.reshape(CHUNKS, 1, SLOTS),
                coverage,
                tile_links.T,
            )
        ]
    )
    updated, new_coverage = pl.pallas_call(
        add_kernel,
        out_shape=(whole, cover_shape),
        in_specs=[vmem, vmem, vmem],
        out_specs=(hbm, hbm),
        scratch_shapes=[
            pltpu.VMEM((19, CX, NY, CZ), F32),
            pltpu.SemaphoreType.DMA((CX + 1,)),
        ],
        compiler_params=pltpu.CompilerParams(vmem_limit_bytes=16 * 1024 * 1024),
    )(read, correction, new_coverage)
    return updated, new_coverage


def solution(mesh):
    in_specs = (
        P(None, "xy", None, "gz"),
        P("xy", None, "gz"),
        P("xy", None, "gz"),
        P("gz", "xy"),
        P("gz", "xy"),
        P(("gz", "xy"), None),
        P(("gz", "xy"), None),
    )
    out_specs = (P(None, "xy", None, "gz"), P(("gz", "xy"), None))
    return jax.shard_map(shards, mesh=mesh, in_specs=in_specs, out_specs=out_specs, check_vma=False)
```

```python
import jax
import jax.numpy as jnp
from jax import lax
from jax.experimental import pallas as pl
from jax.experimental.pallas import tpu as pltpu
from jax.sharding import PartitionSpec as P

MESH = pl.DeviceIdType.MESH
F32 = jnp.float32
BF16 = jnp.bfloat16

VELOCITIES = [
    (0, 0, 0),
    (0, 1, 0),
    (0, -1, 0),
    (1, 0, 0),
    (-1, 0, 0),
    (0, 0, 1),
    (0, 0, -1),
    (1, 1, 0),
    (-1, -1, 0),
    (1, -1, 0),
    (-1, 1, 0),
    (1, 0, 1),
    (-1, 0, -1),
    (1, 0, -1),
    (-1, 0, 1),
    (0, 1, 1),
    (0, -1, -1),
    (0, 1, -1),
    (0, -1, 1),
]
WEIGHTS = [1.0 / 3.0] + [1.0 / 18.0] * 6 + [1.0 / 36.0] * 12
X_PLUS = [q for q in range(19) if VELOCITIES[q][0] == 1]
X_MINUS = [q for q in range(19) if VELOCITIES[q][0] == -1]
Z_PLUS = [q for q in range(19) if VELOCITIES[q][2] == 1]
Z_MINUS = [q for q in range(19) if VELOCITIES[q][2] == -1]

N_GZ = 8
N_XY = 32
CX = 8
NY = 32
CZ = 128
SLOTS = 256
CHUNKS = 16
OTHERS = N_XY - 1
NEAR = 19
GREETED = NEAR + 6
GROUP = 8
GROUPS = N_XY // GROUP


def iota(shape, dim):
    return lax.broadcasted_iota(jnp.int32, shape, dim)


def split(values):
    high = values.astype(BF16)
    low = (values - high.astype(F32)).astype(BF16)
    return high, low


def hits(mask):
    return jnp.where(mask, 1.0, 0.0).astype(BF16)


def hits16(rows, row):
    return jnp.where(rows == row.astype(BF16), BF16(1.0), BF16(0.0))


def dot(left, right):
    return lax.dot_general(left, right, (((1,), (0,)), ((), ())), preferred_element_type=F32)


def dot_nt(left, right):
    return lax.dot_general(left, right, (((1,), (1,)), ((), ())), preferred_element_type=F32)


def centred(step, size):
    return size // 2 + ((step + 1) // 2) * (1 - 2 * (step % 2))


def partner(me, step):
    z = (me % 8 + centred(step // 4, 8)) % 8
    x = (me // 8 + centred(step % 4, 4)) % 4
    return x * 8 + z


def roll(values, shift, axis):
    shift = shift % values.shape[axis]
    return values if shift == 0 else pltpu.roll(values, shift, axis)


def edge_picker():
    cell, lane = iota((512, 128), 0), iota((512, 128), 1)
    side, place = (lane >> 4) & 3, lane & 15
    wanted = jnp.where(
        side == 0,
        place * 16 + 15,
        jnp.where(side == 1, place * 16, jnp.where(side == 2, 240 + place, place)),
    )
    return hits(cell == (lane >> 6) * 256 + wanted)


def tile_edges(cover, picker):
    both = jnp.concatenate([cover[0:8], cover[8:16]], axis=1)
    high, low = split(both)
    return dot(high, picker) + dot(low, picker)


def neighbour_matrix():
    a, b = iota((256, 256), 0), iota((256, 256), 1)
    same_row = (a >> 4) == (b >> 4)
    near = (same_row & (jnp.abs(a - b) == 1)) | (jnp.abs(a - b) == 16)
    inner = hits(near)
    s, k = iota((128, 256), 0), iota((128, 256), 1)
    side, place = (s >> 4) & 3, s & 15
    cell = jnp.where(
        side == 0,
        place * 16,
        jnp.where(side == 1, place * 16 + 15, jnp.where(side == 2, place, 240 + place)),
    )
    return jnp.concatenate([inner, inner, hits(k == cell)], axis=0)


def gather_edges(edges, link_hits, link_half):
    high, low = split(edges)
    found = dot(link_hits, jnp.concatenate([high, low], axis=1))
    lane = iota((16, 64), 1)
    out_high = jnp.zeros((16, 64), F32)
    out_low = jnp.zeros((16, 64), F32)
    for side in range(4):
        part = found[side * 16 : (side + 1) * 16]
        second = link_half[side] == 1
        h = jnp.where(second, part[:, 64:128], part[:, 0:64])
        l = jnp.where(second, part[:, 192:256], part[:, 128:192])
        here = (lane >> 4) == side
        out_high = jnp.where(here, h, out_high)
        out_low = jnp.where(here, l, out_low)
    return jnp.concatenate([out_high, out_low], axis=1)


def sweep(cover, source, borders, matrix):
    high, low = split(cover)
    row = jnp.concatenate([high, low, borders.astype(BF16)], axis=1)
    return (source + 2.0 * dot(row, matrix)) * (1.0 / 9.0)


def kernel(
    pop_hbm,
    solid_hbm,
    knudsen_hbm,
    cells_hbm,
    targets_hbm,
    cover_hbm,
    links_hbm,
    read_ref,
    cover_out,
    correction_out,
    pop,
    solid,
    knudsen,
    cells_ref,
    targets_ref,
    cover_ref,
    links_ref,
    rd,
    zs_p,
    zs_m,
    zr_p,
    zr_m,
    dens,
    owner_hits,
    ranks_ref,
    totals_ref,
    xy_hits,
    lane_hits,
    slot_xy,
    slot_z,
    place_row,
    place_send,
    place_recv,
    value_send,
    value_recv,
    change_send,
    change_recv,
    edge_send0,
    edge_recv0,
    edge_send1,
    edge_recv1,
    link_send,
    link_recv,
    link_table,
    cell_hits,
    rank_hits,
    across_hits,
    along_hits,
    across_place,
    along_place,
    border_terms,
    load_sem,
    halo_send,
    halo_recv,
    ready_sem,
    all_send,
    all_recv,
):
    gz = lax.axis_index("gz")
    me = lax.axis_index("xy")
    gz_up, gz_down = lax.rem(gz + 1, N_GZ), lax.rem(gz + N_GZ - 1, N_GZ)
    up, down = lax.rem(me + 1, N_XY), lax.rem(me + N_XY - 1, N_XY)

    def load(source, target, index):
        copy = pltpu.make_async_copy(source, target, load_sem.at[index])
        copy.start()
        return copy

    plane_loads = {}
    plane_loads[0] = load(pop_hbm.at[:, 0], pop.at[:, 0], 0)
    cell_loads = [load(solid_hbm, solid, 8), load(knudsen_hbm, knudsen, 9)]
    plane_loads[7] = load(pop_hbm.at[:, 7], pop.at[:, 7], 7)
    for x in range(1, 7):
        plane_loads[x] = load(pop_hbm.at[:, x], pop.at[:, x], x)
    wall_loads = [
        load(cells_hbm, cells_ref, 10),
        load(targets_hbm, targets_ref, 11),
        load(cover_hbm, cover_ref, 12),
        load(links_hbm, links_ref, 13),
    ]

    barrier = pltpu.get_barrier_semaphore()

    def near(i):
        step = jnp.where(i >= 8, i + 1, i)
        z = (me % 8 + step // 4 + 6) % 8
        x = (me // 8 + step % 4) % 4
        return x * 8 + z

    def greet_near(semaphore):
        def greet(i, unused):
            pl.semaphore_signal(
                semaphore, inc=1, device_id=(gz, near(i)), device_id_type=MESH
            )
            return unused

        lax.fori_loop(0, NEAR, greet, 0)

    for device in (
        (gz_up, up),
        (gz_up, down),
        (gz_down, up),
        (gz_down, down),
        (gz_up, me),
        (gz_down, me),
    ):
        pl.semaphore_signal(barrier, inc=1, device_id=device, device_id_type=MESH)
    greet_near(barrier)

    def send_one(source, target, index, other):
        pltpu.make_async_remote_copy(
            src_ref=source,
            dst_ref=target,
            send_sem=all_send.at[index],
            recv_sem=all_recv.at[index],
            device_id=(gz, other),
            device_id_type=MESH,
        ).start()

    def send_steps(source_of, target_ref, index, first, last):
        def send(i, unused):
            other = partner(me, i)
            send_one(source_of(other), target_ref.at[me], index, other)
            return unused

        lax.fori_loop(first, last, send, 0)

    def all_copy(ref, index):
        part = ref.at[pl.ds(0, OTHERS)]
        return pltpu.make_async_remote_copy(
            src_ref=part,
            dst_ref=part,
            send_sem=all_send.at[index],
            recv_sem=all_recv.at[index],
            device_id=(gz, up),
            device_id_type=MESH,
        )

    lane8 = iota((8, 128), 1)

    def collide_plane(x):
        kn = knudsen[x]
        sol = solid[x] == 1
        axis_sum = jnp.zeros((NY, CZ), F32)
        diag_sum = jnp.zeros((NY, CZ), F32)
        axis_m = [None] * 3
        diag_m = [None] * 3
        for q in range(1, 19, 2):
            p, m = pop[q, x], pop[q + 1, x]
            if q < 7:
                axis_sum = axis_sum + (p + m)
            else:
                diag_sum = diag_sum + (p + m)
            diff = p - m
            for axis in range(3):
                c = VELOCITIES[q][axis]
                sums = axis_m if q < 7 else diag_m
                if c == 0:
                    continue
                if sums[axis] is None:
                    sums[axis] = diff if c == 1 else -diff
                else:
                    sums[axis] = sums[axis] + diff if c == 1 else sums[axis] - diff
        rest = pop[0, x]
        density = (1.0 / 3.0) * rest + (1.0 / 18.0) * axis_sum + (1.0 / 36.0) * diag_sum
        inverse = 1.0 / density
        speed = [
            ((1.0 / 18.0) * axis_m[axis] + (1.0 / 36.0) * diag_m[axis]) * inverse
            for axis in range(3)
        ]
        square = speed[0] * speed[0] + speed[1] * speed[1] + speed[2] * speed[2]
        relax = (1.0 + 2.0 * kn) / (1.0 + kn)
        keep = 1.0 - relax
        gain = relax * density
        base = gain - 1.5 * gain * square
        gain3 = 3.0 * gain
        rd[0, x + 1] = jnp.where(sol, rest, keep * rest + base)
        tile_p = jnp.zeros((8, 128), F32)
        tile_m = jnp.zeros((8, 128), F32)
        for q in range(1, 19, 2):
            p, m = pop[q, x], pop[q + 1, x]
            along = None
            for axis in range(3):
                c = VELOCITIES[q][axis]
                if c == 0:
                    continue
                if along is None:
                    along = speed[axis] if c == 1 else -speed[axis]
                else:
                    along = along + speed[axis] if c == 1 else along - speed[axis]
            odd = gain3 * along
            even = base + 1.5 * odd * along
            new_p = jnp.where(sol, m, keep * p + (even + odd))
            new_m = jnp.where(sol, p, keep * m + (even - odd))
            for member, value in ((q, new_p), (q + 1, new_m)):
                cx, cy, cz = VELOCITIES[member]
                value = roll(value, cy, 0)
                value = roll(value, cz, 1)
                rd[member, x + 1 + cx] = value
                if cz == 1:
                    k = Z_PLUS.index(member)
                    for block in range(4):
                        at = k * 4 + block
                        moved = roll(value[block * 8 : block * 8 + 8], at, 1)
                        tile_p = jnp.where(lane8 == at, moved, tile_p)
                if cz == -1:
                    k = Z_MINUS.index(member)
                    for block in range(4):
                        at = k * 4 + block
                        moved = roll(value[block * 8 : block * 8 + 8], at + 1, 1)
                        tile_m = jnp.where(lane8 == at, moved, tile_m)
        zs_p[x] = tile_p
        zs_m[x] = tile_m

    def edge_step(i, unused):
        collide_plane(i * 7)
        return unused

    def inner_step(i, unused):
        collide_plane(i)
        return unused

    def halo(source, target, index, device):
        return pltpu.make_async_remote_copy(
            src_ref=source,
            dst_ref=target,
            send_sem=halo_send.at[index],
            recv_sem=halo_recv.at[index],
            device_id=device,
            device_id_type=MESH,
        )

    for copy in cell_loads + [plane_loads[0], plane_loads[7]]:
        copy.wait()
    lax.fori_loop(0, 2, edge_step, 0)
    pl.semaphore_wait(barrier, GREETED)
    halos = []
    halos.append(halo(zs_p.at[7], zr_p.at[0], 12, (gz_up, up)))
    halos.append(halo(zs_p.at[0], zr_p.at[9], 13, (gz_up, down)))
    halos.append(halo(zs_m.at[7], zr_m.at[0], 14, (gz_down, up)))
    halos.append(halo(zs_m.at[0], zr_m.at[9], 15, (gz_down, down)))
    for k in range(5):
        halos.append(halo(rd.at[X_PLUS[k], 9], rd.at[X_PLUS[k], 1], k, (gz, up)))
        halos.append(halo(rd.at[X_MINUS[k], 0], rd.at[X_MINUS[k], 8], 5 + k, (gz, down)))
    for copy in halos:
        copy.start()
    greet_near(ready_sem)
    for x in range(1, 7):
        plane_loads[x].wait()
    lax.fori_loop(1, 7, inner_step, 0)
    faces = [
        halo(zs_p, zr_p.at[pl.ds(1, CX)], 10, (gz_up, me)),
        halo(zs_m, zr_m.at[pl.ds(1, CX)], 11, (gz_down, me)),
    ]
    for copy in faces:
        copy.start()
    halos = halos + faces
    for copy in wall_loads:
        copy.wait()

    owner_row = iota((N_XY, SLOTS), 0)
    row256 = iota((SLOTS, SLOTS), 0).astype(F32).astype(BF16)
    row128 = iota((CZ, SLOTS), 0).astype(F32)
    row128_16 = row128.astype(BF16)
    row32 = iota((N_XY, SLOTS), 0).astype(F32)

    for c in range(CHUNKS):
        owner_hits[c * N_XY : (c + 1) * N_XY, :] = hits(owner_row == (targets_ref[c] >> 12))
    before = hits(iota((SLOTS, SLOTS), 0) < iota((SLOTS, SLOTS), 1))
    ranks_ref[...] = dot(owner_hits[...], before)
    totals_ref[...] = dot(owner_hits[...], jnp.ones((SLOTS, SLOTS), BF16))

    def fill_slots(g, carry):
        base, table = carry
        lefts, rights = [], []
        for k in range(GROUP):
            c = g * GROUP + k
            start = pl.multiple_of(c * N_XY, N_XY)
            ranks = ranks_ref[pl.ds(start, N_XY), :] + base
            base = base + totals_ref[pl.ds(start, N_XY), :]
            target = targets_ref[c]
            cell = cells_ref[c]
            mine = owner_row == (target >> 12)
            rank = jnp.sum(jnp.where(mine, ranks, 0.0), axis=0, keepdims=True)
            place = target & 4095
            fields = [
                cell >> 7,
                (cell & 127) + 1,
                ((place >> 7) & 1) * 16 + (place >> 8),
                place & 127,
            ]
            lefts.append(
                jnp.concatenate(
                    [jnp.where(mine, field.astype(F32), 0.0) for field in fields], axis=0
                ).astype(BF16)
            )
            rank_hits[c] = hits16(row256, rank)
            cell_hits[c] = hits16(row256, fields[0].astype(F32))
            rights.append(rank_hits[c])
        table = table + dot_nt(jnp.concatenate(lefts, axis=1), jnp.concatenate(rights, axis=1))
        return base, table

    unused, table = lax.fori_loop(
        0,
        CHUNKS // GROUP,
        fill_slots,
        (jnp.zeros((N_XY, SLOTS), F32), jnp.zeros((4 * N_XY, SLOTS), F32)),
    )
    places = table[64:96] * 128.0 + table[96:128]
    for owner in range(N_XY):
        slot_xy[owner] = table[owner : owner + 1]
        slot_z[owner] = table[32 + owner : 33 + owner] - 1.0
        place_send[owner] = places[owner : owner + 1]
    place_recv[me] = place_send[me]

    picker = edge_picker()
    cover = cover_ref[...]
    edges = tile_edges(cover, picker)
    edge_send0[...] = edges
    edge_recv0[me] = edges
    links = links_ref[...]
    codes = (links >> 4) * 8 + (links & 7) + ((links >> 3) & 1) * 256
    link_send[...] = jnp.zeros_like(link_send)
    link_send[:, 0:16] = codes.astype(F32)
    link_recv[me] = link_send[...]

    def mark_cells(g, unused):
        for k in range(GROUP):
            owner = g * GROUP + k
            xy_hits[owner] = hits16(row256, slot_xy[owner])
        return unused

    lax.fori_loop(0, GROUPS, mark_cells, 0)

    def border(q, x):
        cx, cy, cz = VELOCITIES[q]
        k = (Z_PLUS if cz == 1 else Z_MINUS).index(q)
        got = (zr_p if cz == 1 else zr_m)[x - cx + 1]
        edge = 0 if cz == 1 else 127
        return jnp.concatenate(
            [roll(got, edge - (k * 4 + block), 1) for block in range(4)], axis=0
        )

    def inner_plane(x, unused):
        total = None
        for q in range(19):
            value = rd[q, x + 1]
            read_ref[q, x] = value
            term = WEIGHTS[q] * value
            total = term if total is None else total + term
        dens[pl.ds(pl.multiple_of(x * NY, NY), NY), :] = total
        return unused

    lax.fori_loop(1, CX - 1, inner_plane, 0)
    pl.semaphore_wait(ready_sem, NEAR)
    send_steps(lambda other: place_send.at[other], place_recv, 1, 0, OTHERS)
    send_steps(lambda other: edge_send0, edge_recv0, 0, 0, OTHERS)

    for copy in halos:
        copy.wait_recv()

    def finish_plane(i, unused):
        x = i * 7
        lane = iota((NY, CZ), 1)
        total = None
        for q in range(19):
            cx, cy, cz = VELOCITIES[q]
            value = rd[q, x + 1]
            if cz != 0:
                value = jnp.where(lane == (0 if cz == 1 else 127), border(q, x), value)
            read_ref[q, x] = value
            term = WEIGHTS[q] * value
            total = term if total is None else total + term
        dens[pl.ds(pl.multiple_of(x * NY, NY), NY), :] = total
        return unused

    def mend_plane(x, unused):
        lane = iota((NY, CZ), 1)
        rows = pl.ds(pl.multiple_of(x * NY, NY), NY)
        total = dens[rows, :]
        for members, edge in ((Z_PLUS, 0), (Z_MINUS, 127)):
            for q in members:
                old = read_ref[q, x]
                new = jnp.where(lane == edge, border(q, x), old)
                read_ref[q, x] = new
                total = total + WEIGHTS[q] * (new - old)
        dens[rows, :] = total
        return unused

    lax.fori_loop(1, CX - 1, mend_plane, 0)
    lax.fori_loop(0, 2, finish_plane, 0)

    high, low = split(jnp.transpose(dens[...]))
    dens_t = jnp.concatenate([high, low], axis=0)

    def send_values(g, unused):
        others = [partner(me, g * GROUP + k) for k in range(GROUP)]
        for other in others:
            found = dot(dens_t, xy_hits[other])
            both = found[0:128] + found[128:256]
            value_send[other] = jnp.sum(
                jnp.where(row128 == slot_z[other], both, 0.0), axis=0, keepdims=True
            )
        send_steps(
            lambda other: value_send.at[other],
            value_recv,
            2,
            g * GROUP,
            jnp.minimum(g * GROUP + GROUP, OTHERS),
        )
        return unused

    lax.fori_loop(0, GROUPS, send_values, 0)
    value_recv[me] = value_send[me]
    send_steps(lambda other: link_send, link_recv, 5, 0, OTHERS)

    links = jnp.transpose(links_ref[...].astype(F32)).astype(jnp.int32)
    link_hits = []
    link_half = []
    lane256 = iota((16, 256), 1)
    for side in range(4):
        tile = links[:, side : side + 1]
        link_hits.append(hits(lane256 == (tile >> 4) * 8 + (tile & 7)))
        link_half.append((tile >> 3) & 1)
    link_hits = jnp.concatenate(link_hits, axis=0)
    matrix = neighbour_matrix()
    all_copy(edge_recv0, 0).wait_recv()
    borders = gather_edges(edge_recv0[...].reshape(256, 128), link_hits, link_half)
    all_copy(place_recv, 1).wait_recv()

    def mark_places(g, unused):
        for k in range(GROUP):
            brick = g * GROUP + k
            place = place_recv[brick]
            row = jnp.floor(place * (1.0 / 128.0))
            place_row[brick] = row
            lane_hits[brick] = hits16(row128_16, place - 128.0 * row)
        return unused

    lax.fori_loop(0, GROUPS, mark_places, 0)
    all_copy(value_recv, 2).wait_recv()

    def add_supply(g, total):
        lefts, rights = [], []
        for k in range(GROUP):
            brick = g * GROUP + k
            value = value_recv[brick]
            here = row32 == place_row[brick]
            high = value.astype(BF16).astype(F32)
            lefts.append(
                jnp.concatenate(
                    [jnp.where(here, high, 0.0), jnp.where(here, value - high, 0.0)], axis=0
                ).astype(BF16)
            )
            rights.append(lane_hits[brick])
        return total + dot_nt(jnp.concatenate(lefts, axis=1), jnp.concatenate(rights, axis=1))

    supply = lax.fori_loop(0, GROUPS, add_supply, jnp.zeros((64, 128), F32))
    supply = supply[0:32] + supply[32:64]
    supply = jnp.concatenate([supply[0:16], supply[16:32]], axis=1)
    source = cover + 0.3 * supply * (1.0 - cover) - 0.2 * cover
    first = sweep(cover, source, borders, matrix)
    edges = tile_edges(first, picker)
    edge_send1[...] = edges
    edge_recv1[me] = edges
    send_steps(lambda other: edge_send1, edge_recv1, 3, 0, OTHERS)
    high, low = split(first)
    second = dot(jnp.concatenate([high, low], axis=1), matrix[0:512])
    second = (source + 2.0 * second) * (1.0 / 9.0)
    change = -0.5 * (second - cover)
    change = jnp.concatenate([change[:, 0:128], change[:, 128:256]], axis=0)
    high, low = split(change)
    change = jnp.concatenate([high, low], axis=0)

    def send_changes(g, unused):
        others = [partner(me, g * GROUP + k) for k in range(GROUP)]
        for other in others:
            found = dot(change, lane_hits[other])
            both = found[0:32] + found[32:64]
            change_send[other] = jnp.sum(
                jnp.where(row32 == place_row[other], both, 0.0), axis=0, keepdims=True
            )
        send_steps(
            lambda other: change_send.at[other],
            change_recv,
            4,
            g * GROUP,
            jnp.minimum(g * GROUP + GROUP, OTHERS),
        )
        return unused

    lax.fori_loop(0, GROUPS, send_changes, 0)
    change_recv[me] = change_send[me]
    for copy in halos:
        copy.wait_send()
    all_copy(link_recv, 5).wait_recv()
    for owner in range(N_XY):
        link_table[owner * 4 : owner * 4 + 4, :] = link_recv[owner]
    codes = jnp.transpose(link_table[...])[0:16]
    second_half = jnp.where(codes >= 256.0, 1.0, 0.0)
    codes = jnp.concatenate([codes - 256.0 * second_half, second_half], axis=0).astype(BF16)
    row16 = iota((16, SLOTS), 0)

    def find_border(select, tile, valid, far, place):
        found = dot(codes, hits16(row128_16, select.astype(F32)))
        here = row16 == tile
        row = jnp.sum(jnp.where(here, found[0:16], 0.0), axis=0, keepdims=True)
        half = jnp.sum(jnp.where(here, found[16:32], 0.0), axis=0, keepdims=True)
        return jnp.where(valid, row, -1.0), half * 32.0 + (far * 16 + place).astype(F32)

    def mark_borders(g, unused):
        for k in range(GROUP):
            c = g * GROUP + k
            target = targets_ref[c]
            owner, tile = target >> 12, (target >> 8) & 15
            y, x = (target >> 4) & 15, target & 15
            far_x = jnp.where(x == 15, 1, 0)
            far_y = jnp.where(y == 15, 1, 0)
            row, place = find_border(owner * 4 + far_x, tile, (x == 0) | (x == 15), far_x, y)
            across_hits[c] = hits16(row256, row)
            across_place[c] = place
            row, place = find_border(owner * 4 + 2 + far_y, tile, (y == 0) | (y == 15), far_y, x)
            along_hits[c] = hits16(row256, row)
            along_place[c] = place
        return unused

    lax.fori_loop(0, CHUNKS // GROUP, mark_borders, 0)
    all_copy(edge_recv1, 3).wait_recv()
    table = edge_recv1[...].reshape(256, 128)
    borders = gather_edges(table, link_hits, link_half)
    cover_out[...] = second + dot(borders.astype(BF16), matrix[512:640]) * (2.0 / 9.0)
    table = jnp.transpose(table)
    high, low = split(jnp.concatenate([table[0:32], table[64:96]], axis=0))
    across = jnp.concatenate([high, low], axis=0)
    high, low = split(jnp.concatenate([table[32:64], table[96:128]], axis=0))
    along = jnp.concatenate([high, low], axis=0)
    row64 = iota((64, SLOTS), 0).astype(F32)

    def add_borders(g, unused):
        for k in range(GROUP):
            c = g * GROUP + k
            found = dot(across, across_hits[c])
            total = jnp.where(row64 == across_place[c], found[0:64] + found[64:128], 0.0)
            found = dot(along, along_hits[c])
            total = total + jnp.where(
                row64 == along_place[c], found[0:64] + found[64:128], 0.0
            )
            border_terms[c] = jnp.sum(total, axis=0, keepdims=True) * (-1.0 / 9.0)
        return unused

    lax.fori_loop(0, CHUNKS // GROUP, add_borders, 0)
    all_copy(change_recv, 4).wait_recv()
    got = jnp.concatenate([change_recv[owner] for owner in range(N_XY)], axis=0)
    high, low = split(got)
    got = jnp.concatenate([high, low], axis=0)

    def add_change(g, total):
        lefts, rights = [], []
        for k in range(GROUP):
            c = g * GROUP + k
            found = dot(got, rank_hits[c])
            mine = owner_row == (targets_ref[c] >> 12)
            value = jnp.sum(
                jnp.where(mine, found[0:32] + found[32:64], 0.0), axis=0, keepdims=True
            )
            value = value + border_terms[c]
            here = row128 == (cells_ref[c] & 127).astype(F32)
            high = value.astype(BF16).astype(F32)
            rights.append(
                jnp.concatenate(
                    [jnp.where(here, high, 0.0), jnp.where(here, value - high, 0.0)], axis=0
                ).astype(BF16)
            )
            lefts.append(cell_hits[c])
        return total + dot_nt(jnp.concatenate(lefts, axis=1), jnp.concatenate(rights, axis=1))

    correction = lax.fori_loop(0, CHUNKS // GROUP, add_change, jnp.zeros((256, 256), F32))
    correction_out[...] = correction[:, 0:128] + correction[:, 128:256]
    for ref, index in (
        (edge_recv0, 0),
        (place_recv, 1),
        (value_recv, 2),
        (edge_recv1, 3),
        (change_recv, 4),
        (link_recv, 5),
    ):
        all_copy(ref, index).wait_send()


def add_kernel(read_ref, correction_ref, cover_ref, updated_hbm, cover_hbm, stage, sem):
    cover_copy = pltpu.make_async_copy(cover_ref, cover_hbm, sem.at[CX])
    cover_copy.start()
    copies = []
    for x in range(CX):
        stage[:, x] = read_ref[:, x] + correction_ref[x * NY : (x + 1) * NY, :][None]
        copies.append(pltpu.make_async_copy(stage.at[:, x], updated_hbm.at[:, x], sem.at[x]))
        copies[-1].start()
    for copy in copies:
        copy.wait()
    cover_copy.wait()


def shards(populations, solid, knudsen, wall_cells, wall_target, coverage, tile_links):
    hbm = pl.BlockSpec(memory_space=pltpu.HBM)
    vmem = pl.BlockSpec(memory_space=pltpu.VMEM)
    slots = pltpu.VMEM((N_XY, 1, SLOTS), F32)
    edge_table = pltpu.VMEM((N_XY, 8, 128), F32)
    by_chunk = pltpu.VMEM((CHUNKS, SLOTS, SLOTS), BF16)
    chunk_rows = pltpu.VMEM((CHUNKS, 1, SLOTS), F32)
    walls = pltpu.VMEM((CHUNKS, 1, SLOTS), jnp.int32)
    whole = jax.ShapeDtypeStruct((19, CX, NY, CZ), F32)
    cover_shape = jax.ShapeDtypeStruct((16, 256), F32)
    read, new_coverage, correction = pl.pallas_call(
        kernel,
        out_shape=(whole, cover_shape, jax.ShapeDtypeStruct((256, 128), F32)),
        in_specs=[hbm] * 7,
        out_specs=(vmem, vmem, vmem),
        scratch_shapes=[
            pltpu.VMEM((19, CX, NY, CZ), F32),
            pltpu.VMEM((CX, NY, CZ), jnp.int32),
            pltpu.VMEM((CX, NY, CZ), F32),
            walls,
            walls,
            pltpu.VMEM((16, 256), F32),
            pltpu.VMEM((4, 16), jnp.int32),
            pltpu.VMEM((19, CX + 2, NY, CZ), F32),
            pltpu.VMEM((CX, 8, 128), F32),
            pltpu.VMEM((CX, 8, 128), F32),
            pltpu.VMEM((CX + 2, 8, 128), F32),
            pltpu.VMEM((CX + 2, 8, 128), F32),
            pltpu.VMEM((CX * NY, CZ), F32),
            pltpu.VMEM((CHUNKS * N_XY, SLOTS), BF16),
            pltpu.VMEM((CHUNKS * N_XY, SLOTS), F32),
            pltpu.VMEM((CHUNKS * N_XY, SLOTS), F32),
            pltpu.VMEM((N_XY, SLOTS, SLOTS), BF16),
            pltpu.VMEM((N_XY, CZ, SLOTS), BF16),
            slots,
            slots,
            slots,
            slots,
            slots,
            slots,
            slots,
            slots,
            slots,
            pltpu.VMEM((8, 128), F32),
            edge_table,
            pltpu.VMEM((8, 128), F32),
            edge_table,
            pltpu.VMEM((4, 128), F32),
            pltpu.VMEM((N_XY, 4, 128), F32),
            pltpu.VMEM((4 * N_XY, 128), F32),
            by_chunk,
            by_chunk,
            by_chunk,
            by_chunk,
            chunk_rows,
            chunk_rows,
            chunk_rows,
            pltpu.SemaphoreType.DMA((14,)),
            pltpu.SemaphoreType.DMA((16,)),
            pltpu.SemaphoreType.DMA((16,)),
            pltpu.SemaphoreType.REGULAR,
            pltpu.SemaphoreType.DMA((6,)),
            pltpu.SemaphoreType.DMA((6,)),
        ],
        compiler_params=pltpu.CompilerParams(
            collective_id=0, has_side_effects=True, vmem_limit_bytes=40 * 1024 * 1024
        ),
    )(
        *[
            pltpu.with_memory_space_constraint(array, pltpu.HBM)
            for array in (
                populations,
                solid,
                knudsen,
                wall_cells.reshape(CHUNKS, 1, SLOTS),
                wall_target.reshape(CHUNKS, 1, SLOTS),
                coverage,
                tile_links.T,
            )
        ]
    )
    updated, new_coverage = pl.pallas_call(
        add_kernel,
        out_shape=(whole, cover_shape),
        in_specs=[vmem, vmem, vmem],
        out_specs=(hbm, hbm),
        scratch_shapes=[
            pltpu.VMEM((19, CX, NY, CZ), F32),
            pltpu.SemaphoreType.DMA((CX + 1,)),
        ],
        compiler_params=pltpu.CompilerParams(vmem_limit_bytes=16 * 1024 * 1024),
    )(read, correction, new_coverage)
    return updated, new_coverage


def solution(mesh):
    in_specs = (
        P(None, "xy", None, "gz"),
        P("xy", None, "gz"),
        P("xy", None, "gz"),
        P("gz", "xy"),
        P("gz", "xy"),
        P(("gz", "xy"), None),
        P(("gz", "xy"), None),
    )
    out_specs = (P(None, "xy", None, "gz"), P(("gz", "xy"), None))
    return jax.shard_map(shards, mesh=mesh, in_specs=in_specs, out_specs=out_specs, check_vma=False)
```

```python
import jax
import jax.numpy as jnp
from jax import lax
from jax.experimental import pallas as pl
from jax.experimental.pallas import tpu as pltpu
from jax.sharding import PartitionSpec as P

MESH = pl.DeviceIdType.MESH
F32 = jnp.float32
BF16 = jnp.bfloat16

VELOCITIES = [
    (0, 0, 0),
    (0, 1, 0),
    (0, -1, 0),
    (1, 0, 0),
    (-1, 0, 0),
    (0, 0, 1),
    (0, 0, -1),
    (1, 1, 0),
    (-1, -1, 0),
    (1, -1, 0),
    (-1, 1, 0),
    (1, 0, 1),
    (-1, 0, -1),
    (1, 0, -1),
    (-1, 0, 1),
    (0, 1, 1),
    (0, -1, -1),
    (0, 1, -1),
    (0, -1, 1),
]
WEIGHTS = [1.0 / 3.0] + [1.0 / 18.0] * 6 + [1.0 / 36.0] * 12
X_PLUS = [q for q in range(19) if VELOCITIES[q][0] == 1]
X_MINUS = [q for q in range(19) if VELOCITIES[q][0] == -1]
Z_PLUS = [q for q in range(19) if VELOCITIES[q][2] == 1]
Z_MINUS = [q for q in range(19) if VELOCITIES[q][2] == -1]

N_GZ = 8
N_XY = 32
CX = 8
NY = 32
CZ = 128
SLOTS = 256
CHUNKS = 16
OTHERS = N_XY - 1
NEAR = 19
GREETED = NEAR + 6
GROUP = 8
BATCH = 16
GROUPS = N_XY // GROUP


def iota(shape, dim):
    return lax.broadcasted_iota(jnp.int32, shape, dim)


def split(values):
    high = values.astype(BF16)
    low = (values - high.astype(F32)).astype(BF16)
    return high, low


def hits(mask):
    return jnp.where(mask, 1.0, 0.0).astype(BF16)


def hits16(rows, row):
    return jnp.where(rows == row.astype(BF16), BF16(1.0), BF16(0.0))


def dot(left, right):
    return lax.dot_general(left, right, (((1,), (0,)), ((), ())), preferred_element_type=F32)


def dot_nt(left, right):
    return lax.dot_general(left, right, (((1,), (1,)), ((), ())), preferred_element_type=F32)


def centred(step, size):
    return size // 2 + ((step + 1) // 2) * (1 - 2 * (step % 2))


def partner(me, step):
    z = lax.rem(lax.rem(me, 8) + centred(step // 4, 8), 8)
    x = lax.rem(lax.div(me, 8) + centred(step % 4, 4), 4)
    return x * 8 + z


def group_partners(me, group):
    place_z, place_x = lax.rem(me, 8), lax.div(me, 8)
    z = (lax.rem(place_z + 4 + group, 8), lax.rem(place_z + 11 - group, 8))
    x = [lax.rem(place_x + centred(k, 4), 4) * 8 for k in range(4)]
    return [x[k % 4] + z[k // 4] for k in range(8)]


def roll(values, shift, axis):
    shift = shift % values.shape[axis]
    return values if shift == 0 else pltpu.roll(values, shift, axis)


def edge_picker():
    cell, lane = iota((512, 128), 0), iota((512, 128), 1)
    side, place = (lane >> 4) & 3, lane & 15
    wanted = jnp.where(
        side == 0,
        place * 16 + 15,
        jnp.where(side == 1, place * 16, jnp.where(side == 2, 240 + place, place)),
    )
    return hits(cell == (lane >> 6) * 256 + wanted)


def tile_edges(cover, picker):
    both = jnp.concatenate([cover[0:8], cover[8:16]], axis=1)
    high, low = split(both)
    return dot(high, picker) + dot(low, picker)


def neighbour_matrix():
    a, b = iota((256, 256), 0), iota((256, 256), 1)
    same_row = (a >> 4) == (b >> 4)
    near = (same_row & (jnp.abs(a - b) == 1)) | (jnp.abs(a - b) == 16)
    inner = hits(near)
    s, k = iota((128, 256), 0), iota((128, 256), 1)
    side, place = (s >> 4) & 3, s & 15
    cell = jnp.where(
        side == 0,
        place * 16,
        jnp.where(side == 1, place * 16 + 15, jnp.where(side == 2, place, 240 + place)),
    )
    return jnp.concatenate([inner, inner, hits(k == cell)], axis=0)


def gather_edges(edges, link_hits, link_half):
    high, low = split(edges)
    found = dot(link_hits, jnp.concatenate([high, low], axis=1))
    lane = iota((16, 64), 1)
    out_high = jnp.zeros((16, 64), F32)
    out_low = jnp.zeros((16, 64), F32)
    for side in range(4):
        part = found[side * 16 : (side + 1) * 16]
        second = link_half[side] == 1
        h = jnp.where(second, part[:, 64:128], part[:, 0:64])
        l = jnp.where(second, part[:, 192:256], part[:, 128:192])
        here = (lane >> 4) == side
        out_high = jnp.where(here, h, out_high)
        out_low = jnp.where(here, l, out_low)
    return jnp.concatenate([out_high, out_low], axis=1)


def sweep(cover, source, borders, matrix):
    high, low = split(cover)
    row = jnp.concatenate([high, low, borders.astype(BF16)], axis=1)
    return (source + 2.0 * dot(row, matrix)) * (1.0 / 9.0)


def kernel(
    pop_hbm,
    solid_hbm,
    knudsen_hbm,
    cells_hbm,
    targets_hbm,
    cover_hbm,
    links_hbm,
    read_ref,
    cover_out,
    correction_out,
    pop,
    solid,
    knudsen,
    cells_ref,
    targets_ref,
    cover_ref,
    links_ref,
    rd,
    zs_p,
    zs_m,
    zr_p,
    zr_m,
    dens,
    owner_hits,
    ranks_ref,
    totals_ref,
    xy_hits,
    lane_hits,
    slot_xy,
    slot_z,
    place_row,
    place_send,
    place_recv,
    value_send,
    value_recv,
    change_send,
    change_recv,
    edge_send0,
    edge_recv0,
    edge_send1,
    edge_recv1,
    link_send,
    link_recv,
    link_table,
    cell_hits,
    rank_hits,
    across_hits,
    along_hits,
    across_place,
    along_place,
    border_terms,
    load_sem,
    halo_send,
    halo_recv,
    ready_sem,
    all_send,
    all_recv,
):
    gz = lax.axis_index("gz")
    me = lax.axis_index("xy")
    gz_up, gz_down = lax.rem(gz + 1, N_GZ), lax.rem(gz + N_GZ - 1, N_GZ)
    up, down = lax.rem(me + 1, N_XY), lax.rem(me + N_XY - 1, N_XY)

    def load(source, target, index):
        copy = pltpu.make_async_copy(source, target, load_sem.at[index])
        copy.start()
        return copy

    plane_loads = {}
    plane_loads[0] = load(pop_hbm.at[:, 0], pop.at[:, 0], 0)
    cell_loads = [load(solid_hbm, solid, 8), load(knudsen_hbm, knudsen, 9)]
    plane_loads[7] = load(pop_hbm.at[:, 7], pop.at[:, 7], 7)
    for x in range(1, 7):
        plane_loads[x] = load(pop_hbm.at[:, x], pop.at[:, x], x)
    wall_loads = [
        load(cells_hbm, cells_ref, 10),
        load(targets_hbm, targets_ref, 11),
        load(cover_hbm, cover_ref, 12),
        load(links_hbm, links_ref, 13),
    ]

    barrier = pltpu.get_barrier_semaphore()

    def greet_near(semaphore):
        for step_z in (2, 6, 1, 7, 0):
            z = lax.rem(lax.rem(me, 8) + step_z, 8)
            for step_x in (2, 1, 3, 0):
                if (step_z, step_x) != (0, 0):
                    x = lax.rem(lax.div(me, 8) + step_x, 4)
                    pl.semaphore_signal(
                        semaphore, inc=1, device_id=(gz, x * 8 + z), device_id_type=MESH
                    )

    for device in (
        (gz_up, up),
        (gz_up, down),
        (gz_down, up),
        (gz_down, down),
        (gz_up, me),
        (gz_down, me),
    ):
        pl.semaphore_signal(barrier, inc=1, device_id=device, device_id_type=MESH)
    greet_near(barrier)

    def send_one(source, target, index, other):
        pltpu.make_async_remote_copy(
            src_ref=source,
            dst_ref=target,
            send_sem=all_send.at[index],
            recv_sem=all_recv.at[index],
            device_id=(gz, other),
            device_id_type=MESH,
        ).start()

    def send_steps(source_of, target_ref, index, first, last):
        for step in range(first, last):
            other = partner(me, step)
            send_one(source_of(other), target_ref.at[me], index, other)

    def send_half(source, target, index, others, group, half):
        for other in others[half * 4 : half * 4 + 4 - half]:
            send_one(source.at[other], target.at[me], index, other)
        if half == 1:

            @pl.when(group < GROUPS - 1)
            def _():
                send_one(source.at[others[-1]], target.at[me], index, others[-1])

    def all_copy(ref, index):
        part = ref.at[pl.ds(0, OTHERS)]
        return pltpu.make_async_remote_copy(
            src_ref=part,
            dst_ref=part,
            send_sem=all_send.at[index],
            recv_sem=all_recv.at[index],
            device_id=(gz, up),
            device_id_type=MESH,
        )

    lane8 = iota((8, 128), 1)

    def collide_plane(x):
        kn = knudsen[x]
        sol = solid[x] == 1
        axis_sum = jnp.zeros((NY, CZ), F32)
        diag_sum = jnp.zeros((NY, CZ), F32)
        axis_m = [None] * 3
        diag_m = [None] * 3
        for q in range(1, 19, 2):
            p, m = pop[q, x], pop[q + 1, x]
            if q < 7:
                axis_sum = axis_sum + (p + m)
            else:
                diag_sum = diag_sum + (p + m)
            diff = p - m
            for axis in range(3):
                c = VELOCITIES[q][axis]
                sums = axis_m if q < 7 else diag_m
                if c == 0:
                    continue
                if sums[axis] is None:
                    sums[axis] = diff if c == 1 else -diff
                else:
                    sums[axis] = sums[axis] + diff if c == 1 else sums[axis] - diff
        rest = pop[0, x]
        density = (1.0 / 3.0) * rest + (1.0 / 18.0) * axis_sum + (1.0 / 36.0) * diag_sum
        inverse = 1.0 / density
        speed = [
            ((1.0 / 18.0) * axis_m[axis] + (1.0 / 36.0) * diag_m[axis]) * inverse
            for axis in range(3)
        ]
        square = speed[0] * speed[0] + speed[1] * speed[1] + speed[2] * speed[2]
        relax = (1.0 + 2.0 * kn) / (1.0 + kn)
        keep = 1.0 - relax
        gain = relax * density
        base = gain - 1.5 * gain * square
        gain3 = 3.0 * gain
        rd[0, x + 1] = jnp.where(sol, rest, keep * rest + base)
        tile_p = jnp.zeros((8, 128), F32)
        tile_m = jnp.zeros((8, 128), F32)
        for q in range(1, 19, 2):
            p, m = pop[q, x], pop[q + 1, x]
            along = None
            for axis in range(3):
                c = VELOCITIES[q][axis]
                if c == 0:
                    continue
                if along is None:
                    along = speed[axis] if c == 1 else -speed[axis]
                else:
                    along = along + speed[axis] if c == 1 else along - speed[axis]
            odd = gain3 * along
            even = base + 1.5 * odd * along
            new_p = jnp.where(sol, m, keep * p + (even + odd))
            new_m = jnp.where(sol, p, keep * m + (even - odd))
            for member, value in ((q, new_p), (q + 1, new_m)):
                cx, cy, cz = VELOCITIES[member]
                value = roll(value, cy, 0)
                value = roll(value, cz, 1)
                rd[member, x + 1 + cx] = value
                if cz == 1:
                    k = Z_PLUS.index(member)
                    for block in range(4):
                        at = k * 4 + block
                        moved = roll(value[block * 8 : block * 8 + 8], at, 1)
                        tile_p = jnp.where(lane8 == at, moved, tile_p)
                if cz == -1:
                    k = Z_MINUS.index(member)
                    for block in range(4):
                        at = k * 4 + block
                        moved = roll(value[block * 8 : block * 8 + 8], at + 1, 1)
                        tile_m = jnp.where(lane8 == at, moved, tile_m)
        zs_p[x] = tile_p
        zs_m[x] = tile_m

    def edge_step(i, unused):
        collide_plane(i * 7)
        return unused

    def inner_step(i, unused):
        collide_plane(i)
        return unused

    def halo(source, target, index, device):
        return pltpu.make_async_remote_copy(
            src_ref=source,
            dst_ref=target,
            send_sem=halo_send.at[index],
            recv_sem=halo_recv.at[index],
            device_id=device,
            device_id_type=MESH,
        )

    for copy in cell_loads + [plane_loads[0], plane_loads[7]]:
        copy.wait()
    lax.fori_loop(0, 2, edge_step, 0)
    pl.semaphore_wait(barrier, GREETED)
    halos = []
    halos.append(halo(zs_p.at[7], zr_p.at[0], 12, (gz_up, up)))
    halos.append(halo(zs_p.at[0], zr_p.at[9], 13, (gz_up, down)))
    halos.append(halo(zs_m.at[7], zr_m.at[0], 14, (gz_down, up)))
    halos.append(halo(zs_m.at[0], zr_m.at[9], 15, (gz_down, down)))
    for k in range(5):
        halos.append(halo(rd.at[X_PLUS[k], 9], rd.at[X_PLUS[k], 1], k, (gz, up)))
        halos.append(halo(rd.at[X_MINUS[k], 0], rd.at[X_MINUS[k], 8], 5 + k, (gz, down)))
    for copy in halos:
        copy.start()
    greet_near(ready_sem)
    for x in range(1, 7):
        plane_loads[x].wait()
    lax.fori_loop(1, 7, inner_step, 0)
    faces = [
        halo(zs_p, zr_p.at[pl.ds(1, CX)], 10, (gz_up, me)),
        halo(zs_m, zr_m.at[pl.ds(1, CX)], 11, (gz_down, me)),
    ]
    for copy in faces:
        copy.start()
    halos = halos + faces
    for copy in wall_loads:
        copy.wait()

    owner_row = iota((N_XY, SLOTS), 0)
    row256 = iota((SLOTS, SLOTS), 0).astype(F32).astype(BF16)
    row128 = iota((CZ, SLOTS), 0).astype(F32)
    row128_16 = row128.astype(BF16)
    row32 = iota((N_XY, SLOTS), 0).astype(F32)

    for c in range(CHUNKS):
        owner_hits[c * N_XY : (c + 1) * N_XY, :] = hits(owner_row == (targets_ref[c] >> 12))
    before = hits(iota((SLOTS, SLOTS), 0) < iota((SLOTS, SLOTS), 1))
    ranks_ref[...] = dot(owner_hits[...], before)
    totals_ref[...] = dot(owner_hits[...], jnp.ones((SLOTS, SLOTS), BF16))

    def fill_slots(g, carry):
        base, table = carry
        lefts, rights = [], []
        for k in range(BATCH):
            c = g * BATCH + k
            start = pl.multiple_of(c * N_XY, N_XY)
            ranks = ranks_ref[pl.ds(start, N_XY), :] + base
            base = base + totals_ref[pl.ds(start, N_XY), :]
            target = targets_ref[c]
            cell = cells_ref[c]
            mine = owner_row == (target >> 12)
            rank = jnp.sum(jnp.where(mine, ranks, 0.0), axis=0, keepdims=True)
            place = target & 4095
            fields = [
                cell >> 7,
                (cell & 127) + 1,
                ((place >> 7) & 1) * 16 + (place >> 8),
                place & 127,
            ]
            lefts.append(
                jnp.concatenate(
                    [jnp.where(mine, field.astype(F32), 0.0) for field in fields], axis=0
                ).astype(BF16)
            )
            rank_hits[c] = hits16(row256, rank)
            cell_hits[c] = hits16(row256, fields[0].astype(F32))
            rights.append(rank_hits[c])
        table = table + dot_nt(jnp.concatenate(lefts, axis=1), jnp.concatenate(rights, axis=1))
        return base, table

    unused, table = lax.fori_loop(
        0,
        CHUNKS // BATCH,
        fill_slots,
        (jnp.zeros((N_XY, SLOTS), F32), jnp.zeros((4 * N_XY, SLOTS), F32)),
    )
    places = table[64:96] * 128.0 + table[96:128]
    for owner in range(N_XY):
        slot_xy[owner] = table[owner : owner + 1]
        slot_z[owner] = table[32 + owner : 33 + owner] - 1.0
        place_send[owner] = places[owner : owner + 1]
    place_recv[me] = place_send[me]

    picker = edge_picker()
    cover = cover_ref[...]
    edges = tile_edges(cover, picker)
    edge_send0[...] = edges
    edge_recv0[me] = edges
    links = links_ref[...]
    codes = (links >> 4) * 8 + (links & 7) + ((links >> 3) & 1) * 256
    link_send[...] = jnp.zeros_like(link_send)
    link_send[:, 0:16] = codes.astype(F32)
    link_recv[me] = link_send[...]

    def mark_cells(g, unused):
        for k in range(GROUP):
            owner = g * GROUP + k
            xy_hits[owner] = hits16(row256, slot_xy[owner])
        return unused

    lax.fori_loop(0, GROUPS, mark_cells, 0)

    def border(q, x):
        cx, cy, cz = VELOCITIES[q]
        k = (Z_PLUS if cz == 1 else Z_MINUS).index(q)
        got = (zr_p if cz == 1 else zr_m)[x - cx + 1]
        edge = 0 if cz == 1 else 127
        return jnp.concatenate(
            [roll(got, edge - (k * 4 + block), 1) for block in range(4)], axis=0
        )

    def inner_plane(x, unused):
        total = None
        for q in range(19):
            value = rd[q, x + 1]
            read_ref[q, x] = value
            term = WEIGHTS[q] * value
            total = term if total is None else total + term
        dens[pl.ds(pl.multiple_of(x * NY, NY), NY), :] = total
        return unused

    lax.fori_loop(1, CX - 1, inner_plane, 0)
    pl.semaphore_wait(ready_sem, NEAR)
    send_steps(lambda other: place_send.at[other], place_recv, 1, 0, OTHERS)
    send_steps(lambda other: edge_send0, edge_recv0, 0, 0, OTHERS)

    for copy in halos:
        copy.wait_recv()

    def finish_plane(i, unused):
        x = i * 7
        lane = iota((NY, CZ), 1)
        total = None
        for q in range(19):
            cx, cy, cz = VELOCITIES[q]
            value = rd[q, x + 1]
            if cz != 0:
                value = jnp.where(lane == (0 if cz == 1 else 127), border(q, x), value)
            read_ref[q, x] = value
            term = WEIGHTS[q] * value
            total = term if total is None else total + term
        dens[pl.ds(pl.multiple_of(x * NY, NY), NY), :] = total
        return unused

    def mend_plane(x, unused):
        lane = iota((NY, CZ), 1)
        rows = pl.ds(pl.multiple_of(x * NY, NY), NY)
        total = dens[rows, :]
        for members, edge in ((Z_PLUS, 0), (Z_MINUS, 127)):
            for q in members:
                old = read_ref[q, x]
                new = jnp.where(lane == edge, border(q, x), old)
                read_ref[q, x] = new
                total = total + WEIGHTS[q] * (new - old)
        dens[rows, :] = total
        return unused

    lax.fori_loop(1, CX - 1, mend_plane, 0)
    lax.fori_loop(0, 2, finish_plane, 0)

    high, low = split(jnp.transpose(dens[...]))
    dens_t = jnp.concatenate([high, low], axis=0)

    def send_values(g, unused):
        others = group_partners(me, g)
        for half in range(2):
            for other in others[half * 4 : half * 4 + 4]:
                found = dot(dens_t, xy_hits[other])
                both = found[0:128] + found[128:256]
                value_send[other] = jnp.sum(
                    jnp.where(row128 == slot_z[other], both, 0.0), axis=0, keepdims=True
                )
            send_half(value_send, value_recv, 2, others, g, half)
        return unused

    lax.fori_loop(0, GROUPS, send_values, 0)
    value_recv[me] = value_send[me]
    send_steps(lambda other: link_send, link_recv, 5, 0, OTHERS)

    links = jnp.transpose(links_ref[...].astype(F32)).astype(jnp.int32)
    link_hits = []
    link_half = []
    lane256 = iota((16, 256), 1)
    for side in range(4):
        tile = links[:, side : side + 1]
        link_hits.append(hits(lane256 == (tile >> 4) * 8 + (tile & 7)))
        link_half.append((tile >> 3) & 1)
    link_hits = jnp.concatenate(link_hits, axis=0)
    matrix = neighbour_matrix()
    all_copy(edge_recv0, 0).wait_recv()
    borders = gather_edges(edge_recv0[...].reshape(256, 128), link_hits, link_half)
    all_copy(place_recv, 1).wait_recv()

    def mark_places(g, unused):
        for k in range(GROUP):
            brick = g * GROUP + k
            place = place_recv[brick]
            row = jnp.floor(place * (1.0 / 128.0))
            place_row[brick] = row
            lane_hits[brick] = hits16(row128_16, place - 128.0 * row)
        return unused

    lax.fori_loop(0, GROUPS, mark_places, 0)
    all_copy(value_recv, 2).wait_recv()

    def add_supply(g, total):
        lefts, rights = [], []
        for k in range(16):
            brick = g * 16 + k
            value = value_recv[brick]
            here = row32 == place_row[brick]
            high = value.astype(BF16).astype(F32)
            lefts.append(
                jnp.concatenate(
                    [jnp.where(here, high, 0.0), jnp.where(here, value - high, 0.0)], axis=0
                ).astype(BF16)
            )
            rights.append(lane_hits[brick])
        return total + dot_nt(jnp.concatenate(lefts, axis=1), jnp.concatenate(rights, axis=1))

    supply = lax.fori_loop(0, N_XY // 16, add_supply, jnp.zeros((64, 128), F32))
    supply = supply[0:32] + supply[32:64]
    supply = jnp.concatenate([supply[0:16], supply[16:32]], axis=1)
    source = cover + 0.3 * supply * (1.0 - cover) - 0.2 * cover
    first = sweep(cover, source, borders, matrix)
    edges = tile_edges(first, picker)
    edge_send1[...] = edges
    edge_recv1[me] = edges
    send_steps(lambda other: edge_send1, edge_recv1, 3, 0, OTHERS)
    high, low = split(first)
    second = dot(jnp.concatenate([high, low], axis=1), matrix[0:512])
    second = (source + 2.0 * second) * (1.0 / 9.0)
    change = -0.5 * (second - cover)
    change = jnp.concatenate([change[:, 0:128], change[:, 128:256]], axis=0)
    high, low = split(change)
    change = jnp.concatenate([high, low], axis=0)

    def send_changes(g, unused):
        others = group_partners(me, g)
        for half in range(2):
            for other in others[half * 4 : half * 4 + 4]:
                found = dot(change, lane_hits[other])
                both = found[0:32] + found[32:64]
                change_send[other] = jnp.sum(
                    jnp.where(row32 == place_row[other], both, 0.0), axis=0, keepdims=True
                )
            send_half(change_send, change_recv, 4, others, g, half)
        return unused

    lax.fori_loop(0, GROUPS, send_changes, 0)
    change_recv[me] = change_send[me]
    for copy in halos:
        copy.wait_send()
    all_copy(link_recv, 5).wait_recv()
    for owner in range(N_XY):
        link_table[owner * 4 : owner * 4 + 4, :] = link_recv[owner]
    codes = jnp.transpose(link_table[...])[0:16]
    second_half = jnp.where(codes >= 256.0, 1.0, 0.0)
    codes = jnp.concatenate([codes - 256.0 * second_half, second_half], axis=0).astype(BF16)
    row16 = iota((16, SLOTS), 0)

    def find_border(select, tile, valid, far, place):
        found = dot(codes, hits16(row128_16, select.astype(F32)))
        here = row16 == tile
        row = jnp.sum(jnp.where(here, found[0:16], 0.0), axis=0, keepdims=True)
        half = jnp.sum(jnp.where(here, found[16:32], 0.0), axis=0, keepdims=True)
        return jnp.where(valid, row, -1.0), half * 32.0 + (far * 16 + place).astype(F32)

    def mark_borders(g, unused):
        for k in range(BATCH):
            c = g * BATCH + k
            target = targets_ref[c]
            owner, tile = target >> 12, (target >> 8) & 15
            y, x = (target >> 4) & 15, target & 15
            far_x = jnp.where(x == 15, 1, 0)
            far_y = jnp.where(y == 15, 1, 0)
            row, place = find_border(owner * 4 + far_x, tile, (x == 0) | (x == 15), far_x, y)
            across_hits[c] = hits16(row256, row)
            across_place[c] = place
            row, place = find_border(owner * 4 + 2 + far_y, tile, (y == 0) | (y == 15), far_y, x)
            along_hits[c] = hits16(row256, row)
            along_place[c] = place
        return unused

    lax.fori_loop(0, CHUNKS // BATCH, mark_borders, 0)
    all_copy(edge_recv1, 3).wait_recv()
    table = edge_recv1[...].reshape(256, 128)
    table_t = jnp.transpose(table)
    high, low = split(jnp.concatenate([table_t[0:32], table_t[64:96]], axis=0))
    across = jnp.concatenate([high, low], axis=0)
    high, low = split(jnp.concatenate([table_t[32:64], table_t[96:128]], axis=0))
    along = jnp.concatenate([high, low], axis=0)
    row64 = iota((64, SLOTS), 0).astype(F32)

    def add_borders(g, unused):
        for k in range(BATCH):
            c = g * BATCH + k
            found = dot(across, across_hits[c])
            total = jnp.where(row64 == across_place[c], found[0:64] + found[64:128], 0.0)
            found = dot(along, along_hits[c])
            total = total + jnp.where(
                row64 == along_place[c], found[0:64] + found[64:128], 0.0
            )
            border_terms[c] = jnp.sum(total, axis=0, keepdims=True) * (-1.0 / 9.0)
        return unused

    lax.fori_loop(0, CHUNKS // BATCH, add_borders, 0)
    borders = gather_edges(table, link_hits, link_half)
    cover_out[...] = second + dot(borders.astype(BF16), matrix[512:640]) * (2.0 / 9.0)
    all_copy(change_recv, 4).wait_recv()
    got = jnp.concatenate([change_recv[owner] for owner in range(N_XY)], axis=0)
    high, low = split(got)
    got = jnp.concatenate([high, low], axis=0)

    def add_change(g, total):
        lefts, rights = [], []
        for k in range(BATCH):
            c = g * BATCH + k
            found = dot(got, rank_hits[c])
            mine = owner_row == (targets_ref[c] >> 12)
            value = jnp.sum(
                jnp.where(mine, found[0:32] + found[32:64], 0.0), axis=0, keepdims=True
            )
            value = value + border_terms[c]
            here = row128 == (cells_ref[c] & 127).astype(F32)
            high = value.astype(BF16).astype(F32)
            rights.append(
                jnp.concatenate(
                    [jnp.where(here, high, 0.0), jnp.where(here, value - high, 0.0)], axis=0
                ).astype(BF16)
            )
            lefts.append(cell_hits[c])
        return total + dot_nt(jnp.concatenate(lefts, axis=1), jnp.concatenate(rights, axis=1))

    correction = lax.fori_loop(0, CHUNKS // BATCH, add_change, jnp.zeros((256, 256), F32))
    correction_out[...] = correction[:, 0:128] + correction[:, 128:256]
    for ref, index in (
        (edge_recv0, 0),
        (place_recv, 1),
        (value_recv, 2),
        (edge_recv1, 3),
        (change_recv, 4),
        (link_recv, 5),
    ):
        all_copy(ref, index).wait_send()


def add_kernel(read_ref, correction_ref, cover_ref, updated_hbm, cover_hbm, stage, sem):
    cover_copy = pltpu.make_async_copy(cover_ref, cover_hbm, sem.at[CX])
    cover_copy.start()
    copies = []
    for x in range(CX):
        for part in (pl.ds(0, 10), pl.ds(10, 9)):
            stage[part, x] = read_ref[part, x] + correction_ref[x * NY : (x + 1) * NY, :][None]
        copies.append(pltpu.make_async_copy(stage.at[:, x], updated_hbm.at[:, x], sem.at[x]))
        copies[-1].start()
    for copy in copies:
        copy.wait()
    cover_copy.wait()


def shards(populations, solid, knudsen, wall_cells, wall_target, coverage, tile_links):
    hbm = pl.BlockSpec(memory_space=pltpu.HBM)
    vmem = pl.BlockSpec(memory_space=pltpu.VMEM)
    slots = pltpu.VMEM((N_XY, 1, SLOTS), F32)
    edge_table = pltpu.VMEM((N_XY, 8, 128), F32)
    by_chunk = pltpu.VMEM((CHUNKS, SLOTS, SLOTS), BF16)
    chunk_rows = pltpu.VMEM((CHUNKS, 1, SLOTS), F32)
    walls = pltpu.VMEM((CHUNKS, 1, SLOTS), jnp.int32)
    whole = jax.ShapeDtypeStruct((19, CX, NY, CZ), F32)
    cover_shape = jax.ShapeDtypeStruct((16, 256), F32)
    read, new_coverage, correction = pl.pallas_call(
        kernel,
        out_shape=(whole, cover_shape, jax.ShapeDtypeStruct((256, 128), F32)),
        in_specs=[hbm] * 7,
        out_specs=(vmem, vmem, vmem),
        scratch_shapes=[
            pltpu.VMEM((19, CX, NY, CZ), F32),
            pltpu.VMEM((CX, NY, CZ), jnp.int32),
            pltpu.VMEM((CX, NY, CZ), F32),
            walls,
            walls,
            pltpu.VMEM((16, 256), F32),
            pltpu.VMEM((4, 16), jnp.int32),
            pltpu.VMEM((19, CX + 2, NY, CZ), F32),
            pltpu.VMEM((CX, 8, 128), F32),
            pltpu.VMEM((CX, 8, 128), F32),
            pltpu.VMEM((CX + 2, 8, 128), F32),
            pltpu.VMEM((CX + 2, 8, 128), F32),
            pltpu.VMEM((CX * NY, CZ), F32),
            pltpu.VMEM((CHUNKS * N_XY, SLOTS), BF16),
            pltpu.VMEM((CHUNKS * N_XY, SLOTS), F32),
            pltpu.VMEM((CHUNKS * N_XY, SLOTS), F32),
            pltpu.VMEM((N_XY, SLOTS, SLOTS), BF16),
            pltpu.VMEM((N_XY, CZ, SLOTS), BF16),
            slots,
            slots,
            slots,
            slots,
            slots,
            slots,
            slots,
            slots,
            slots,
            pltpu.VMEM((8, 128), F32),
            edge_table,
            pltpu.VMEM((8, 128), F32),
            edge_table,
            pltpu.VMEM((4, 128), F32),
            pltpu.VMEM((N_XY, 4, 128), F32),
            pltpu.VMEM((4 * N_XY, 128), F32),
            by_chunk,
            by_chunk,
            by_chunk,
            by_chunk,
            chunk_rows,
            chunk_rows,
            chunk_rows,
            pltpu.SemaphoreType.DMA((14,)),
            pltpu.SemaphoreType.DMA((16,)),
            pltpu.SemaphoreType.DMA((16,)),
            pltpu.SemaphoreType.REGULAR,
            pltpu.SemaphoreType.DMA((6,)),
            pltpu.SemaphoreType.DMA((6,)),
        ],
        compiler_params=pltpu.CompilerParams(
            collective_id=0, has_side_effects=True, vmem_limit_bytes=40 * 1024 * 1024
        ),
    )(
        *[
            pltpu.with_memory_space_constraint(array, pltpu.HBM)
            for array in (
                populations,
                solid,
                knudsen,
                wall_cells.reshape(CHUNKS, 1, SLOTS),
                wall_target.reshape(CHUNKS, 1, SLOTS),
                coverage,
                tile_links.T,
            )
        ]
    )
    updated, new_coverage = pl.pallas_call(
        add_kernel,
        out_shape=(whole, cover_shape),
        in_specs=[vmem, vmem, vmem],
        out_specs=(hbm, hbm),
        scratch_shapes=[
            pltpu.VMEM((19, CX, NY, CZ), F32),
            pltpu.SemaphoreType.DMA((CX + 1,)),
        ],
        compiler_params=pltpu.CompilerParams(vmem_limit_bytes=16 * 1024 * 1024),
    )(read, correction, new_coverage)
    return updated, new_coverage


def solution(mesh):
    in_specs = (
        P(None, "xy", None, "gz"),
        P("xy", None, "gz"),
        P("xy", None, "gz"),
        P("gz", "xy"),
        P("gz", "xy"),
        P(("gz", "xy"), None),
        P(("gz", "xy"), None),
    )
    out_specs = (P(None, "xy", None, "gz"), P(("gz", "xy"), None))
    return jax.shard_map(shards, mesh=mesh, in_specs=in_specs, out_specs=out_specs, check_vma=False)
```

```python
import jax
import jax.numpy as jnp
from jax import lax
from jax.experimental import pallas as pl
from jax.experimental.pallas import tpu as pltpu
from jax.sharding import PartitionSpec as P

MESH = pl.DeviceIdType.MESH
F32 = jnp.float32
BF16 = jnp.bfloat16

VELOCITIES = [
    (0, 0, 0),
    (0, 1, 0),
    (0, -1, 0),
    (1, 0, 0),
    (-1, 0, 0),
    (0, 0, 1),
    (0, 0, -1),
    (1, 1, 0),
    (-1, -1, 0),
    (1, -1, 0),
    (-1, 1, 0),
    (1, 0, 1),
    (-1, 0, -1),
    (1, 0, -1),
    (-1, 0, 1),
    (0, 1, 1),
    (0, -1, -1),
    (0, 1, -1),
    (0, -1, 1),
]
WEIGHTS = [1.0 / 3.0] + [1.0 / 18.0] * 6 + [1.0 / 36.0] * 12
X_PLUS = [q for q in range(19) if VELOCITIES[q][0] == 1]
X_MINUS = [q for q in range(19) if VELOCITIES[q][0] == -1]
Z_PLUS = [q for q in range(19) if VELOCITIES[q][2] == 1]
Z_MINUS = [q for q in range(19) if VELOCITIES[q][2] == -1]

N_GZ = 8
N_XY = 32
CX = 8
NY = 32
CZ = 128
SLOTS = 256
CHUNKS = 16
OTHERS = N_XY - 1
NEAR = 19
GREETED = NEAR + 6
GROUP = 8
BATCH = 16
GROUPS = N_XY // GROUP


def iota(shape, dim):
    return lax.broadcasted_iota(jnp.int32, shape, dim)


def split(values):
    high = values.astype(BF16)
    low = (values - high.astype(F32)).astype(BF16)
    return high, low


def hits(mask):
    return jnp.where(mask, 1.0, 0.0).astype(BF16)


def hits16(rows, row):
    return jnp.where(rows == row.astype(BF16), BF16(1.0), BF16(0.0))


def dot(left, right):
    return lax.dot_general(left, right, (((1,), (0,)), ((), ())), preferred_element_type=F32)


def dot_nt(left, right):
    return lax.dot_general(left, right, (((1,), (1,)), ((), ())), preferred_element_type=F32)


def centred(step, size):
    return size // 2 + ((step + 1) // 2) * (1 - 2 * (step % 2))


def partner(me, step):
    z = lax.rem(lax.rem(me, 8) + centred(step // 4, 8), 8)
    x = lax.rem(lax.div(me, 8) + centred(step % 4, 4), 4)
    return x * 8 + z


def group_partners(me, group):
    place_z, place_x = lax.rem(me, 8), lax.div(me, 8)
    z = (lax.rem(place_z + 4 + group, 8), lax.rem(place_z + 11 - group, 8))
    x = [lax.rem(place_x + centred(k, 4), 4) * 8 for k in range(4)]
    return [x[k % 4] + z[k // 4] for k in range(8)]


def roll(values, shift, axis):
    shift = shift % values.shape[axis]
    return values if shift == 0 else pltpu.roll(values, shift, axis)


def edge_picker():
    cell, lane = iota((512, 128), 0), iota((512, 128), 1)
    side, place = (lane >> 4) & 3, lane & 15
    wanted = jnp.where(
        side == 0,
        place * 16 + 15,
        jnp.where(side == 1, place * 16, jnp.where(side == 2, 240 + place, place)),
    )
    return hits(cell == (lane >> 6) * 256 + wanted)


def tile_edges(cover, picker):
    both = jnp.concatenate([cover[0:8], cover[8:16]], axis=1)
    high, low = split(both)
    twice = jnp.concatenate([picker, picker], axis=0)
    return dot(jnp.concatenate([high, low], axis=1), twice)


def neighbour_matrix():
    a, b = iota((256, 256), 0), iota((256, 256), 1)
    same_row = (a >> 4) == (b >> 4)
    near = (same_row & (jnp.abs(a - b) == 1)) | (jnp.abs(a - b) == 16)
    inner = hits(near)
    s, k = iota((128, 256), 0), iota((128, 256), 1)
    side, place = (s >> 4) & 3, s & 15
    cell = jnp.where(
        side == 0,
        place * 16,
        jnp.where(side == 1, place * 16 + 15, jnp.where(side == 2, place, 240 + place)),
    )
    return jnp.concatenate([inner, inner, hits(k == cell)], axis=0)


def gather_edges(edges, link_hits, link_half):
    high, low = split(edges)
    found = dot(link_hits, jnp.concatenate([high, low], axis=1))
    lane = iota((16, 64), 1)
    out_high = jnp.zeros((16, 64), F32)
    out_low = jnp.zeros((16, 64), F32)
    for side in range(4):
        part = found[side * 16 : (side + 1) * 16]
        second = link_half[side] == 1
        h = jnp.where(second, part[:, 64:128], part[:, 0:64])
        l = jnp.where(second, part[:, 192:256], part[:, 128:192])
        here = (lane >> 4) == side
        out_high = jnp.where(here, h, out_high)
        out_low = jnp.where(here, l, out_low)
    return jnp.concatenate([out_high, out_low], axis=1)


def neighbour_sum(cover, borders, matrix):
    high, low = split(cover)
    return dot(jnp.concatenate([high, low, borders.astype(BF16)], axis=1), matrix)


def kernel(
    pop_hbm,
    solid_hbm,
    knudsen_hbm,
    cells_hbm,
    targets_hbm,
    cover_hbm,
    links_hbm,
    read_ref,
    cover_out,
    correction_out,
    pop,
    solid,
    knudsen,
    cells_ref,
    targets_ref,
    cover_ref,
    links_ref,
    rd,
    zs_p,
    zs_m,
    zr_p,
    zr_m,
    dens,
    owner_hits,
    ranks_ref,
    totals_ref,
    xy_hits,
    lane_hits,
    slot_xy,
    slot_z,
    place_row,
    place_send,
    place_recv,
    value_send,
    value_recv,
    change_send,
    change_recv,
    edge_send0,
    edge_recv0,
    edge_send1,
    edge_recv1,
    link_send,
    link_recv,
    link_table,
    cell_hits,
    rank_hits,
    across_hits,
    along_hits,
    across_place,
    along_place,
    border_terms,
    load_sem,
    halo_send,
    halo_recv,
    ready_sem,
    all_send,
    all_recv,
):
    gz = lax.axis_index("gz")
    me = lax.axis_index("xy")
    gz_up, gz_down = lax.rem(gz + 1, N_GZ), lax.rem(gz + N_GZ - 1, N_GZ)
    up, down = lax.rem(me + 1, N_XY), lax.rem(me + N_XY - 1, N_XY)

    def load(source, target, index):
        copy = pltpu.make_async_copy(source, target, load_sem.at[index])
        copy.start()
        return copy

    plane_loads = {}
    plane_loads[0] = load(pop_hbm.at[:, 0], pop.at[:, 0], 0)
    cell_loads = [load(solid_hbm, solid, 8), load(knudsen_hbm, knudsen, 9)]
    plane_loads[7] = load(pop_hbm.at[:, 7], pop.at[:, 7], 7)

    barrier = pltpu.get_barrier_semaphore()

    def greet_near(semaphore):
        for step_z in (2, 6, 1, 7, 0):
            z = lax.rem(lax.rem(me, 8) + step_z, 8)
            for step_x in (2, 1, 3, 0):
                if (step_z, step_x) != (0, 0):
                    x = lax.rem(lax.div(me, 8) + step_x, 4)
                    pl.semaphore_signal(
                        semaphore, inc=1, device_id=(gz, x * 8 + z), device_id_type=MESH
                    )

    for device in (
        (gz_up, up),
        (gz_up, down),
        (gz_down, up),
        (gz_down, down),
        (gz_up, me),
        (gz_down, me),
    ):
        pl.semaphore_signal(barrier, inc=1, device_id=device, device_id_type=MESH)
    greet_near(barrier)
    for x in range(1, 7):
        plane_loads[x] = load(pop_hbm.at[:, x], pop.at[:, x], x)
    wall_loads = [
        load(cells_hbm, cells_ref, 10),
        load(targets_hbm, targets_ref, 11),
        load(cover_hbm, cover_ref, 12),
        load(links_hbm, links_ref, 13),
    ]

    def send_one(source, target, index, other):
        pltpu.make_async_remote_copy(
            src_ref=source,
            dst_ref=target,
            send_sem=all_send.at[index],
            recv_sem=all_recv.at[index],
            device_id=(gz, other),
            device_id_type=MESH,
        ).start()

    def send_steps(source_of, target_ref, index, first, last):
        for step in range(first, last):
            other = partner(me, step)
            send_one(source_of(other), target_ref.at[me], index, other)

    def send_half(source, target, index, others, group, half):
        for other in others[half * 4 : half * 4 + 4 - half]:
            send_one(source.at[other], target.at[me], index, other)
        if half == 1:

            @pl.when(group < GROUPS - 1)
            def _():
                send_one(source.at[others[-1]], target.at[me], index, others[-1])

    def all_copy(ref, index):
        part = ref.at[pl.ds(0, OTHERS)]
        return pltpu.make_async_remote_copy(
            src_ref=part,
            dst_ref=part,
            send_sem=all_send.at[index],
            recv_sem=all_recv.at[index],
            device_id=(gz, up),
            device_id_type=MESH,
        )

    lane8 = iota((8, 128), 1)

    def collide_plane(x):
        kn = knudsen[x]
        sol = solid[x] == 1
        axis_sum = jnp.zeros((NY, CZ), F32)
        diag_sum = jnp.zeros((NY, CZ), F32)
        axis_m = [None] * 3
        diag_m = [None] * 3
        for q in range(1, 19, 2):
            p, m = pop[q, x], pop[q + 1, x]
            if q < 7:
                axis_sum = axis_sum + (p + m)
            else:
                diag_sum = diag_sum + (p + m)
            diff = p - m
            for axis in range(3):
                c = VELOCITIES[q][axis]
                sums = axis_m if q < 7 else diag_m
                if c == 0:
                    continue
                if sums[axis] is None:
                    sums[axis] = diff if c == 1 else -diff
                else:
                    sums[axis] = sums[axis] + diff if c == 1 else sums[axis] - diff
        rest = pop[0, x]
        density = (1.0 / 3.0) * rest + (1.0 / 18.0) * axis_sum + (1.0 / 36.0) * diag_sum
        inverse = 1.0 / density
        speed = [
            ((1.0 / 18.0) * axis_m[axis] + (1.0 / 36.0) * diag_m[axis]) * inverse
            for axis in range(3)
        ]
        square = speed[0] * speed[0] + speed[1] * speed[1] + speed[2] * speed[2]
        relax = (1.0 + 2.0 * kn) / (1.0 + kn)
        keep = 1.0 - relax
        gain = relax * density
        base = gain - 1.5 * gain * square
        gain3 = 3.0 * gain
        rd[0, x + 1] = jnp.where(sol, rest, keep * rest + base)
        tile_p = jnp.zeros((8, 128), F32)
        tile_m = jnp.zeros((8, 128), F32)
        for q in range(1, 19, 2):
            p, m = pop[q, x], pop[q + 1, x]
            along = None
            for axis in range(3):
                c = VELOCITIES[q][axis]
                if c == 0:
                    continue
                if along is None:
                    along = speed[axis] if c == 1 else -speed[axis]
                else:
                    along = along + speed[axis] if c == 1 else along - speed[axis]
            odd = gain3 * along
            even = base + 1.5 * odd * along
            new_p = jnp.where(sol, m, keep * p + (even + odd))
            new_m = jnp.where(sol, p, keep * m + (even - odd))
            for member, value in ((q, new_p), (q + 1, new_m)):
                cx, cy, cz = VELOCITIES[member]
                value = roll(value, cy, 0)
                value = roll(value, cz, 1)
                rd[member, x + 1 + cx] = value
                if cz == 1:
                    k = Z_PLUS.index(member)
                    for block in range(4):
                        at = k * 4 + block
                        moved = roll(value[block * 8 : block * 8 + 8], at, 1)
                        tile_p = jnp.where(lane8 == at, moved, tile_p)
                if cz == -1:
                    k = Z_MINUS.index(member)
                    for block in range(4):
                        at = k * 4 + block
                        moved = roll(value[block * 8 : block * 8 + 8], at + 1, 1)
                        tile_m = jnp.where(lane8 == at, moved, tile_m)
        zs_p[x] = tile_p
        zs_m[x] = tile_m

    def edge_step(i, unused):
        collide_plane(i * 7)
        return unused

    def inner_step(i, unused):
        collide_plane(i)
        return unused

    def halo(source, target, index, device):
        return pltpu.make_async_remote_copy(
            src_ref=source,
            dst_ref=target,
            send_sem=halo_send.at[index],
            recv_sem=halo_recv.at[index],
            device_id=device,
            device_id_type=MESH,
        )

    for copy in cell_loads + [plane_loads[0], plane_loads[7]]:
        copy.wait()
    lax.fori_loop(0, 2, edge_step, 0)
    pl.semaphore_wait(barrier, GREETED)
    halos = []
    halos.append(halo(zs_p.at[7], zr_p.at[0], 12, (gz_up, up)))
    halos.append(halo(zs_p.at[0], zr_p.at[9], 13, (gz_up, down)))
    halos.append(halo(zs_m.at[7], zr_m.at[0], 14, (gz_down, up)))
    halos.append(halo(zs_m.at[0], zr_m.at[9], 15, (gz_down, down)))
    for k in range(5):
        halos.append(halo(rd.at[X_PLUS[k], 9], rd.at[X_PLUS[k], 1], k, (gz, up)))
        halos.append(halo(rd.at[X_MINUS[k], 0], rd.at[X_MINUS[k], 8], 5 + k, (gz, down)))
    for copy in halos:
        copy.start()
    greet_near(ready_sem)
    for x in range(1, 7):
        plane_loads[x].wait()
    lax.fori_loop(1, 7, inner_step, 0)
    faces = [
        halo(zs_p, zr_p.at[pl.ds(1, CX)], 10, (gz_up, me)),
        halo(zs_m, zr_m.at[pl.ds(1, CX)], 11, (gz_down, me)),
    ]
    for copy in faces:
        copy.start()
    halos = halos + faces
    for copy in wall_loads:
        copy.wait()

    owner_row = iota((N_XY, SLOTS), 0)
    row256 = iota((SLOTS, SLOTS), 0).astype(F32).astype(BF16)
    row128 = iota((CZ, SLOTS), 0).astype(F32)
    row128_16 = row128.astype(BF16)
    row32 = iota((N_XY, SLOTS), 0).astype(F32)

    for c in range(CHUNKS):
        owner_hits[c * N_XY : (c + 1) * N_XY, :] = hits(owner_row == (targets_ref[c] >> 12))
    before = hits(iota((SLOTS, SLOTS), 0) < iota((SLOTS, SLOTS), 1))
    ranks_ref[...] = dot(owner_hits[...], before)
    totals_ref[...] = dot(owner_hits[...], jnp.ones((SLOTS, SLOTS), BF16))

    def fill_slots(g, carry):
        base, table = carry
        lefts, rights = [], []
        for k in range(BATCH):
            c = g * BATCH + k
            start = pl.multiple_of(c * N_XY, N_XY)
            ranks = ranks_ref[pl.ds(start, N_XY), :] + base
            base = base + totals_ref[pl.ds(start, N_XY), :]
            target = targets_ref[c]
            cell = cells_ref[c]
            mine = owner_row == (target >> 12)
            rank = jnp.sum(jnp.where(mine, ranks, 0.0), axis=0, keepdims=True)
            place = target & 4095
            fields = [
                cell >> 7,
                (cell & 127) + 1,
                ((place >> 7) & 1) * 16 + (place >> 8),
                place & 127,
            ]
            lefts.append(
                jnp.concatenate(
                    [jnp.where(mine, field.astype(F32), 0.0) for field in fields], axis=0
                ).astype(BF16)
            )
            rank_hits[c] = hits16(row256, rank)
            rights.append(rank_hits[c])
        table = table + dot_nt(jnp.concatenate(lefts, axis=1), jnp.concatenate(rights, axis=1))
        return base, table

    unused, table = lax.fori_loop(
        0,
        CHUNKS // BATCH,
        fill_slots,
        (jnp.zeros((N_XY, SLOTS), F32), jnp.zeros((4 * N_XY, SLOTS), F32)),
    )
    places = table[64:96] * 128.0 + table[96:128]
    for owner in range(N_XY):
        slot_xy[owner] = table[owner : owner + 1]
        slot_z[owner] = table[32 + owner : 33 + owner] - 1.0
        place_send[owner] = places[owner : owner + 1]
    place_recv[me] = place_send[me]

    picker = edge_picker()
    cover = cover_ref[...]
    edges = tile_edges(cover, picker)
    edge_send0[...] = edges
    edge_recv0[me] = edges
    links = links_ref[...]
    codes = (links >> 4) * 8 + (links & 7) + ((links >> 3) & 1) * 256
    link_send[...] = jnp.zeros_like(link_send)
    link_send[:, 0:16] = codes.astype(F32)
    link_recv[me] = link_send[...]

    def mark_cells(g, unused):
        for k in range(GROUP):
            owner = g * GROUP + k
            xy_hits[owner] = hits16(row256, slot_xy[owner])
        return unused

    lax.fori_loop(0, GROUPS, mark_cells, 0)

    def border(q, x):
        cx, cy, cz = VELOCITIES[q]
        k = (Z_PLUS if cz == 1 else Z_MINUS).index(q)
        got = (zr_p if cz == 1 else zr_m)[x - cx + 1]
        edge = 0 if cz == 1 else 127
        return jnp.concatenate(
            [roll(got, edge - (k * 4 + block), 1) for block in range(4)], axis=0
        )

    def inner_plane(x, unused):
        total = None
        for q in range(19):
            value = rd[q, x + 1]
            read_ref[q, x] = value
            term = WEIGHTS[q] * value
            total = term if total is None else total + term
        dens[pl.ds(pl.multiple_of(x * NY, NY), NY), :] = total
        return unused

    lax.fori_loop(1, CX - 1, inner_plane, 0)
    pl.semaphore_wait(ready_sem, NEAR)
    send_steps(lambda other: place_send.at[other], place_recv, 1, 0, OTHERS)
    send_steps(lambda other: edge_send0, edge_recv0, 0, 0, OTHERS)

    for copy in halos[:4] + faces:
        copy.wait_recv()

    def finish_plane(i, unused):
        x = i * 7
        lane = iota((NY, CZ), 1)
        total = None
        for q in range(19):
            cx, cy, cz = VELOCITIES[q]
            value = rd[q, x + 1]
            if cz != 0:
                value = jnp.where(lane == (0 if cz == 1 else 127), border(q, x), value)
            read_ref[q, x] = value
            term = WEIGHTS[q] * value
            total = term if total is None else total + term
        dens[pl.ds(pl.multiple_of(x * NY, NY), NY), :] = total
        return unused

    def mend_plane(x, unused):
        lane = iota((NY, CZ), 1)
        rows = pl.ds(pl.multiple_of(x * NY, NY), NY)
        total = dens[rows, :]
        for members, edge in ((Z_PLUS, 0), (Z_MINUS, 127)):
            for q in members:
                old = read_ref[q, x]
                new = jnp.where(lane == edge, border(q, x), old)
                read_ref[q, x] = new
                total = total + WEIGHTS[q] * (new - old)
        dens[rows, :] = total
        return unused

    lax.fori_loop(1, CX - 1, mend_plane, 0)
    for copy in halos[4:14]:
        copy.wait_recv()
    lax.fori_loop(0, 2, finish_plane, 0)

    high, low = split(jnp.transpose(dens[...]))
    dens_t = jnp.concatenate([high, low], axis=0)

    def send_values(g, unused):
        others = group_partners(me, g)
        for half in range(2):
            for other in others[half * 4 : half * 4 + 4]:
                found = dot(dens_t, xy_hits[other])
                both = found[0:128] + found[128:256]
                value_send[other] = jnp.sum(
                    jnp.where(row128 == slot_z[other], both, 0.0), axis=0, keepdims=True
                )
            send_half(value_send, value_recv, 2, others, g, half)
        return unused

    lax.fori_loop(0, GROUPS, send_values, 0)
    value_recv[me] = value_send[me]
    send_steps(lambda other: link_send, link_recv, 5, 0, OTHERS)

    links = jnp.transpose(links_ref[...].astype(F32)).astype(jnp.int32)
    link_hits = []
    link_half = []
    lane256 = iota((16, 256), 1)
    for side in range(4):
        tile = links[:, side : side + 1]
        link_hits.append(hits(lane256 == (tile >> 4) * 8 + (tile & 7)))
        link_half.append((tile >> 3) & 1)
    link_hits = jnp.concatenate(link_hits, axis=0)
    matrix = neighbour_matrix()
    all_copy(edge_recv0, 0).wait_recv()
    borders = gather_edges(edge_recv0[...].reshape(256, 128), link_hits, link_half)
    all_copy(place_recv, 1).wait_recv()

    def mark_places(g, unused):
        for k in range(GROUP):
            brick = g * GROUP + k
            place = place_recv[brick]
            row = jnp.floor(place * (1.0 / 128.0))
            place_row[brick] = row
            lane_hits[brick] = hits16(row128_16, place - 128.0 * row)
        return unused

    lax.fori_loop(0, GROUPS, mark_places, 0)
    spread = 2.0 * neighbour_sum(cover, borders, matrix) + 0.8 * cover
    all_copy(value_recv, 2).wait_recv()

    def add_supply(g, total):
        lefts, rights = [], []
        for k in range(16):
            brick = g * 16 + k
            value = value_recv[brick]
            here = row32 == place_row[brick]
            high = value.astype(BF16).astype(F32)
            lefts.append(
                jnp.concatenate(
                    [jnp.where(here, high, 0.0), jnp.where(here, value - high, 0.0)], axis=0
                ).astype(BF16)
            )
            rights.append(lane_hits[brick])
        return total + dot_nt(jnp.concatenate(lefts, axis=1), jnp.concatenate(rights, axis=1))

    supply = lax.fori_loop(0, N_XY // 16, add_supply, jnp.zeros((64, 128), F32))
    supply = supply[0:32] + supply[32:64]
    supply = jnp.concatenate([supply[0:16], supply[16:32]], axis=1)
    gained = 0.3 * supply * (1.0 - cover)
    first = (gained + spread) * (1.0 / 9.0)
    edges = tile_edges(first, picker)
    edge_send1[...] = edges
    edge_recv1[me] = edges
    send_steps(lambda other: edge_send1, edge_recv1, 3, 0, OTHERS)
    high, low = split(first)
    second = dot(jnp.concatenate([high, low], axis=1), matrix[0:512])
    second = (gained + 0.8 * cover + 2.0 * second) * (1.0 / 9.0)
    change = -0.5 * (second - cover)
    change = jnp.concatenate([change[:, 0:128], change[:, 128:256]], axis=0)
    high, low = split(change)
    change = jnp.concatenate([high, low], axis=0)

    def send_changes(g, unused):
        others = group_partners(me, g)
        for half in range(2):
            for other in others[half * 4 : half * 4 + 4]:
                found = dot(change, lane_hits[other])
                both = found[0:32] + found[32:64]
                change_send[other] = jnp.sum(
                    jnp.where(row32 == place_row[other], both, 0.0), axis=0, keepdims=True
                )
            send_half(change_send, change_recv, 4, others, g, half)
        return unused

    lax.fori_loop(0, GROUPS, send_changes, 0)
    change_recv[me] = change_send[me]
    for copy in halos:
        copy.wait_send()
    all_copy(link_recv, 5).wait_recv()
    for owner in range(N_XY):
        link_table[owner * 4 : owner * 4 + 4, :] = link_recv[owner]
    codes = jnp.transpose(link_table[...])[0:16]
    second_half = jnp.where(codes >= 256.0, 1.0, 0.0)
    codes = jnp.concatenate([codes - 256.0 * second_half, second_half], axis=0).astype(BF16)
    row16 = iota((16, SLOTS), 0)

    def find_border(select, tile, valid, far, place):
        found = dot(codes, hits16(row128_16, select.astype(F32)))
        here = row16 == tile
        row = jnp.sum(jnp.where(here, found[0:16], 0.0), axis=0, keepdims=True)
        half = jnp.sum(jnp.where(here, found[16:32], 0.0), axis=0, keepdims=True)
        return jnp.where(valid, row, -1.0), half * 32.0 + (far * 16 + place).astype(F32)

    def mark_borders(g, unused):
        for k in range(BATCH):
            c = g * BATCH + k
            target = targets_ref[c]
            owner, tile = target >> 12, (target >> 8) & 15
            cell_hits[c] = hits16(row256, (cells_ref[c] >> 7).astype(F32))
            y, x = (target >> 4) & 15, target & 15
            far_x = jnp.where(x == 15, 1, 0)
            far_y = jnp.where(y == 15, 1, 0)
            row, place = find_border(owner * 4 + far_x, tile, (x == 0) | (x == 15), far_x, y)
            across_hits[c] = hits16(row256, row)
            across_place[c] = place
            row, place = find_border(owner * 4 + 2 + far_y, tile, (y == 0) | (y == 15), far_y, x)
            along_hits[c] = hits16(row256, row)
            along_place[c] = place
        return unused

    lax.fori_loop(0, CHUNKS // BATCH, mark_borders, 0)
    all_copy(edge_recv1, 3).wait_recv()
    table = edge_recv1[...].reshape(256, 128)
    table_t = jnp.transpose(table)
    high, low = split(jnp.concatenate([table_t[0:32], table_t[64:96]], axis=0))
    across = jnp.concatenate([high, low], axis=0)
    high, low = split(jnp.concatenate([table_t[32:64], table_t[96:128]], axis=0))
    along = jnp.concatenate([high, low], axis=0)
    row64 = iota((64, SLOTS), 0).astype(F32)

    def add_borders(g, unused):
        for k in range(BATCH):
            c = g * BATCH + k
            found = dot(across, across_hits[c])
            total = jnp.where(row64 == across_place[c], found[0:64] + found[64:128], 0.0)
            found = dot(along, along_hits[c])
            total = total + jnp.where(
                row64 == along_place[c], found[0:64] + found[64:128], 0.0
            )
            border_terms[c] = jnp.sum(total, axis=0, keepdims=True) * (-1.0 / 9.0)
        return unused

    lax.fori_loop(0, CHUNKS // BATCH, add_borders, 0)
    borders = gather_edges(table, link_hits, link_half)
    cover_out[...] = second + dot(borders.astype(BF16), matrix[512:640]) * (2.0 / 9.0)
    all_copy(change_recv, 4).wait_recv()
    got = jnp.concatenate([change_recv[owner] for owner in range(N_XY)], axis=0)
    high, low = split(got)
    got = jnp.concatenate([high, low], axis=0)

    def add_change(g, total):
        lefts, rights = [], []
        for k in range(BATCH):
            c = g * BATCH + k
            found = dot(got, rank_hits[c])
            mine = owner_row == (targets_ref[c] >> 12)
            value = jnp.sum(
                jnp.where(mine, found[0:32] + found[32:64], 0.0), axis=0, keepdims=True
            )
            value = value + border_terms[c]
            here = row128 == (cells_ref[c] & 127).astype(F32)
            high = value.astype(BF16).astype(F32)
            rights.append(
                jnp.concatenate(
                    [jnp.where(here, high, 0.0), jnp.where(here, value - high, 0.0)], axis=0
                ).astype(BF16)
            )
            lefts.append(cell_hits[c])
        return total + dot_nt(jnp.concatenate(lefts, axis=1), jnp.concatenate(rights, axis=1))

    correction = lax.fori_loop(0, CHUNKS // BATCH, add_change, jnp.zeros((256, 256), F32))
    correction_out[...] = correction[:, 0:128] + correction[:, 128:256]
    for ref, index in (
        (edge_recv0, 0),
        (place_recv, 1),
        (value_recv, 2),
        (edge_recv1, 3),
        (change_recv, 4),
        (link_recv, 5),
    ):
        all_copy(ref, index).wait_send()


def add_kernel(read_ref, correction_ref, cover_ref, updated_hbm, cover_hbm, stage, sem):
    cover_copy = pltpu.make_async_copy(cover_ref, cover_hbm, sem.at[CX])
    cover_copy.start()
    copies = []
    for x in range(CX):
        for part in (pl.ds(0, 10), pl.ds(10, 9)):
            stage[part, x] = read_ref[part, x] + correction_ref[x * NY : (x + 1) * NY, :][None]
        copies.append(pltpu.make_async_copy(stage.at[:, x], updated_hbm.at[:, x], sem.at[x]))
        copies[-1].start()
    for copy in copies:
        copy.wait()
    cover_copy.wait()


def shards(populations, solid, knudsen, wall_cells, wall_target, coverage, tile_links):
    hbm = pl.BlockSpec(memory_space=pltpu.HBM)
    vmem = pl.BlockSpec(memory_space=pltpu.VMEM)
    slots = pltpu.VMEM((N_XY, 1, SLOTS), F32)
    edge_table = pltpu.VMEM((N_XY, 8, 128), F32)
    by_chunk = pltpu.VMEM((CHUNKS, SLOTS, SLOTS), BF16)
    chunk_rows = pltpu.VMEM((CHUNKS, 1, SLOTS), F32)
    walls = pltpu.VMEM((CHUNKS, 1, SLOTS), jnp.int32)
    whole = jax.ShapeDtypeStruct((19, CX, NY, CZ), F32)
    cover_shape = jax.ShapeDtypeStruct((16, 256), F32)
    read, new_coverage, correction = pl.pallas_call(
        kernel,
        out_shape=(whole, cover_shape, jax.ShapeDtypeStruct((256, 128), F32)),
        in_specs=[hbm] * 7,
        out_specs=(vmem, vmem, vmem),
        scratch_shapes=[
            pltpu.VMEM((19, CX, NY, CZ), F32),
            pltpu.VMEM((CX, NY, CZ), jnp.int32),
            pltpu.VMEM((CX, NY, CZ), F32),
            walls,
            walls,
            pltpu.VMEM((16, 256), F32),
            pltpu.VMEM((4, 16), jnp.int32),
            pltpu.VMEM((19, CX + 2, NY, CZ), F32),
            pltpu.VMEM((CX, 8, 128), F32),
            pltpu.VMEM((CX, 8, 128), F32),
            pltpu.VMEM((CX + 2, 8, 128), F32),
            pltpu.VMEM((CX + 2, 8, 128), F32),
            pltpu.VMEM((CX * NY, CZ), F32),
            pltpu.VMEM((CHUNKS * N_XY, SLOTS), BF16),
            pltpu.VMEM((CHUNKS * N_XY, SLOTS), F32),
            pltpu.VMEM((CHUNKS * N_XY, SLOTS), F32),
            pltpu.VMEM((N_XY, SLOTS, SLOTS), BF16),
            pltpu.VMEM((N_XY, CZ, SLOTS), BF16),
            slots,
            slots,
            slots,
            slots,
            slots,
            slots,
            slots,
            slots,
            slots,
            pltpu.VMEM((8, 128), F32),
            edge_table,
            pltpu.VMEM((8, 128), F32),
            edge_table,
            pltpu.VMEM((4, 128), F32),
            pltpu.VMEM((N_XY, 4, 128), F32),
            pltpu.VMEM((4 * N_XY, 128), F32),
            by_chunk,
            by_chunk,
            by_chunk,
            by_chunk,
            chunk_rows,
            chunk_rows,
            chunk_rows,
            pltpu.SemaphoreType.DMA((14,)),
            pltpu.SemaphoreType.DMA((16,)),
            pltpu.SemaphoreType.DMA((16,)),
            pltpu.SemaphoreType.REGULAR,
            pltpu.SemaphoreType.DMA((6,)),
            pltpu.SemaphoreType.DMA((6,)),
        ],
        compiler_params=pltpu.CompilerParams(
            collective_id=0, has_side_effects=True, vmem_limit_bytes=40 * 1024 * 1024
        ),
    )(
        *[
            pltpu.with_memory_space_constraint(array, pltpu.HBM)
            for array in (
                populations,
                solid,
                knudsen,
                wall_cells.reshape(CHUNKS, 1, SLOTS),
                wall_target.reshape(CHUNKS, 1, SLOTS),
                coverage,
                tile_links.T,
            )
        ]
    )
    updated, new_coverage = pl.pallas_call(
        add_kernel,
        out_shape=(whole, cover_shape),
        in_specs=[vmem, vmem, vmem],
        out_specs=(hbm, hbm),
        scratch_shapes=[
            pltpu.VMEM((19, CX, NY, CZ), F32),
            pltpu.SemaphoreType.DMA((CX + 1,)),
        ],
        compiler_params=pltpu.CompilerParams(vmem_limit_bytes=16 * 1024 * 1024),
    )(read, correction, new_coverage)
    return updated, new_coverage


def solution(mesh):
    in_specs = (
        P(None, "xy", None, "gz"),
        P("xy", None, "gz"),
        P("xy", None, "gz"),
        P("gz", "xy"),
        P("gz", "xy"),
        P(("gz", "xy"), None),
        P(("gz", "xy"), None),
    )
    out_specs = (P(None, "xy", None, "gz"), P(("gz", "xy"), None))
    return jax.shard_map(shards, mesh=mesh, in_specs=in_specs, out_specs=out_specs, check_vma=False)
```

```python
import jax
import jax.numpy as jnp
from jax import lax
from jax.experimental import pallas as pl
from jax.experimental.pallas import tpu as pltpu
from jax.sharding import PartitionSpec as P

MESH = pl.DeviceIdType.MESH
F32 = jnp.float32
BF16 = jnp.bfloat16

VELOCITIES = [
    (0, 0, 0),
    (0, 1, 0),
    (0, -1, 0),
    (1, 0, 0),
    (-1, 0, 0),
    (0, 0, 1),
    (0, 0, -1),
    (1, 1, 0),
    (-1, -1, 0),
    (1, -1, 0),
    (-1, 1, 0),
    (1, 0, 1),
    (-1, 0, -1),
    (1, 0, -1),
    (-1, 0, 1),
    (0, 1, 1),
    (0, -1, -1),
    (0, 1, -1),
    (0, -1, 1),
]
WEIGHTS = [1.0 / 3.0] + [1.0 / 18.0] * 6 + [1.0 / 36.0] * 12
X_PLUS = [q for q in range(19) if VELOCITIES[q][0] == 1]
X_MINUS = [q for q in range(19) if VELOCITIES[q][0] == -1]
Z_PLUS = [q for q in range(19) if VELOCITIES[q][2] == 1]
Z_MINUS = [q for q in range(19) if VELOCITIES[q][2] == -1]

N_GZ = 8
N_XY = 32
CX = 8
NY = 32
CZ = 128
SLOTS = 256
CHUNKS = 16
OTHERS = N_XY - 1
NEAR = 19
GREETED = NEAR + 6
GROUP = 8
BATCH = 16
GROUPS = N_XY // GROUP


def iota(shape, dim):
    return lax.broadcasted_iota(jnp.int32, shape, dim)


def split(values):
    high = values.astype(BF16)
    low = (values - high.astype(F32)).astype(BF16)
    return high, low


def hits(mask):
    return jnp.where(mask, 1.0, 0.0).astype(BF16)


def hits16(rows, row):
    return jnp.where(rows == row.astype(BF16), BF16(1.0), BF16(0.0))


def dot(left, right):
    return lax.dot_general(left, right, (((1,), (0,)), ((), ())), preferred_element_type=F32)


def dot_nt(left, right):
    return lax.dot_general(left, right, (((1,), (1,)), ((), ())), preferred_element_type=F32)


def centred(step, size):
    return size // 2 + ((step + 1) // 2) * (1 - 2 * (step % 2))


def partner(me, step):
    z = lax.rem(lax.rem(me, 8) + centred(step // 4, 8), 8)
    x = lax.rem(lax.div(me, 8) + centred(step % 4, 4), 4)
    return x * 8 + z


def group_partners(me, group):
    place_z, place_x = lax.rem(me, 8), lax.div(me, 8)
    z = (lax.rem(place_z + 4 + group, 8), lax.rem(place_z + 11 - group, 8))
    x = [lax.rem(place_x + centred(k, 4), 4) * 8 for k in range(4)]
    return [x[k % 4] + z[k // 4] for k in range(8)]


def roll(values, shift, axis):
    shift = shift % values.shape[axis]
    return values if shift == 0 else pltpu.roll(values, shift, axis)


def edge_picker():
    cell, lane = iota((512, 128), 0), iota((512, 128), 1)
    side, place = (lane >> 4) & 3, lane & 15
    wanted = jnp.where(
        side == 0,
        place * 16 + 15,
        jnp.where(side == 1, place * 16, jnp.where(side == 2, 240 + place, place)),
    )
    return hits(cell == (lane >> 6) * 256 + wanted)


def tile_edges(cover, picker):
    both = jnp.concatenate([cover[0:8], cover[8:16]], axis=1)
    high, low = split(both)
    twice = jnp.concatenate([picker, picker], axis=0)
    return dot(jnp.concatenate([high, low], axis=1), twice)


def neighbour_matrix():
    a, b = iota((256, 256), 0), iota((256, 256), 1)
    same_row = (a >> 4) == (b >> 4)
    near = (same_row & (jnp.abs(a - b) == 1)) | (jnp.abs(a - b) == 16)
    inner = hits(near)
    s, k = iota((128, 256), 0), iota((128, 256), 1)
    side, place = (s >> 4) & 3, s & 15
    cell = jnp.where(
        side == 0,
        place * 16,
        jnp.where(side == 1, place * 16 + 15, jnp.where(side == 2, place, 240 + place)),
    )
    return jnp.concatenate([inner, inner, hits(k == cell)], axis=0)


def gather_edges(edges, link_hits, link_half):
    high, low = split(edges)
    found = dot(link_hits, jnp.concatenate([high, low], axis=1))
    lane = iota((16, 64), 1)
    out_high = jnp.zeros((16, 64), F32)
    out_low = jnp.zeros((16, 64), F32)
    for side in range(4):
        part = found[side * 16 : (side + 1) * 16]
        second = link_half[side] == 1
        h = jnp.where(second, part[:, 64:128], part[:, 0:64])
        l = jnp.where(second, part[:, 192:256], part[:, 128:192])
        here = (lane >> 4) == side
        out_high = jnp.where(here, h, out_high)
        out_low = jnp.where(here, l, out_low)
    return jnp.concatenate([out_high, out_low], axis=1)


def neighbour_sum(cover, borders, matrix):
    high, low = split(cover)
    return dot(jnp.concatenate([high, low, borders.astype(BF16)], axis=1), matrix)


def kernel(
    pop_hbm,
    solid_hbm,
    knudsen_hbm,
    cells_hbm,
    targets_hbm,
    cover_hbm,
    links_hbm,
    read_ref,
    cover_out,
    correction_out,
    pop,
    solid,
    knudsen,
    cells_ref,
    targets_ref,
    cover_ref,
    links_ref,
    rd,
    zs_p,
    zs_m,
    zr_p,
    zr_m,
    dens,
    owner_hits,
    ranks_ref,
    totals_ref,
    xy_hits,
    lane_hits,
    slot_xy,
    slot_z,
    place_row,
    place_send,
    place_recv,
    value_send,
    value_recv,
    change_send,
    change_recv,
    edge_send0,
    edge_recv0,
    edge_send1,
    edge_recv1,
    link_send,
    link_recv,
    link_table,
    cell_hits,
    rank_hits,
    across_hits,
    along_hits,
    across_place,
    along_place,
    border_terms,
    load_sem,
    halo_send,
    halo_recv,
    ready_sem,
    all_send,
    all_recv,
):
    gz = lax.axis_index("gz")
    me = lax.axis_index("xy")
    gz_up, gz_down = lax.rem(gz + 1, N_GZ), lax.rem(gz + N_GZ - 1, N_GZ)
    up, down = lax.rem(me + 1, N_XY), lax.rem(me + N_XY - 1, N_XY)

    def load(source, target, index):
        copy = pltpu.make_async_copy(source, target, load_sem.at[index])
        copy.start()
        return copy

    plane_loads = {}
    plane_loads[0] = load(pop_hbm.at[:, 0], pop.at[:, 0], 0)
    cell_loads = [load(solid_hbm, solid, 8), load(knudsen_hbm, knudsen, 9)]
    plane_loads[7] = load(pop_hbm.at[:, 7], pop.at[:, 7], 7)

    barrier = pltpu.get_barrier_semaphore()

    def greet_near(semaphore):
        for step_z in (2, 6, 1, 7, 0):
            z = lax.rem(lax.rem(me, 8) + step_z, 8)
            for step_x in (2, 1, 3, 0):
                if (step_z, step_x) != (0, 0):
                    x = lax.rem(lax.div(me, 8) + step_x, 4)
                    pl.semaphore_signal(
                        semaphore, inc=1, device_id=(gz, x * 8 + z), device_id_type=MESH
                    )

    for device in (
        (gz_up, up),
        (gz_up, down),
        (gz_down, up),
        (gz_down, down),
        (gz_up, me),
        (gz_down, me),
    ):
        pl.semaphore_signal(barrier, inc=1, device_id=device, device_id_type=MESH)
    greet_near(barrier)
    for x in range(1, 7):
        plane_loads[x] = load(pop_hbm.at[:, x], pop.at[:, x], x)
    wall_loads = [
        load(cells_hbm, cells_ref, 10),
        load(targets_hbm, targets_ref, 11),
        load(cover_hbm, cover_ref, 12),
        load(links_hbm, links_ref, 13),
    ]

    def send_one(source, target, index, other):
        pltpu.make_async_remote_copy(
            src_ref=source,
            dst_ref=target,
            send_sem=all_send.at[index],
            recv_sem=all_recv.at[index],
            device_id=(gz, other),
            device_id_type=MESH,
        ).start()

    def send_steps(source_of, target_ref, index, first, last):
        for step in range(first, last):
            other = partner(me, step)
            send_one(source_of(other), target_ref.at[me], index, other)

    def send_half(source, target, index, others, group, half):
        for other in others[half * 4 : half * 4 + 4 - half]:
            send_one(source.at[other], target.at[me], index, other)
        if half == 1:

            @pl.when(group < GROUPS - 1)
            def _():
                send_one(source.at[others[-1]], target.at[me], index, others[-1])

    def all_copy(ref, index):
        part = ref.at[pl.ds(0, OTHERS)]
        return pltpu.make_async_remote_copy(
            src_ref=part,
            dst_ref=part,
            send_sem=all_send.at[index],
            recv_sem=all_recv.at[index],
            device_id=(gz, up),
            device_id_type=MESH,
        )

    lane8 = iota((8, 128), 1)

    def collide_plane(x):
        kn = knudsen[x]
        sol = solid[x] == 1
        axis_sum = jnp.zeros((NY, CZ), F32)
        diag_sum = jnp.zeros((NY, CZ), F32)
        axis_m = [None] * 3
        diag_m = [None] * 3
        for q in range(1, 19, 2):
            p, m = pop[q, x], pop[q + 1, x]
            if q < 7:
                axis_sum = axis_sum + (p + m)
            else:
                diag_sum = diag_sum + (p + m)
            diff = p - m
            for axis in range(3):
                c = VELOCITIES[q][axis]
                sums = axis_m if q < 7 else diag_m
                if c == 0:
                    continue
                if sums[axis] is None:
                    sums[axis] = diff if c == 1 else -diff
                else:
                    sums[axis] = sums[axis] + diff if c == 1 else sums[axis] - diff
        rest = pop[0, x]
        density = (1.0 / 3.0) * rest + (1.0 / 18.0) * axis_sum + (1.0 / 36.0) * diag_sum
        inverse = 1.0 / density
        speed = [
            ((1.0 / 18.0) * axis_m[axis] + (1.0 / 36.0) * diag_m[axis]) * inverse
            for axis in range(3)
        ]
        square = speed[0] * speed[0] + speed[1] * speed[1] + speed[2] * speed[2]
        relax = (1.0 + 2.0 * kn) / (1.0 + kn)
        keep = 1.0 - relax
        gain = relax * density
        base = gain - 1.5 * gain * square
        gain3 = 3.0 * gain
        rd[0, x + 1] = jnp.where(sol, rest, keep * rest + base)
        tile_p = jnp.zeros((8, 128), F32)
        tile_m = jnp.zeros((8, 128), F32)
        for q in range(1, 19, 2):
            p, m = pop[q, x], pop[q + 1, x]
            along = None
            for axis in range(3):
                c = VELOCITIES[q][axis]
                if c == 0:
                    continue
                if along is None:
                    along = speed[axis] if c == 1 else -speed[axis]
                else:
                    along = along + speed[axis] if c == 1 else along - speed[axis]
            odd = gain3 * along
            even = base + 1.5 * odd * along
            new_p = jnp.where(sol, m, keep * p + (even + odd))
            new_m = jnp.where(sol, p, keep * m + (even - odd))
            for member, value in ((q, new_p), (q + 1, new_m)):
                cx, cy, cz = VELOCITIES[member]
                value = roll(value, cy, 0)
                value = roll(value, cz, 1)
                rd[member, x + 1 + cx] = value
                if cz == 1:
                    k = Z_PLUS.index(member)
                    for block in range(4):
                        at = k * 4 + block
                        moved = roll(value[block * 8 : block * 8 + 8], at, 1)
                        tile_p = jnp.where(lane8 == at, moved, tile_p)
                if cz == -1:
                    k = Z_MINUS.index(member)
                    for block in range(4):
                        at = k * 4 + block
                        moved = roll(value[block * 8 : block * 8 + 8], at + 1, 1)
                        tile_m = jnp.where(lane8 == at, moved, tile_m)
        zs_p[x] = tile_p
        zs_m[x] = tile_m

    def edge_step(i, unused):
        collide_plane(i * 7)
        return unused

    def inner_step(i, unused):
        collide_plane(i)
        return unused

    def halo(source, target, index, device):
        return pltpu.make_async_remote_copy(
            src_ref=source,
            dst_ref=target,
            send_sem=halo_send.at[index],
            recv_sem=halo_recv.at[index],
            device_id=device,
            device_id_type=MESH,
        )

    for copy in cell_loads + [plane_loads[0], plane_loads[7]]:
        copy.wait()
    lax.fori_loop(0, 2, edge_step, 0)
    pl.semaphore_wait(barrier, GREETED)
    halos = []
    halos.append(halo(zs_p.at[7], zr_p.at[0], 12, (gz_up, up)))
    halos.append(halo(zs_p.at[0], zr_p.at[9], 13, (gz_up, down)))
    halos.append(halo(zs_m.at[7], zr_m.at[0], 14, (gz_down, up)))
    halos.append(halo(zs_m.at[0], zr_m.at[9], 15, (gz_down, down)))
    for k in range(5):
        halos.append(halo(rd.at[X_PLUS[k], 9], rd.at[X_PLUS[k], 1], k, (gz, up)))
        halos.append(halo(rd.at[X_MINUS[k], 0], rd.at[X_MINUS[k], 8], 5 + k, (gz, down)))
    for copy in halos:
        copy.start()
    greet_near(ready_sem)
    for x in range(1, 7):
        plane_loads[x].wait()
    lax.fori_loop(1, 7, inner_step, 0)
    faces = [
        halo(zs_p, zr_p.at[pl.ds(1, CX)], 10, (gz_up, me)),
        halo(zs_m, zr_m.at[pl.ds(1, CX)], 11, (gz_down, me)),
    ]
    for copy in faces:
        copy.start()
    halos = halos + faces
    for copy in wall_loads:
        copy.wait()

    owner_row = iota((N_XY, SLOTS), 0)
    row256 = iota((SLOTS, SLOTS), 0).astype(F32).astype(BF16)
    row128 = iota((CZ, SLOTS), 0).astype(F32)
    row128_16 = row128.astype(BF16)
    row32 = iota((N_XY, SLOTS), 0).astype(F32)

    for c in range(CHUNKS):
        owner_hits[c * N_XY : (c + 1) * N_XY, :] = hits(owner_row == (targets_ref[c] >> 12))
    before = hits(iota((SLOTS, SLOTS), 0) < iota((SLOTS, SLOTS), 1))
    ranks_ref[...] = dot(owner_hits[...], before)
    totals_ref[...] = dot(owner_hits[...], jnp.ones((SLOTS, SLOTS), BF16))

    def fill_slots(g, carry):
        base, table = carry
        lefts, rights = [], []
        for k in range(BATCH):
            c = g * BATCH + k
            start = pl.multiple_of(c * N_XY, N_XY)
            ranks = ranks_ref[pl.ds(start, N_XY), :] + base
            base = base + totals_ref[pl.ds(start, N_XY), :]
            target = targets_ref[c]
            cell = cells_ref[c]
            mine = owner_row == (target >> 12)
            rank = jnp.sum(jnp.where(mine, ranks, 0.0), axis=0, keepdims=True)
            place = target & 4095
            fields = [
                cell >> 7,
                (cell & 127) + 1,
                ((place >> 7) & 1) * 16 + (place >> 8),
                place & 127,
            ]
            lefts.append(
                jnp.concatenate(
                    [jnp.where(mine, field.astype(F32), 0.0) for field in fields], axis=0
                ).astype(BF16)
            )
            rank_hits[c] = hits16(row256, rank)
            rights.append(rank_hits[c])
        table = table + dot_nt(jnp.concatenate(lefts, axis=1), jnp.concatenate(rights, axis=1))
        return base, table

    unused, table = lax.fori_loop(
        0,
        CHUNKS // BATCH,
        fill_slots,
        (jnp.zeros((N_XY, SLOTS), F32), jnp.zeros((4 * N_XY, SLOTS), F32)),
    )
    places = table[64:96] * 128.0 + table[96:128]
    for owner in range(N_XY):
        slot_xy[owner] = table[owner : owner + 1]
        slot_z[owner] = table[32 + owner : 33 + owner] - 1.0
        place_send[owner] = places[owner : owner + 1]
    place_recv[me] = place_send[me]

    picker = edge_picker()
    cover = cover_ref[...]
    edges = tile_edges(cover, picker)
    edge_send0[...] = edges
    edge_recv0[me] = edges
    links = links_ref[...]
    codes = (links >> 4) * 8 + (links & 7) + ((links >> 3) & 1) * 256
    link_send[...] = jnp.zeros_like(link_send)
    link_send[:, 0:16] = codes.astype(F32)
    link_recv[me] = link_send[...]

    def mark_cells(g, unused):
        for k in range(GROUP):
            owner = g * GROUP + k
            xy_hits[owner] = hits16(row256, slot_xy[owner])
        return unused

    lax.fori_loop(0, GROUPS, mark_cells, 0)

    def border(q, x):
        cx, cy, cz = VELOCITIES[q]
        k = (Z_PLUS if cz == 1 else Z_MINUS).index(q)
        got = (zr_p if cz == 1 else zr_m)[x - cx + 1]
        edge = 0 if cz == 1 else 127
        return jnp.concatenate(
            [roll(got, edge - (k * 4 + block), 1) for block in range(4)], axis=0
        )

    def inner_plane(x, unused):
        total = None
        for q in range(19):
            value = rd[q, x + 1]
            read_ref[q, x] = value
            term = WEIGHTS[q] * value
            total = term if total is None else total + term
        dens[pl.ds(pl.multiple_of(x * NY, NY), NY), :] = total
        return unused

    lax.fori_loop(1, CX - 1, inner_plane, 0)
    pl.semaphore_wait(ready_sem, NEAR)
    send_steps(lambda other: place_send.at[other], place_recv, 1, 0, OTHERS)
    send_steps(lambda other: edge_send0, edge_recv0, 0, 0, OTHERS)

    for copy in halos[:4] + faces:
        copy.wait_recv()

    def finish_plane(i, unused):
        x = i * 7
        lane = iota((NY, CZ), 1)
        total = None
        for q in range(19):
            cx, cy, cz = VELOCITIES[q]
            value = rd[q, x + 1]
            if cz != 0:
                value = jnp.where(lane == (0 if cz == 1 else 127), border(q, x), value)
            read_ref[q, x] = value
            term = WEIGHTS[q] * value
            total = term if total is None else total + term
        dens[pl.ds(pl.multiple_of(x * NY, NY), NY), :] = total
        return unused

    def mend_plane(x, unused):
        lane = iota((NY, CZ), 1)
        rows = pl.ds(pl.multiple_of(x * NY, NY), NY)
        total = dens[rows, :]
        for members, edge in ((Z_PLUS, 0), (Z_MINUS, 127)):
            for q in members:
                old = read_ref[q, x]
                new = jnp.where(lane == edge, border(q, x), old)
                read_ref[q, x] = new
                total = total + WEIGHTS[q] * (new - old)
        dens[rows, :] = total
        return unused

    lax.fori_loop(1, CX - 1, mend_plane, 0)
    for copy in halos[4:14]:
        copy.wait_recv()
    lax.fori_loop(0, 2, finish_plane, 0)

    high, low = split(jnp.transpose(dens[...]))
    dens_t = jnp.concatenate([high, low], axis=0)

    def send_values(g, unused):
        others = group_partners(me, g)
        for half in range(2):
            for other in others[half * 4 : half * 4 + 4]:
                found = dot(dens_t, xy_hits[other])
                both = found[0:128] + found[128:256]
                value_send[other] = jnp.sum(
                    jnp.where(row128 == slot_z[other], both, 0.0), axis=0, keepdims=True
                )
            send_half(value_send, value_recv, 2, others, g, half)
        return unused

    lax.fori_loop(0, GROUPS, send_values, 0)
    value_recv[me] = value_send[me]
    send_steps(lambda other: link_send, link_recv, 5, 0, OTHERS)

    links = jnp.transpose(links_ref[...].astype(F32)).astype(jnp.int32)
    link_hits = []
    link_half = []
    lane256 = iota((16, 256), 1)
    for side in range(4):
        tile = links[:, side : side + 1]
        link_hits.append(hits(lane256 == (tile >> 4) * 8 + (tile & 7)))
        link_half.append((tile >> 3) & 1)
    link_hits = jnp.concatenate(link_hits, axis=0)
    matrix = neighbour_matrix()
    all_copy(edge_recv0, 0).wait_recv()
    borders = gather_edges(edge_recv0[...].reshape(256, 128), link_hits, link_half)
    all_copy(place_recv, 1).wait_recv()

    def mark_places(g, unused):
        for k in range(GROUP):
            brick = g * GROUP + k
            place = place_recv[brick]
            row = jnp.floor(place * (1.0 / 128.0))
            place_row[brick] = row
            lane_hits[brick] = hits16(row128_16, place - 128.0 * row)
        return unused

    lax.fori_loop(0, GROUPS, mark_places, 0)
    spread = 2.0 * neighbour_sum(cover, borders, matrix) + 0.8 * cover
    all_copy(value_recv, 2).wait_recv()

    def add_supply(g, total):
        lefts, rights = [], []
        for k in range(16):
            brick = g * 16 + k
            value = value_recv[brick]
            here = row32 == place_row[brick]
            high = value.astype(BF16).astype(F32)
            lefts.append(
                jnp.concatenate(
                    [jnp.where(here, high, 0.0), jnp.where(here, value - high, 0.0)], axis=0
                ).astype(BF16)
            )
            rights.append(lane_hits[brick])
        return total + dot_nt(jnp.concatenate(lefts, axis=1), jnp.concatenate(rights, axis=1))

    supply = lax.fori_loop(0, N_XY // 16, add_supply, jnp.zeros((64, 128), F32))
    supply = supply[0:32] + supply[32:64]
    supply = jnp.concatenate([supply[0:16], supply[16:32]], axis=1)
    gained = 0.3 * supply * (1.0 - cover)
    first = (gained + spread) * (1.0 / 9.0)
    edges = tile_edges(first, picker)
    edge_send1[...] = edges
    edge_recv1[me] = edges
    send_steps(lambda other: edge_send1, edge_recv1, 3, 0, 16)
    high, low = split(first)
    second = dot(jnp.concatenate([high, low], axis=1), matrix[0:512])
    second = (gained + 0.8 * cover + 2.0 * second) * (1.0 / 9.0)
    change = -0.5 * (second - cover)
    change = jnp.concatenate([change[:, 0:128], change[:, 128:256]], axis=0)
    high, low = split(change)
    change = jnp.concatenate([high, low], axis=0)

    def send_changes(g, unused):
        others = group_partners(me, g)
        for half in range(2):
            for other in others[half * 4 : half * 4 + 4]:
                found = dot(change, lane_hits[other])
                both = found[0:32] + found[32:64]
                change_send[other] = jnp.sum(
                    jnp.where(row32 == place_row[other], both, 0.0), axis=0, keepdims=True
                )
            send_half(change_send, change_recv, 4, others, g, half)
        return unused

    lax.fori_loop(0, 1, send_changes, 0)
    send_steps(lambda other: edge_send1, edge_recv1, 3, 16, OTHERS)
    lax.fori_loop(1, GROUPS, send_changes, 0)
    change_recv[me] = change_send[me]
    for copy in halos:
        copy.wait_send()
    all_copy(link_recv, 5).wait_recv()
    for owner in range(N_XY):
        link_table[owner * 4 : owner * 4 + 4, :] = link_recv[owner]
    codes = jnp.transpose(link_table[...])[0:16]
    second_half = jnp.where(codes >= 256.0, 1.0, 0.0)
    codes = jnp.concatenate([codes - 256.0 * second_half, second_half], axis=0).astype(BF16)
    row16 = iota((16, SLOTS), 0)

    def find_border(select, tile, valid, far, place):
        found = dot(codes, hits16(row128_16, select.astype(F32)))
        here = row16 == tile
        row = jnp.sum(jnp.where(here, found[0:16], 0.0), axis=0, keepdims=True)
        half = jnp.sum(jnp.where(here, found[16:32], 0.0), axis=0, keepdims=True)
        return jnp.where(valid, row, -1.0), half * 32.0 + (far * 16 + place).astype(F32)

    def mark_borders(g, unused):
        for k in range(BATCH):
            c = g * BATCH + k
            target = targets_ref[c]
            owner, tile = target >> 12, (target >> 8) & 15
            cell_hits[c] = hits16(row256, (cells_ref[c] >> 7).astype(F32))
            y, x = (target >> 4) & 15, target & 15
            far_x = jnp.where(x == 15, 1, 0)
            far_y = jnp.where(y == 15, 1, 0)
            row, place = find_border(owner * 4 + far_x, tile, (x == 0) | (x == 15), far_x, y)
            across_hits[c] = hits16(row256, row)
            across_place[c] = place
            row, place = find_border(owner * 4 + 2 + far_y, tile, (y == 0) | (y == 15), far_y, x)
            along_hits[c] = hits16(row256, row)
            along_place[c] = place
        return unused

    lax.fori_loop(0, CHUNKS // BATCH, mark_borders, 0)
    all_copy(edge_recv1, 3).wait_recv()
    table = edge_recv1[...].reshape(256, 128)
    table_t = jnp.transpose(table)
    high, low = split(jnp.concatenate([table_t[0:32], table_t[64:96]], axis=0))
    across = jnp.concatenate([high, low], axis=0)
    high, low = split(jnp.concatenate([table_t[32:64], table_t[96:128]], axis=0))
    along = jnp.concatenate([high, low], axis=0)
    row64 = iota((64, SLOTS), 0).astype(F32)

    def add_borders(g, unused):
        for k in range(BATCH):
            c = g * BATCH + k
            found = dot(across, across_hits[c])
            total = jnp.where(row64 == across_place[c], found[0:64] + found[64:128], 0.0)
            found = dot(along, along_hits[c])
            total = total + jnp.where(
                row64 == along_place[c], found[0:64] + found[64:128], 0.0
            )
            border_terms[c] = jnp.sum(total, axis=0, keepdims=True) * (-1.0 / 9.0)
        return unused

    lax.fori_loop(0, CHUNKS // BATCH, add_borders, 0)
    borders = gather_edges(table, link_hits, link_half)
    cover_out[...] = second + dot(borders.astype(BF16), matrix[512:640]) * (2.0 / 9.0)
    all_copy(change_recv, 4).wait_recv()
    got = jnp.concatenate([change_recv[owner] for owner in range(N_XY)], axis=0)
    high, low = split(got)
    got = jnp.concatenate([high, low], axis=0)

    def add_change(g, total):
        lefts, rights = [], []
        for k in range(BATCH):
            c = g * BATCH + k
            found = dot(got, rank_hits[c])
            mine = owner_row == (targets_ref[c] >> 12)
            value = jnp.sum(
                jnp.where(mine, found[0:32] + found[32:64], 0.0), axis=0, keepdims=True
            )
            value = value + border_terms[c]
            here = row128 == (cells_ref[c] & 127).astype(F32)
            high = value.astype(BF16).astype(F32)
            rights.append(
                jnp.concatenate(
                    [jnp.where(here, high, 0.0), jnp.where(here, value - high, 0.0)], axis=0
                ).astype(BF16)
            )
            lefts.append(cell_hits[c])
        return total + dot_nt(jnp.concatenate(lefts, axis=1), jnp.concatenate(rights, axis=1))

    correction = lax.fori_loop(0, CHUNKS // BATCH, add_change, jnp.zeros((256, 256), F32))
    correction_out[...] = correction[:, 0:128] + correction[:, 128:256]
    for ref, index in (
        (edge_recv0, 0),
        (place_recv, 1),
        (value_recv, 2),
        (edge_recv1, 3),
        (change_recv, 4),
        (link_recv, 5),
    ):
        all_copy(ref, index).wait_send()


def add_kernel(read_ref, correction_ref, cover_ref, updated_hbm, cover_hbm, stage, sem):
    cover_copy = pltpu.make_async_copy(cover_ref, cover_hbm, sem.at[CX])
    cover_copy.start()
    copies = []
    for x in range(CX):
        for part in (pl.ds(0, 10), pl.ds(10, 9)):
            stage[part, x] = read_ref[part, x] + correction_ref[x * NY : (x + 1) * NY, :][None]
        copies.append(pltpu.make_async_copy(stage.at[:, x], updated_hbm.at[:, x], sem.at[x]))
        copies[-1].start()
    for copy in copies:
        copy.wait()
    cover_copy.wait()


def shards(populations, solid, knudsen, wall_cells, wall_target, coverage, tile_links):
    hbm = pl.BlockSpec(memory_space=pltpu.HBM)
    vmem = pl.BlockSpec(memory_space=pltpu.VMEM)
    slots = pltpu.VMEM((N_XY, 1, SLOTS), F32)
    edge_table = pltpu.VMEM((N_XY, 8, 128), F32)
    by_chunk = pltpu.VMEM((CHUNKS, SLOTS, SLOTS), BF16)
    chunk_rows = pltpu.VMEM((CHUNKS, 1, SLOTS), F32)
    walls = pltpu.VMEM((CHUNKS, 1, SLOTS), jnp.int32)
    whole = jax.ShapeDtypeStruct((19, CX, NY, CZ), F32)
    cover_shape = jax.ShapeDtypeStruct((16, 256), F32)
    read, new_coverage, correction = pl.pallas_call(
        kernel,
        out_shape=(whole, cover_shape, jax.ShapeDtypeStruct((256, 128), F32)),
        in_specs=[hbm] * 7,
        out_specs=(vmem, vmem, vmem),
        scratch_shapes=[
            pltpu.VMEM((19, CX, NY, CZ), F32),
            pltpu.VMEM((CX, NY, CZ), jnp.int32),
            pltpu.VMEM((CX, NY, CZ), F32),
            walls,
            walls,
            pltpu.VMEM((16, 256), F32),
            pltpu.VMEM((4, 16), jnp.int32),
            pltpu.VMEM((19, CX + 2, NY, CZ), F32),
            pltpu.VMEM((CX, 8, 128), F32),
            pltpu.VMEM((CX, 8, 128), F32),
            pltpu.VMEM((CX + 2, 8, 128), F32),
            pltpu.VMEM((CX + 2, 8, 128), F32),
            pltpu.VMEM((CX * NY, CZ), F32),
            pltpu.VMEM((CHUNKS * N_XY, SLOTS), BF16),
            pltpu.VMEM((CHUNKS * N_XY, SLOTS), F32),
            pltpu.VMEM((CHUNKS * N_XY, SLOTS), F32),
            pltpu.VMEM((N_XY, SLOTS, SLOTS), BF16),
            pltpu.VMEM((N_XY, CZ, SLOTS), BF16),
            slots,
            slots,
            slots,
            slots,
            slots,
            slots,
            slots,
            slots,
            slots,
            pltpu.VMEM((8, 128), F32),
            edge_table,
            pltpu.VMEM((8, 128), F32),
            edge_table,
            pltpu.VMEM((4, 128), F32),
            pltpu.VMEM((N_XY, 4, 128), F32),
            pltpu.VMEM((4 * N_XY, 128), F32),
            by_chunk,
            by_chunk,
            by_chunk,
            by_chunk,
            chunk_rows,
            chunk_rows,
            chunk_rows,
            pltpu.SemaphoreType.DMA((14,)),
            pltpu.SemaphoreType.DMA((16,)),
            pltpu.SemaphoreType.DMA((16,)),
            pltpu.SemaphoreType.REGULAR,
            pltpu.SemaphoreType.DMA((6,)),
            pltpu.SemaphoreType.DMA((6,)),
        ],
        compiler_params=pltpu.CompilerParams(
            collective_id=0, has_side_effects=True, vmem_limit_bytes=40 * 1024 * 1024
        ),
    )(
        *[
            pltpu.with_memory_space_constraint(array, pltpu.HBM)
            for array in (
                populations,
                solid,
                knudsen,
                wall_cells.reshape(CHUNKS, 1, SLOTS),
                wall_target.reshape(CHUNKS, 1, SLOTS),
                coverage,
                tile_links.T,
            )
        ]
    )
    updated, new_coverage = pl.pallas_call(
        add_kernel,
        out_shape=(whole, cover_shape),
        in_specs=[vmem, vmem, vmem],
        out_specs=(hbm, hbm),
        scratch_shapes=[
            pltpu.VMEM((19, CX, NY, CZ), F32),
            pltpu.SemaphoreType.DMA((CX + 1,)),
        ],
        compiler_params=pltpu.CompilerParams(vmem_limit_bytes=16 * 1024 * 1024),
    )(read, correction, new_coverage)
    return updated, new_coverage


def solution(mesh):
    in_specs = (
        P(None, "xy", None, "gz"),
        P("xy", None, "gz"),
        P("xy", None, "gz"),
        P("gz", "xy"),
        P("gz", "xy"),
        P(("gz", "xy"), None),
        P(("gz", "xy"), None),
    )
    out_specs = (P(None, "xy", None, "gz"), P(("gz", "xy"), None))
    return jax.shard_map(shards, mesh=mesh, in_specs=in_specs, out_specs=out_specs, check_vma=False)
```
